128 devices in a mesh: section: 2 (over core), ctx: 8 (over x_lo, z), fsdp: 8 (over y, x_hi).
Axes of the slice: x: 4 (x_hi: 2, x_lo: 2; x = x_hi * 2 + x_lo), y: 4, z: 4, core: 2. Of those that a mesh axis runs over, the one named last changes fastest.
Arguments:
- x_in: bfloat16 [2, 8, 1024, 768], P(None, 'fsdp', 'ctx'), may hold values from -6 to 6
- cotangent: bfloat16 [2, 8, 1024, 768], P(None, 'fsdp', 'ctx'), may hold values from -6 to 6
- group_ids: int32 [2, 8, 1024], P(None, 'fsdp'), may hold values from 0 to 8, as said below
- routes: int32 [2, 2, 8, 1024, 2], P('section', None, 'fsdp', 'ctx'), may hold values from 0 to 7, all different within a row
- priority: int32 [2, 2, 8, 1024, 2], P('section', None, 'fsdp', 'ctx'), may hold values from 0 to 4095
- gains: bfloat16 [2, 768, 2], P('section', ('ctx', 'fsdp')), may hold values from 0.5 to 1.5
- w_qkv: bfloat16 [2, 768, 2304], P('section', ('ctx', 'fsdp')), may hold values from -0.21875 to 0.21875
- w_out: bfloat16 [2, 768, 768], P('section', ('ctx', 'fsdp')), may hold values from -1.75 to 1.75
- router: bfloat16 [2, 768, 8], P('section', ('ctx', 'fsdp')), may hold values from -0.15625 to 0.15625
- shared_gate_up: bfloat16 [2, 768, 4096], P('section', ('ctx', 'fsdp')), may hold values from -0.21875 to 0.21875
- shared_down: bfloat16 [2, 2048, 768], P('section', ('ctx', 'fsdp')), may hold values from -0.125 to 0.125
- expert_gate_up: bfloat16 [2, 8, 768, 4096], P('section', 'ctx', 'fsdp'), may hold values from -0.21875 to 0.21875
- expert_down: bfloat16 [2, 8, 2048, 768], P('section', 'ctx', 'fsdp'), may hold values from -0.125 to 0.125
Outputs:
- section_outputs: bfloat16 [2, 2, 8, 1024, 768], P('section', None, 'fsdp', 'ctx')
- input_grads: float32 [2, 2, 8, 1024, 768], P('section', None, 'fsdp', 'ctx')
- gains_grad: float32 [2, 768, 2], P('section', ('ctx', 'fsdp'))
- w_qkv_grad: float32 [2, 768, 2304], P('section', ('ctx', 'fsdp'))
- w_out_grad: float32 [2, 768, 768], P('section', ('ctx', 'fsdp'))
- router_grad: float32 [2, 768, 8], P('section', ('ctx', 'fsdp'))
- shared_gate_up_grad: float32 [2, 768, 4096], P('section', ('ctx', 'fsdp'))
- shared_down_grad: float32 [2, 2048, 768], P('section', ('ctx', 'fsdp'))
- expert_gate_up_grad: float32 [2, 8, 768, 4096], P('section', 'ctx', 'fsdp')
- expert_down_grad: float32 [2, 8, 2048, 768], P('section', 'ctx', 'fsdp')
The draws below stay inside these ranges and needn't reach their ends.
Inputs may be any that keep to these rules, and one draw needn't show every extreme that they name: `group_ids`: in each row a prompt labelled 0 takes the first 384 to 512 tokens; labels 1 to 8 follow in order, each a nonempty contiguous run. `routes`: each token names 2 different experts.
All inputs are finite; a program needn't handle non-finite values.
Results may differ from the reference program's by a relative error of at most 0.025.
Values may be sent and summed in bfloat16 or wider, within the bound.
A program may use at most 320 MiB of HBM per device.

```python
import math
import jax
import jax.numpy as jnp
from jax import lax

D = 768
HEADS = 12
HEAD_DIM = 64
FF = 2048
SHARED_FF = 2048
TOP = 2
MICRO = 2
CONT = 8
EXPERTS = 8
SEQ = 1024
ROWS = 128
CAP = 40
GROUPS = 8
N_CTX = 8


def draw_group_ids(key, part):
    key = jax.random.fold_in(key, 11)

    def one_row(row_key):
        first_key, second_key = jax.random.split(row_key)
        prompt_len = SEQ // 2 - jax.random.randint(first_key, (), 0, SEQ // 8 + 1)
        token_index = jnp.arange(SEQ, dtype=jnp.int32)
        order_scores = jax.random.randint(second_key, (SEQ,), 0, 2 ** 17) * SEQ + token_index
        order_scores = jnp.where(token_index > prompt_len, order_scores, -1)
        cut_values, _ = lax.top_k(order_scores, CONT - 1)
        cut_points = cut_values % SEQ
        later_runs = jnp.sum((cut_points[None, :] <= token_index[:, None]).astype(jnp.int32), axis=1)
        return jnp.where(token_index < prompt_len, 0, 1 + later_runs).astype(jnp.int32)
    row_keys = jax.random.split(key, MICRO * GROUPS)
    return jax.vmap(one_row)(row_keys).reshape(MICRO, GROUPS, SEQ)


def place_ends(drawn, rng, least, largest):
    longest = drawn.shape.index(max(drawn.shape))
    spots = []
    for shift in (0, 1):
        where = [jax.random.randint(jax.random.fold_in(rng, axis), (), 0, length) for axis, length in enumerate(drawn.shape)]
        where[longest] = (where[longest] + shift) % drawn.shape[longest]
        spots.append(tuple(where))
    return drawn.at[spots[0]].set(least).at[spots[1]].set(largest)


def steps_of(key, dims, shards, low, high):
    def one(axis_at, shards_of):
        draws = jax.random.uniform(jax.random.fold_in(jax.random.fold_in(key, 6), axis_at), (shards_of,), jnp.float32, low / len(shards), high / len(shards))
        return jnp.repeat(jnp.exp(draws), dims[axis_at] // shards_of).reshape((-1,) + (1,) * (len(dims) - axis_at - 1))

    level = one(*shards[0])
    for cut in shards[1:]:
        level = level * one(*cut)
    return level


def choose_distinct(stream_key, rows, number_of, top, lift):
    ranking = jax.random.permutation(jax.random.fold_in(stream_key, 1), number_of)
    boost = ranking
    for power in range(3):
        boost = boost * boost // number_of
    boost = boost * lift // number_of
    lots = jax.random.randint(jax.random.fold_in(stream_key, 2), (rows, number_of), 0, 4096) + boost
    holders = jax.random.permutation(jax.random.fold_in(stream_key, 3), rows)[jnp.arange(number_of) % rows]
    lots = jnp.where(jnp.arange(rows)[:, None] == holders[None, :], 1 << 14, lots)
    score = lots * number_of + jnp.arange(number_of)
    return lax.top_k(score.astype(jnp.int32), top)[1].astype(jnp.int32)


def scatter_about(own_key, extent, width, most, pieces=(), kind=jnp.bfloat16):
    level = steps_of(own_key, extent, pieces, -0.22, 0.18) if pieces else 1.0
    drawn = jax.random.normal(own_key, extent, jnp.float32) * width * level
    return jnp.minimum(jnp.maximum(drawn, -most), most).astype(kind)


def setup_inputs(seed: int = 0) -> dict:
    seeds = jax.random.split(jax.random.key(seed), 14)
    x_in = scatter_about(seeds[0], (MICRO, GROUPS, SEQ, D), 1.0, 6.0, ((1, 8), (2, 8)))
    cotangent = scatter_about(seeds[1], (MICRO, GROUPS, SEQ, D), 1.0, 6.0, ((1, 8), (2, 8)))
    group_ids = draw_group_ids(jax.random.fold_in(seeds[13], 71), 0)
    routes = choose_distinct(seeds[3], 2 * MICRO * GROUPS * SEQ, EXPERTS, TOP, 2048).reshape((2, MICRO, GROUPS, SEQ, TOP))
    priority = place_ends(jax.random.randint(seeds[4], (2, MICRO, GROUPS, SEQ, TOP), 0, 4096), jax.random.fold_in(seeds[4], 1), 0, 4095).astype(jnp.int32)
    gains = jnp.clip(1.0 + 0.1 * jax.random.normal(seeds[5], (2, D, 2), jnp.float32), 0.5, 1.5).astype(jnp.bfloat16)
    w_qkv = scatter_about(seeds[6], (2, D, 3 * D), D ** -0.5, 0.21875, ((0, 2), (1, 64)))
    w_out = scatter_about(seeds[7], (2, D, D), (D // 64) ** -0.5, 1.75, ((0, 2), (1, 64)))
    router = scatter_about(seeds[8], (2, D, EXPERTS), (2 * D) ** -0.5, 0.15625, ((0, 2), (1, 64)))
    shared_gate_up = scatter_about(seeds[9], (2, D, 2 * SHARED_FF), D ** -0.5, 0.21875, ((0, 2), (1, 64)))
    shared_down = scatter_about(seeds[10], (2, SHARED_FF, D), SHARED_FF ** -0.5, 0.125, ((0, 2), (1, 64)))
    expert_gate_up = scatter_about(seeds[11], (2, EXPERTS, D, 2 * FF), D ** -0.5, 0.21875, ((0, 2), (1, 8), (2, 8)))
    expert_down = scatter_about(seeds[12], (2, EXPERTS, FF, D), FF ** -0.5, 0.125, ((0, 2), (1, 8), (2, 8)))
    return dict(x_in=x_in, cotangent=cotangent, group_ids=group_ids, routes=routes, priority=priority, gains=gains, w_qkv=w_qkv, w_out=w_out, router=router, shared_gate_up=shared_gate_up, shared_down=shared_down, expert_gate_up=expert_gate_up, expert_down=expert_down)


EPS = 1e-06
NEG = -1e+30
HIGH = lax.Precision.HIGHEST

@jax.custom_vjp
def low(v):
    return lax.optimization_barrier(v.astype(jnp.bfloat16)).astype(jnp.float32)

@jax.custom_vjp
def low_back(v):
    return v

def low_keep(v):
    return (low(v), None)

def low_pass(kept, grad):
    return (grad,)

def back_keep(v):
    return (v, None)

def back_low(kept, grad):
    return (low(grad),)
low.defvjp(low_keep, low_pass)
low_back.defvjp(back_keep, back_low)

def rms_scale(values, gain):
    mean_sq = lax.optimization_barrier(jnp.mean(values * values, axis=-1, keepdims=True))
    return values * lax.rsqrt(mean_sq + EPS) * gain

def swiglu(joined):
    half_width = joined.shape[-1] // 2
    return jax.nn.silu(joined[..., :half_width]) * joined[..., half_width:]

def rotary(values, angles):
    half_width = values.shape[-1] // 2
    cosine = jnp.cos(angles)[:, None, :]
    sine = jnp.sin(angles)[:, None, :]
    first_half = values[..., :half_width]
    second_half = values[..., half_width:]
    return jnp.concatenate([first_half * cosine - second_half * sine, second_half * cosine + first_half * sine], axis=-1)

def rotary_angles(positions, head_width):
    half_width = head_width // 2
    frequency = jnp.exp(-math.log(10000.0) * jnp.arange(half_width, dtype=jnp.float32) / half_width)
    return positions.astype(jnp.float32)[:, None] * frequency[None, :]

def token_positions(group_row, label_count):
    labels = jnp.arange(label_count + 1, dtype=jnp.int32)
    member = (group_row[:, None] == labels[None, :]).astype(jnp.int32)
    run_sizes = lax.optimization_barrier(jnp.sum(member, axis=0))
    run_starts = jnp.cumsum(run_sizes) - run_sizes
    first_index = lax.optimization_barrier(jnp.sum(member * run_starts[None, :], axis=1))
    token_index = jnp.arange(group_row.shape[0], dtype=jnp.int32)
    return jnp.where(group_row == 0, token_index, run_sizes[0] + token_index - first_index)

def slot_of_pairs(route_block, rank_block, capacity):
    pair_count = route_block.shape[0] * route_block.shape[1]
    expert_of = route_block.reshape(-1)
    order_key = rank_block.reshape(-1) * pair_count + jnp.arange(pair_count, dtype=jnp.int32)
    earlier = (expert_of[None, :] == expert_of[:, None]) & (order_key[None, :] < order_key[:, None])
    slot_number = lax.optimization_barrier(jnp.sum(earlier.astype(jnp.int32), axis=1))
    kept_pair = slot_number < capacity
    place_of = expert_of * capacity + jnp.minimum(slot_number, capacity - 1)
    return (place_of, kept_pair)

def matmul(left, right):
    return jnp.dot(left, right, precision=HIGH)

def attention(query_heads, key_heads, value_heads, group_row):
    seq_len = query_heads.shape[0]
    block_width = math.gcd(seq_len, 512)
    score_scale = 1.0 / math.sqrt(HEAD_DIM)
    index_all = jnp.arange(seq_len, dtype=jnp.int32)
    blocks = (query_heads.reshape(seq_len // block_width, block_width, HEADS, HEAD_DIM), index_all.reshape(-1, block_width), group_row.reshape(-1, block_width))

    def one_block(block):
        query_block, query_index, query_group = block
        raw_scores = low_back(jnp.einsum('qhd,khd->hqk', query_block, key_heads, precision=HIGH) * score_scale)
        visible = (index_all[None, :] <= query_index[:, None]) & ((group_row[None, :] == 0) | (group_row[None, :] == query_group[:, None]))
        scores = jnp.where(visible[None], raw_scores, NEG)
        weights = low(jax.nn.softmax(scores, axis=-1))
        return jnp.einsum('hqk,khd->qhd', weights, value_heads, precision=HIGH)
    result = lax.map(jax.checkpoint(one_block), blocks)
    return result.reshape(seq_len, HEADS * HEAD_DIM)

def expert_mix(normed, gates, gate_up, down_proj, place_of, kept_pair):

    def one_block(normed_block, place_block, kept_block, gate_block):
        pair_rows = jnp.repeat(normed_block, TOP, axis=0)
        slots_all = jnp.arange(EXPERTS * CAP, dtype=jnp.int32)
        onehot = jnp.where((place_block[None, :] == slots_all[:, None]) & kept_block[None, :], 1.0, 0.0).astype(normed.dtype)
        sent = low_back(matmul(onehot, pair_rows)).reshape(EXPERTS, CAP, D)
        joined = low_back(jnp.einsum('ecd,edf->ecf', sent, gate_up, precision=HIGH))
        hidden = low(swiglu(joined))
        returned = low_back(low(jnp.einsum('ecf,efd->ecd', hidden, down_proj, precision=HIGH))).reshape(EXPERTS * CAP, D)
        picked = jnp.where(kept_block[:, None], jnp.take(returned, place_block, axis=0), 0.0)
        return lax.optimization_barrier(jnp.sum((picked * gate_block.reshape(-1)[:, None]).reshape(ROWS, TOP, D), axis=1))
    mixed = jax.vmap(one_block)(normed.reshape(N_CTX, ROWS, D), place_of, kept_pair, gates.reshape(N_CTX, ROWS, TOP))
    return mixed.reshape(SEQ, D)

def layer(state, weights, angles, group_row, place_of, kept_pair, route):
    gains, w_qkv, w_out, router, shared_gate_up, shared_down, expert_gate_up, expert_down = weights
    seq_len = state.shape[0]
    heads_shape = (seq_len, HEADS, HEAD_DIM)
    normed_attn = low(rms_scale(state, gains[:, 0]))
    joined_qkv = low_back(matmul(normed_attn, w_qkv))
    queries = low(rotary(joined_qkv[:, :D].reshape(heads_shape), angles))
    keys = low(rotary(joined_qkv[:, D:2 * D].reshape(heads_shape), angles))
    values = low(joined_qkv[:, 2 * D:].reshape(heads_shape))
    attended = low_back(low(attention(queries, keys, values, group_row)))
    residual = state + low_back(matmul(attended, w_out))
    normed_ffn = low(rms_scale(residual, gains[:, 1]))
    logits = matmul(normed_ffn, router)
    gates = jax.nn.softmax(jnp.take_along_axis(logits, route, axis=1), axis=-1)
    shared_joined = low_back(matmul(normed_ffn, shared_gate_up))
    shared_out = low_back(matmul(low(swiglu(shared_joined)), shared_down))
    mixed = expert_mix(normed_ffn, gates, expert_gate_up, expert_down, place_of, kept_pair)
    return residual + shared_out + mixed

def reference(x_in, cotangent, group_ids, routes, priority, gains, w_qkv, w_out, router, shared_gate_up, shared_down, expert_gate_up, expert_down):
    stacked = (gains, w_qkv, w_out, router, shared_gate_up, shared_down, expert_gate_up, expert_down)
    first_weights = tuple((weight_pair[0].astype(jnp.float32) for weight_pair in stacked))
    second_weights = tuple((weight_pair[1].astype(jnp.float32) for weight_pair in stacked))
    item_count = MICRO * GROUPS
    route_all = routes.reshape(2, item_count, SEQ, TOP)
    rank_all = priority.reshape(2, item_count, SEQ, TOP)
    inputs_all = (x_in.reshape(item_count, SEQ, D), cotangent.reshape(item_count, SEQ, D), group_ids.reshape(item_count, SEQ), route_all[0], route_all[1], rank_all[0], rank_all[1])

    def route_slots(route, rank):
        return jax.vmap(lambda route_block, rank_block: slot_of_pairs(route_block, rank_block, CAP))(route.reshape(N_CTX, ROWS, TOP), rank.reshape(N_CTX, ROWS, TOP))

    def one_item(running, entry):
        inputs, grads_out, group_row, route_first, route_second, rank_first, rank_second = entry
        angles = rotary_angles(token_positions(group_row, CONT), HEAD_DIM)
        place_first, kept_first = route_slots(route_first, rank_first)
        place_second, kept_second = route_slots(route_second, rank_second)

        def first_layer(state, weights):
            return low(layer(state, weights, angles, group_row, place_first, kept_first, route_first))

        def second_layer(state, weights):
            return layer(state, weights, angles, group_row, place_second, kept_second, route_second)
        hidden, back_first = jax.vjp(first_layer, inputs.astype(jnp.float32), first_weights)
        final, back_second = jax.vjp(second_layer, hidden, second_weights)
        hidden_grad, second_grads = back_second(grads_out.astype(jnp.float32))
        input_grad, first_grads = back_first(low(hidden_grad))
        running = (jax.tree.map(jnp.add, running[0], first_grads), jax.tree.map(jnp.add, running[1], second_grads))
        return (running, (hidden.astype(jnp.bfloat16), final.astype(jnp.bfloat16), input_grad, hidden_grad))
    zeros_start = (tuple((jnp.zeros_like(weight) for weight in first_weights)), tuple((jnp.zeros_like(weight) for weight in second_weights)))
    (grads_first, grads_second), (hiddens, finals, first_input_grads, hidden_grads) = lax.scan(one_item, zeros_start, inputs_all)
    section_outputs = jnp.stack([hiddens, finals]).reshape(2, MICRO, GROUPS, SEQ, D)
    input_grads = jnp.stack([first_input_grads, hidden_grads]).reshape(2, MICRO, GROUPS, SEQ, D)
    weight_grads = tuple((jnp.stack([first_grad, second_grad]) for first_grad, second_grad in zip(grads_first, grads_second)))
    return (section_outputs, input_grads, weight_grads[0], weight_grads[1], weight_grads[2], weight_grads[3], weight_grads[4], weight_grads[5], weight_grads[6], weight_grads[7])
```

```python
import functools
import math

import jax
import jax.numpy as jnp
from jax import lax
from jax.experimental import pallas as pl
from jax.experimental.pallas import tpu as pltpu
from jax.sharding import PartitionSpec as P

MESH = pl.DeviceIdType.MESH
ANY = pl.BlockSpec(memory_space=pl.ANY)
VMEM = pl.BlockSpec(memory_space=pltpu.VMEM)
DMA = pltpu.SemaphoreType.DMA

D = 768
FF = 2048
WIDE = 3072
SMALL = 128
PACK = WIDE + 2 * FF + SMALL
OWN = 12
HEADS = 12
HEAD_DIM = 64
TOP = 2
CONT = 8
EXPERTS = 8
SEQ = 1024
ROWS = 128
CAP = 40
PAD_CAP = 48
SLOTS = EXPERTS * PAD_CAP
SCALE = 1.0 / math.sqrt(HEAD_DIM)
EPS = 1e-06
NEG = -1e30
HIGH = lax.Precision.HIGHEST


def place_ids():
    section = lax.axis_index("section")
    ctx = lax.axis_index("ctx")
    fsdp = lax.axis_index("fsdp")
    return section, ctx // 4, lax.rem(ctx, 4), fsdp // 2, lax.rem(fsdp, 2)


def ctx_of(half, ring):
    return lax.rem(half + 2, 2) * 4 + lax.rem(ring + 4, 4)


def fsdp_of(ring, half):
    return lax.rem(ring + 4, 4) * 2 + lax.rem(half + 2, 2)


def neighbours():
    section, a, z, y, h = place_ids()
    ctx, fsdp = ctx_of(a, z), fsdp_of(y, h)
    return dict(
        core=(1 - section, ctx, fsdp),
        zp=(section, ctx_of(a, z + 1), fsdp),
        zm=(section, ctx_of(a, z - 1), fsdp),
        zx=(section, ctx_of(a + 1, z), fsdp),
        yp=(section, ctx, fsdp_of(y + 1, h)),
        ym=(section, ctx, fsdp_of(y - 1, h)),
        yx=(section, ctx, fsdp_of(y, h + 1)),
    )


def greet(devices):
    barrier = pltpu.get_barrier_semaphore()
    for device in devices:
        pl.semaphore_signal(barrier, inc=1, device_id=device, device_id_type=MESH)
    pl.semaphore_wait(barrier, len(devices))


def rows_at(ref, block, rows, part=None):
    if part is None:
        return ref.at[pl.ds(pl.multiple_of(block * rows, 16), rows)]
    half = rows // 2
    return ref.at[pl.ds(pl.multiple_of(block * rows + part * half, 16), half)]


class Hop:
    def __init__(self, sources, targets, device, send, recv):
        self.copies = [
            pltpu.make_async_remote_copy(s, t, send.at[i], recv.at[i], device_id=device, device_id_type=MESH)
            for i, (s, t) in enumerate(zip(sources, targets))
        ]

    def start(self):
        for copy in self.copies:
            copy.start()
        return self

    def wait_recv(self):
        for copy in self.copies:
            copy.wait_recv()

    def wait_send(self):
        for copy in self.copies:
            copy.wait_send()


def gather_kernel(
    pack, sd, egu, ed, sel,
    w_wide, w_gu, w_small, w_sd, w_egu, w_ed,
    packs, own_wide, own_gu, own_small, own_sd,
    s_send, s_recv, d_send, d_recv, e_send, e_recv, c_send, c_recv, l_sem,
):
    section, a, z, y, h = place_ids()
    ctx, fsdp = ctx_of(a, z), fsdp_of(y, h)
    near = neighbours()
    others = [(dy, dh) for dy in (1, 3, 2, 0) for dh in (0, 1) if (dy, dh) != (0, 0)]
    f_peers = [(section, ctx, fsdp_of(y + dy, h + dh)) for dy, dh in others]
    greet([near["core"], near["zp"], near["zm"], near["zx"]] + f_peers)

    first = []
    for k, device in enumerate(f_peers):
        hop = Hop(
            [pack, sd], [rows_at(packs, fsdp, 16), rows_at(own_sd, fsdp, 32)], device, s_send.at[k], s_recv.at[k]
        )
        first.append(hop.start())
    locals_ = [
        pltpu.make_async_copy(pack, rows_at(packs, fsdp, 16), l_sem.at[0]),
        pltpu.make_async_copy(sd, rows_at(own_sd, fsdp, 32), l_sem.at[1]),
    ]
    for copy in locals_:
        copy.start()

    me_w = [w.at[section] for w in (w_wide, w_gu, w_small, w_sd)]
    me_e = [w.at[section] for w in (w_egu, w_ed)]
    d_rows = (96, 96, 96, 256)
    e_rows = (96, 256)

    def dense(block, part=None):
        return [rows_at(w, block, r, part) for w, r in zip(me_w, d_rows)]

    def expert(block, part=None):
        return [rows_at(w, block, r, part) for w, r in zip(me_e, e_rows)]

    cores = []

    def to_core(refs, block_refs, index):
        cores.append(Hop(refs, block_refs, near["core"], c_send.at[index], c_recv.at[index]).start())

    for hop in first:
        hop.wait_recv()
    for copy in locals_:
        copy.wait()

    e_own = [egu, ed]
    e_hops = {}

    def e_hop(index, refs, block_refs, device):
        e_hops[index] = Hop(refs, block_refs, near[device], e_send.at[index], e_recv.at[index]).start()

    for index, device in ((0, "yp"), (1, "ym"), (2, "yx")):
        e_hop(index, e_own, expert(fsdp), device)

    for target, start, width in ((own_wide, 0, WIDE), (own_gu, WIDE, 2 * FF), (own_small, WIDE + 2 * FF, SMALL)):
        step = min(width, 512)

        @pl.loop(0, width // step)
        def _(j, target=target, start=start, step=step):
            off = pl.multiple_of(j * step, 128)
            block = packs[:, pl.ds(start + off, step)]
            target[:, pl.ds(off, step)] = jnp.dot(sel[...], block, preferred_element_type=jnp.float32).astype(jnp.bfloat16)

    d_own = [own_wide, own_gu, own_small, own_sd]
    d_hops = {}

    def d_hop(index, refs, block_refs, device):
        d_hops[index] = Hop(refs, block_refs, near[device], d_send.at[index], d_recv.at[index]).start()

    for index, device in ((0, "zp"), (1, "zm"), (2, "zx")):
        d_hop(index, d_own, dense(ctx), device)
    own_copies = [
        pltpu.make_async_copy(s, t, l_sem.at[2 + i])
        for i, (s, t) in enumerate(zip(d_own + e_own, dense(ctx) + expert(fsdp)))
    ]
    for copy in own_copies:
        copy.start()
    to_core(d_own + e_own, dense(ctx) + expert(fsdp), 0)

    def e_block(dy, dh):
        return fsdp_of(y + dy, h + dh)

    def d_block(dz, da):
        return ctx_of(a + da, z + dz)

    def e_pass(index, block, part, device):
        e_hop(index, expert(block, part), expert(block, part), device)

    def d_pass(index, block, part, device):
        d_hop(index, dense(block, part), dense(block, part), device)

    e_hops[0].wait_recv()
    e_pass(3, e_block(-1, 0), 0, "yp")
    e_hops[1].wait_recv()
    e_pass(4, e_block(1, 0), 1, "ym")
    d_hops[0].wait_recv()
    d_pass(3, d_block(-1, 0), 0, "zp")
    d_hops[1].wait_recv()
    d_pass(4, d_block(1, 0), 1, "zm")
    e_hops[2].wait_recv()
    e_pass(5, e_block(0, 1), None, "yp")
    e_pass(6, e_block(0, 1), None, "ym")
    d_hops[2].wait_recv()
    d_pass(5, d_block(0, 1), None, "zp")
    d_pass(6, d_block(0, 1), None, "zm")
    to_core(dense(d_block(-1, 0)) + expert(e_block(-1, 0)), dense(d_block(-1, 0)) + expert(e_block(-1, 0)), 1)
    to_core(dense(d_block(1, 0)) + expert(e_block(1, 0)), dense(d_block(1, 0)) + expert(e_block(1, 0)), 2)
    to_core(dense(d_block(0, 1)) + expert(e_block(0, 1)), dense(d_block(0, 1)) + expert(e_block(0, 1)), 3)
    d_hops[3].wait_recv()
    d_hops[4].wait_recv()
    d_pass(7, d_block(2, 0), None, "zx")
    e_hops[3].wait_recv()
    e_hops[4].wait_recv()
    to_core(dense(d_block(2, 0)) + expert(e_block(2, 0)), dense(d_block(2, 0)) + expert(e_block(2, 0)), 4)
    e_hops[5].wait_recv()
    e_pass(7, e_block(-1, 1), 0, "yp")
    e_hops[6].wait_recv()
    e_pass(8, e_block(1, 1), 1, "ym")
    d_hops[5].wait_recv()
    to_core(dense(d_block(-1, 1)) + expert(e_block(-1, 1)), dense(d_block(-1, 1)) + expert(e_block(-1, 1)), 5)
    d_hops[6].wait_recv()
    to_core(dense(d_block(1, 1)) + expert(e_block(1, 1)), dense(d_block(1, 1)) + expert(e_block(1, 1)), 6)
    d_hops[7].wait_recv()
    e_hops[7].wait_recv()
    e_hops[8].wait_recv()
    to_core(dense(d_block(2, 1)) + expert(e_block(2, 1)), dense(d_block(2, 1)) + expert(e_block(2, 1)), 7)
    for copy in own_copies:
        copy.wait()
    for hop in first + list(d_hops.values()) + list(e_hops.values()):
        hop.wait_send()
    for hop in cores:
        hop.wait_recv()
        hop.wait_send()


def gather_weights(pack, sd, egu, ed):
    rows = jnp.arange(96)
    cols = jnp.arange(128)
    sel = ((rows[:, None] // OWN == cols[None, :] // 16) & (rows[:, None] % OWN == cols[None, :] % 16)).astype(jnp.bfloat16)
    bf = jnp.bfloat16
    shapes = [(2, D, WIDE), (2, D, 2 * FF), (2, D, SMALL), (2, FF, D), (2, D, 2 * FF), (2, FF, D)]
    return pl.pallas_call(
        gather_kernel,
        out_shape=[jax.ShapeDtypeStruct(s, bf) for s in shapes],
        in_specs=[ANY, ANY, ANY, ANY, VMEM],
        out_specs=[ANY] * 6,
        scratch_shapes=[
            pltpu.VMEM((128, PACK), bf),
            pltpu.VMEM((96, WIDE), bf),
            pltpu.VMEM((96, 2 * FF), bf),
            pltpu.VMEM((96, SMALL), bf),
            pltpu.VMEM((256, D), bf),
            DMA((7, 2)), DMA((7, 2)),
            DMA((8, 4)), DMA((8, 4)),
            DMA((9, 2)), DMA((9, 2)),
            DMA((8, 6)), DMA((8, 6)),
            DMA((8,)),
        ],
        compiler_params=pltpu.CompilerParams(collective_id=0, has_side_effects=True, vmem_limit_bytes=48 << 20),
        name="gather_weights",
    )(pack, sd, egu, ed, sel)


def exchange_kernel(eight_from, with_eight, with_four, *refs):
    count = int(with_eight) + int(with_four)
    sources, targets = refs[:count], refs[count : 2 * count]
    send8, recv8, send4, recv4, l_sem = refs[2 * count :]
    section, a, z, y, h = place_ids()
    fsdp = fsdp_of(y, h)
    ctx = ctx_of(a, z)
    offsets = [(0, 1), (0, 3), (0, 2)]
    if with_eight:
        offsets = [(1, 0), (1, 1), (1, 3), (1, 2)] + offsets
    peers = [(ctx_of(a + da, z + dz), lax.rem(z + dz, 4)) for da, dz in offsets]
    greet([(section, c, fsdp) for c, _ in peers])
    copies = []
    for k, ((da, dz), (c, zz)) in enumerate(zip(offsets, peers)):
        device = (section, c, fsdp)
        if with_eight:
            block = c if eight_from == 8 else zz
            copies.append(
                pltpu.make_async_remote_copy(
                    sources[0].at[block], targets[0].at[ctx], send8.at[k], recv8.at[k], device_id=device, device_id_type=MESH
                )
            )
        if with_four and da == 0:
            copies.append(
                pltpu.make_async_remote_copy(
                    sources[-1].at[zz], targets[-1].at[z], send4.at[k], recv4.at[k], device_id=device, device_id_type=MESH
                )
            )
    for copy in copies:
        copy.start()
    stays = []
    if with_eight:
        stays.append(pltpu.make_async_copy(sources[0].at[ctx if eight_from == 8 else z], targets[0].at[ctx], l_sem.at[0]))
    if with_four:
        stays.append(pltpu.make_async_copy(sources[-1].at[z], targets[-1].at[z], l_sem.at[1]))
    for copy in stays:
        copy.start()
    for copy in stays + copies:
        copy.wait()


def exchange(name, collective_id, eight=None, four=None):
    arrays = [v for v in (eight, four) if v is not None]
    shapes = []
    if eight is not None:
        shapes.append(jax.ShapeDtypeStruct((8,) + eight.shape[1:], eight.dtype))
    if four is not None:
        shapes.append(jax.ShapeDtypeStruct(four.shape, four.dtype))
    return pl.pallas_call(
        functools.partial(exchange_kernel, 0 if eight is None else eight.shape[0], eight is not None, four is not None),
        out_shape=shapes,
        in_specs=[ANY] * len(arrays),
        out_specs=[ANY] * len(arrays),
        scratch_shapes=[DMA((7,)), DMA((7,)), DMA((7,)), DMA((7,)), DMA((2,))],
        compiler_params=pltpu.CompilerParams(collective_id=collective_id, has_side_effects=True),
        name=name,
    )(*arrays)


def visible_keys(qidx, qlab, klab):
    kidx = lax.broadcasted_iota(jnp.int32, (qidx.shape[0], klab.shape[1]), 1)
    return (kidx <= qidx) & ((klab == 0) | (klab == qlab))


def attend_kernel(q_ref, kv_ref, qidx_ref, qlab_ref, klab_ref, o_ref, lse_ref):
    seen = visible_keys(qidx_ref[...], qlab_ref[...], klab_ref[...])
    for head in range(3):
        q = q_ref[:, 64 * head : 64 * head + 64]
        k = kv_ref[:, 64 * head : 64 * head + 64]
        v = kv_ref[:, 192 + 64 * head : 256 + 64 * head]
        scores = lax.dot_general(q, k, (((1,), (1,)), ((), ())), preferred_element_type=jnp.float32) * SCALE
        scores = jnp.where(seen, scores, NEG)
        top = jnp.max(scores, axis=-1, keepdims=True)
        weights = jnp.exp(scores - top)
        total = jnp.sum(weights, axis=-1, keepdims=True)
        probs = (weights / total).astype(jnp.bfloat16)
        out = jnp.dot(probs, v, preferred_element_type=jnp.float32)
        o_ref[:, 64 * head : 64 * head + 64] = out.astype(jnp.bfloat16)
        lse_ref[:, head : head + 1] = top + jnp.log(total)


def attend_back_kernel(q_ref, kv_ref, do_ref, lse_ref, qidx_ref, qlab_ref, klab_ref, dq_ref, dkv_ref, acc):
    step = pl.program_id(0)

    @pl.when(step == 0)
    def _():
        acc[...] = jnp.zeros_like(acc)

    seen = visible_keys(qidx_ref[...], qlab_ref[...], klab_ref[...])
    rows = (((0,), (0,)), ((), ()))
    cols = (((1,), (1,)), ((), ()))
    for head in range(3):
        span = slice(64 * head, 64 * head + 64)
        vspan = slice(192 + 64 * head, 256 + 64 * head)
        q = q_ref[:, span]
        k = kv_ref[:, span]
        v = kv_ref[:, vspan]
        do = do_ref[:, span]
        scores = lax.dot_general(q, k, cols, preferred_element_type=jnp.float32) * SCALE
        probs = jnp.where(seen, jnp.exp(scores - lse_ref[:, head : head + 1]), 0.0)
        dprobs = lax.dot_general(do, v, cols, preferred_element_type=jnp.float32)
        delta = jnp.sum(probs * dprobs, axis=-1, keepdims=True)
        dscores = (probs * (dprobs - delta)).astype(jnp.bfloat16)
        dq_ref[:, span] = (jnp.dot(dscores, k, preferred_element_type=jnp.float32) * SCALE).astype(jnp.bfloat16)
        acc[:, span] += lax.dot_general(dscores, q, rows, preferred_element_type=jnp.float32) * SCALE
        acc[:, vspan] += lax.dot_general(probs.astype(jnp.bfloat16), do, rows, preferred_element_type=jnp.float32)

    @pl.when(step == pl.num_programs(0) - 1)
    def _():
        dkv_ref[...] = acc[...].astype(jnp.bfloat16)


def row_block(width):
    return pl.BlockSpec((128, width), lambda i: (i, 0))


def whole(rows, width):
    return pl.BlockSpec((rows, width), lambda i: (0, 0))


def attend(q, kv, qidx, qlab, klab):
    return pl.pallas_call(
        attend_kernel,
        grid=(4,),
        out_shape=[jax.ShapeDtypeStruct((512, 192), jnp.bfloat16), jax.ShapeDtypeStruct((512, 128), jnp.float32)],
        in_specs=[row_block(192), whole(1024, 384), row_block(1), row_block(1), whole(1, 1024)],
        out_specs=[row_block(192), row_block(128)],
        compiler_params=pltpu.CompilerParams(vmem_limit_bytes=40 << 20),
        name="attend",
    )(q, kv, qidx, qlab, klab)


def attend_back(q, kv, do, lse, qidx, qlab, klab):
    return pl.pallas_call(
        attend_back_kernel,
        grid=(4,),
        out_shape=[jax.ShapeDtypeStruct((512, 192), jnp.bfloat16), jax.ShapeDtypeStruct((1024, 384), jnp.bfloat16)],
        in_specs=[row_block(192), whole(1024, 384), row_block(192), row_block(128), row_block(1), row_block(1), whole(1, 1024)],
        out_specs=[row_block(192), whole(1024, 384)],
        scratch_shapes=[pltpu.VMEM((1024, 384), jnp.float32)],
        compiler_params=pltpu.CompilerParams(vmem_limit_bytes=40 << 20),
        name="attend_back",
    )(q, kv, do, lse, qidx, qlab, klab)


LEFT = (("na", D, 128), ("at", D, 128), ("nf", D, 128), ("sh", FF, 128), ("rc", D, SLOTS), ("hd", FF, SLOTS))
RIGHT = (("qkv", 128, 3 * D), ("pr", 128, D), ("gu", 128, 2 * FF), ("sd", 128, D), ("j", SLOTS, 2 * FF), ("er", SLOTS, D))
N_OPS = len(LEFT) + len(RIGHT)
DENSE = (("wide", "na", "qkv", 96, 0, 3 * D), ("wide", "at", "pr", 96, 3 * D, D), ("gu", "nf", "gu", 96, 0, 2 * FF), ("sd", "sh", "sd", 256, 0, D))
EXPERT = (("egu", "rc", "j", 96, 0, 2 * FF), ("ed", "hd", "er", 256, 0, D))


def grads_kernel(*refs):
    lower, upper = refs[:N_OPS], refs[N_OPS : 2 * N_OPS]
    small, sel_t = refs[2 * N_OPS : 2 * N_OPS + 2]
    out_pack, out_sd, out_egu, out_ed = refs[2 * N_OPS + 2 : 2 * N_OPS + 6]
    rest = refs[2 * N_OPS + 6 :]
    held = rest[:N_OPS]
    (b_wide, b_gu, b_small, b_sd, c_gu, c_sd, packs, in_pack, in_sd,
     o_send, o_recv, o_local, d_send, d_recv, e_send, e_recv, s_send, s_recv) = rest[N_OPS:]
    names = [n for n, _, _ in LEFT] + [n for n, _, _ in RIGHT]
    ops = dict(zip(names, held))
    section, a, z, y, h = place_ids()
    ctx, fsdp = ctx_of(a, z), fsdp_of(y, h)
    near = neighbours()
    others = [(dy, dh) for dy in (1, 3, 2, 0) for dh in (0, 1) if (dy, dh) != (0, 0)]
    f_peers = [(section, ctx, fsdp_of(y + dy, h + dh)) for dy, dh in others]
    greet([near["core"], near["zp"], near["zm"], near["zx"]] + f_peers)

    def slot_of(i, which):
        n, r, c = (LEFT + RIGHT)[i]
        if i < len(LEFT):
            return held[i].at[:, pl.ds(which * c, c)]
        return held[i].at[pl.ds(which * r, r)]

    def bring(mine, theirs):
        for i in range(N_OPS):
            pltpu.make_async_remote_copy(
                theirs[i], slot_of(i, 1), o_send.at[i], o_recv.at[i], device_id=near["core"], device_id_type=MESH
            ).start()
            pltpu.make_async_copy(mine[i], slot_of(i, 0), o_local.at[i]).start()

    @pl.when(section == 0)
    def _():
        bring(lower, upper)

    @pl.when(section == 1)
    def _():
        bring(upper, lower)

    def ready(wanted):
        for i, n in enumerate(names):
            if n in wanted:
                pltpu.make_async_copy(lower[i], slot_of(i, 0), o_local.at[i]).wait()
                pltpu.make_async_remote_copy(
                    lower[i], slot_of(i, 1), o_send.at[i], o_recv.at[i], device_id=near["core"], device_id_type=MESH
                ).wait_recv()

    kinds = dict(wide=b_wide, gu=b_gu, small=b_small, sd=b_sd, egu=c_gu, ed=c_sd)

    def combine(pieces, block, slot, adds=(), part=None, target=None):
        for kind, left, right, rows, first, width in pieces:
            n = rows if part is None else rows // 2
            off = 0 if part is None else part * n
            lhs_rows = pl.ds(pl.multiple_of(block * rows + off, 16), n)

            @pl.loop(0, width // 256)
            def _(j, kind=kind, left=left, right=right, first=first, n=n, off=off, lhs_rows=lhs_rows):
                at = pl.ds(pl.multiple_of(j * 256, 256), 256)
                to = pl.ds(pl.multiple_of(first + j * 256, 256), 256)
                total = jnp.dot(ops[left][lhs_rows, :], ops[right][:, at], preferred_element_type=jnp.float32)
                for other in adds:
                    total += kinds[kind][other, off : off + n, to].astype(jnp.float32)
                if target is None:
                    kinds[kind][slot, off : off + n, to] = total.astype(jnp.bfloat16)
                else:
                    target[kind][off : off + n, to] = total

        if pieces is DENSE:
            n = 96 if part is None else 48
            off = 0 if part is None else part * n
            total = small[pl.ds(pl.multiple_of(block * 96 + off, 16), n), :]
            for other in adds:
                total += b_small[other, off : off + n, :].astype(jnp.float32)
            b_small[slot, off : off + n, :] = total.astype(jnp.bfloat16)

    def views(pieces, slot, part):
        if pieces is DENSE:
            bufs = ((b_wide, 96), (b_gu, 96), (b_small, 96), (b_sd, 256))
        else:
            bufs = ((c_gu, 96), (c_sd, 256))
        return [rows_at(b.at[slot], 0, r, part) for b, r in bufs]

    hops = {}

    def send(pieces, index, slot, to_slot, device, part=None):
        sems = (d_send, d_recv) if pieces is DENSE else (e_send, e_recv)
        tag = "d" if pieces is DENSE else "e"
        hops[tag, index] = Hop(
            views(pieces, slot, part), views(pieces, to_slot, part), near[device], sems[0].at[index], sems[1].at[index]
        ).start()

    def d_block(dz, da):
        return ctx_of(a + da, z + dz)

    def e_block(dy, dh):
        return fsdp_of(y + dy, h + dh)

    ready(("na", "qkv", "at", "pr", "nf", "gu", "sh", "sd"))
    combine(DENSE, d_block(2, 1), 0)
    send(DENSE, 0, 0, 1, "zx")
    combine(DENSE, d_block(-1, 1), 2)
    send(DENSE, 1, 2, 5, "zm")
    combine(DENSE, d_block(1, 1), 3)
    send(DENSE, 2, 3, 6, "zp")
    ready(("rc", "j", "hd", "er"))
    combine(EXPERT, e_block(2, 1), 0)
    send(EXPERT, 0, 0, 4, "ym", 0)
    send(EXPERT, 1, 0, 4, "yp", 1)
    combine(EXPERT, e_block(2, 0), 1)
    send(EXPERT, 2, 1, 5, "ym", 0)
    send(EXPERT, 3, 1, 5, "yp", 1)
    hops["d", 0].wait_recv()
    combine(DENSE, d_block(2, 0), 1, (1,))
    send(DENSE, 3, 1, 4, "zm", 0)
    send(DENSE, 4, 1, 4, "zp", 1)
    combine(EXPERT, e_block(-1, 1), 2, (), 1)
    combine(EXPERT, e_block(1, 1), 3, (), 0)
    hops["e", 0].wait_recv()
    combine_half(combine, EXPERT, e_block(-1, 1), 2, 4, 0)
    send(EXPERT, 4, 2, 6, "ym")
    hops["e", 1].wait_recv()
    combine_half(combine, EXPERT, e_block(1, 1), 3, 4, 1)
    send(EXPERT, 5, 3, 7, "yp")
    hops["d", 0].wait_send()
    combine(DENSE, d_block(-1, 0), 0, (), 1)
    hops["d", 3].wait_recv()
    combine_half(combine, DENSE, d_block(-1, 0), 0, 4, 0)
    send(DENSE, 5, 0, 7, "zm")
    hops["d", 3].wait_send()
    hops["d", 4].wait_send()
    combine(DENSE, d_block(1, 0), 1, (), 0)
    hops["d", 4].wait_recv()
    combine_half(combine, DENSE, d_block(1, 0), 1, 4, 1)
    send(DENSE, 6, 1, 8, "zp")
    hops["e", 0].wait_send()
    hops["e", 1].wait_send()
    combine(EXPERT, e_block(-1, 0), 0, (), 1)
    hops["e", 2].wait_recv()
    combine_half(combine, EXPERT, e_block(-1, 0), 0, 5, 0)
    send(EXPERT, 6, 0, 8, "ym")
    hops["e", 2].wait_send()
    hops["e", 3].wait_send()
    combine(EXPERT, e_block(1, 0), 1, (), 0)
    hops["e", 3].wait_recv()
    combine_half(combine, EXPERT, e_block(1, 0), 1, 5, 1)
    send(EXPERT, 7, 1, 9, "yp")
    hops["d", 1].wait_recv()
    hops["d", 2].wait_recv()
    combine(DENSE, d_block(0, 1), 5, (5, 6))
    send(DENSE, 7, 5, 9, "zx")
    hops["e", 4].wait_recv()
    hops["e", 5].wait_recv()
    combine(EXPERT, e_block(0, 1), 6, (6, 7))
    send(EXPERT, 8, 6, 10, "yx")
    for index in (5, 6, 7):
        hops["d", index].wait_recv()
    combine(DENSE, ctx, 7, (7, 8, 9))

    for kind, start, width in (("wide", 0, WIDE), ("gu", WIDE, 2 * FF), ("small", WIDE + 2 * FF, SMALL)):
        step = min(width, 512)

        @pl.loop(0, width // step)
        def _(j, kind=kind, start=start, step=step):
            off = pl.multiple_of(j * step, 128)
            block = kinds[kind][7, :, pl.ds(off, step)]
            packs[:, pl.ds(start + off, step)] = jnp.dot(sel_t[...], block, preferred_element_type=jnp.float32).astype(jnp.bfloat16)

    last = []
    for k, ((dy, dh), device) in enumerate(zip(others, f_peers)):
        block = e_block(dy, dh)
        last.append(
            Hop(
                [rows_at(packs, block, 16), rows_at(b_sd.at[7], block, 32)],
                [in_pack.at[k], in_sd.at[k]],
                device, s_send.at[k], s_recv.at[k],
            ).start()
        )
    for index in (6, 7, 8):
        hops["e", index].wait_recv()
    combine(EXPERT, fsdp, 0, (8, 9, 10), None, dict(egu=out_egu, ed=out_ed))
    for hop in last:
        hop.wait_recv()

    @pl.loop(0, PACK // 128)
    def _(j):
        at = pl.ds(pl.multiple_of(j * 128, 128), 128)
        total = packs[pl.ds(pl.multiple_of(fsdp * 16, 16), 16), at].astype(jnp.float32)
        for k in range(7):
            total += in_pack[k, :, at].astype(jnp.float32)
        out_pack[:, at] = total

    total = b_sd[7, pl.ds(pl.multiple_of(fsdp * 32, 16), 32), :].astype(jnp.float32)
    for k in range(7):
        total += in_sd[k].astype(jnp.float32)
    out_sd[...] = total
    for hop in list(hops.values())[:]:
        pass
    for key in (("d", 1), ("d", 2), ("d", 5), ("d", 6), ("d", 7), ("e", 4), ("e", 5), ("e", 6), ("e", 7), ("e", 8)):
        hops[key].wait_send()
    for hop in last:
        hop.wait_send()
    for i in range(N_OPS):
        pltpu.make_async_remote_copy(
            lower[i], slot_of(i, 1), o_send.at[i], o_recv.at[i], device_id=near["core"], device_id_type=MESH
        ).wait_send()


def combine_half(combine, pieces, block, slot, half_slot, part):
    combine(pieces, block, slot, (half_slot,), part)


def weight_grads(lower, upper, small):
    rows = jnp.arange(128)
    cols = jnp.arange(96)
    sel_t = ((cols[None, :] // OWN == rows[:, None] // 16) & (cols[None, :] % OWN == rows[:, None] % 16)).astype(jnp.bfloat16)
    bf, f32 = jnp.bfloat16, jnp.float32
    held = [pltpu.VMEM((r, 2 * c), bf) for _, r, c in LEFT] + [pltpu.VMEM((2 * r, c), bf) for _, r, c in RIGHT]
    return pl.pallas_call(
        grads_kernel,
        out_shape=[
            jax.ShapeDtypeStruct((16, PACK), f32),
            jax.ShapeDtypeStruct((32, D), f32),
            jax.ShapeDtypeStruct((96, 2 * FF), f32),
            jax.ShapeDtypeStruct((256, D), f32),
        ],
        in_specs=[ANY] * (2 * N_OPS) + [VMEM, VMEM],
        out_specs=[VMEM] * 4,
        scratch_shapes=held + [
            pltpu.VMEM((10, 96, WIDE), bf),
            pltpu.VMEM((10, 96, 2 * FF), bf),
            pltpu.VMEM((10, 96, SMALL), bf),
            pltpu.VMEM((10, 256, D), bf),
            pltpu.VMEM((11, 96, 2 * FF), bf),
            pltpu.VMEM((11, 256, D), bf),
            pltpu.VMEM((128, PACK), bf),
            pltpu.VMEM((7, 16, PACK), bf),
            pltpu.VMEM((7, 32, D), bf),
            DMA((N_OPS,)), DMA((N_OPS,)), DMA((N_OPS,)),
            DMA((8, 4)), DMA((8, 4)),
            DMA((9, 2)), DMA((9, 2)),
            DMA((7, 2)), DMA((7, 2)),
        ],
        compiler_params=pltpu.CompilerParams(collective_id=5, has_side_effects=True, vmem_limit_bytes=62 << 20),
        name="weight_grads",
    )(*lower, *upper, small, sel_t)


def rms_parts(values):
    scale = lax.rsqrt(jnp.mean(values * values, axis=-1, keepdims=True) + EPS)
    return scale, values * scale


def rms_back(grad, gain, scale, unit):
    inner = grad * gain
    grad_values = scale * (inner - unit * jnp.mean(inner * unit, axis=-1, keepdims=True))
    return grad_values, jnp.sum(grad * unit, axis=0)


def token_positions(group_row):
    labels = jnp.arange(CONT + 1, dtype=jnp.int32)
    member = (group_row[:, None] == labels[None, :]).astype(jnp.int32)
    run_sizes = jnp.sum(member, axis=0)
    run_starts = jnp.cumsum(run_sizes) - run_sizes
    first_index = jnp.sum(member * run_starts[None, :], axis=1)
    token_index = jnp.arange(group_row.shape[0], dtype=jnp.int32)
    return jnp.where(group_row == 0, token_index, run_sizes[0] + token_index - first_index)


def rotation_tables(positions):
    half = HEAD_DIM // 2
    frequency = jnp.exp(-math.log(10000.0) * jnp.arange(half, dtype=jnp.float32) / half)
    angles = positions.astype(jnp.float32)[:, None] * frequency[None, :]
    cosine, sine = jnp.cos(angles), jnp.sin(angles)
    cosine = jnp.tile(jnp.concatenate([cosine, cosine], axis=1), (1, HEADS))
    sine = jnp.tile(jnp.concatenate([-sine, sine], axis=1), (1, HEADS))
    return cosine, sine


def rotate(values, cosine, sine):
    half = HEAD_DIM // 2
    ahead = jnp.concatenate([values[:, half:], values[:, :half]], axis=1)
    behind = jnp.concatenate([values[:, -half:], values[:, :-half]], axis=1)
    lower = lax.broadcasted_iota(jnp.int32, values.shape, 1) % HEAD_DIM < half
    return values * cosine + jnp.where(lower, ahead, behind) * sine


def slot_tables(route, rank):
    pairs = ROWS * TOP
    expert = route.reshape(-1)
    key = rank.reshape(-1) * pairs + jnp.arange(pairs, dtype=jnp.int32)
    earlier = (expert[None, :] == expert[:, None]) & (key[None, :] < key[:, None])
    slot = jnp.sum(earlier.astype(jnp.int32), axis=1)
    place = jnp.where(slot < CAP, expert * PAD_CAP + slot, -1).reshape(ROWS, TOP)
    every = jnp.arange(EXPERTS * PAD_CAP, dtype=jnp.int32)
    return [(place[:, c : c + 1] == every[None, :]) for c in range(TOP)]


def heads_out(values, count):
    return [values[:, 192 * g : 192 * g + 192] for g in range(count)]


def dot(left, right):
    return jnp.dot(left, right, preferred_element_type=jnp.float32)


def dot_t(left, right):
    return lax.dot_general(left, right, (((1,), (1,)), ((), ())), preferred_element_type=jnp.float32)


def t_dot(left, right, precision=None):
    return lax.dot_general(left, right, (((0,), (0,)), ((), ())), precision=precision, preferred_element_type=jnp.float32)


def low(values):
    return values.astype(jnp.bfloat16)


def silu_parts(joined):
    gate, up = joined[:, :FF], joined[:, FF:]
    return gate, up, jax.nn.sigmoid(gate)


def swiglu(joined):
    gate, up, sig = silu_parts(joined)
    return gate * sig * up


def swiglu_back(joined, grad):
    gate, up, sig = silu_parts(joined)
    return jnp.concatenate([grad * up * sig * (1.0 + gate * (1.0 - sig)), grad * gate * sig], axis=1)


def layer_forward(state, weights, geometry, route, chosen):
    w_wide, w_gu, w_small, w_sd, w_egu, w_ed = weights
    cosine, sine, qidx, qlab, klab = geometry
    gains = w_small[:, :2].astype(jnp.float32)
    router = w_small[:, 2 : 2 + EXPERTS]
    scale_attn, unit_attn = rms_parts(state)
    normed_attn = low(unit_attn * gains[:, 0])
    joined = dot(normed_attn, w_wide[:, : 3 * D])
    queries = low(rotate(joined[:, :D], cosine, sine))
    keys = low(rotate(joined[:, D : 2 * D], cosine, sine))
    values = low(joined[:, 2 * D :])
    kv = jnp.stack([jnp.concatenate([k, v], axis=1) for k, v in zip(heads_out(keys, 4), heads_out(values, 4))])
    kv_all, q_all = exchange("exchange_qkv", 1, kv, jnp.stack(heads_out(queries, 4)))
    kv_all, q_all = kv_all.reshape(SEQ, 384), q_all.reshape(512, 192)
    mixed_heads, lse = attend(q_all, kv_all, qidx, qlab, klab)
    (back,) = exchange("exchange_heads", 2, None, mixed_heads.reshape(4, ROWS, 192))
    attended = jnp.concatenate([back[g] for g in range(4)], axis=1)
    residual = state + dot(attended, w_wide[:, 3 * D :])
    scale_ffn, unit_ffn = rms_parts(residual)
    normed_ffn = low(unit_ffn * gains[:, 1])
    logits = dot(normed_ffn, router)
    labels = jnp.arange(EXPERTS, dtype=jnp.int32)
    picks = [(route[:, c : c + 1] == labels[None, :]) for c in range(TOP)]
    pair_logits = jnp.concatenate([jnp.sum(jnp.where(p, logits, 0.0), axis=1, keepdims=True) for p in picks], axis=1)
    gates = jax.nn.softmax(pair_logits, axis=-1)
    taken = low(chosen[0] | chosen[1])
    sent = low(t_dot(taken, normed_ffn))
    (received,) = exchange("exchange_slots", 4, sent.reshape(EXPERTS, PAD_CAP, D))
    shared_joined = dot(normed_ffn, w_gu)
    shared_hidden = low(swiglu(shared_joined))
    shared_out = dot(shared_hidden, w_sd)
    received = received.reshape(SLOTS, D)
    expert_joined = dot(received, w_egu)
    expert_hidden = low(swiglu(expert_joined))
    result = low(dot(expert_hidden, w_ed))
    (returned,) = exchange("exchange_slots", 4, result.reshape(EXPERTS, PAD_CAP, D))
    returned = returned.reshape(SLOTS, D)
    weights_of = jnp.where(chosen[0], gates[:, 0:1], 0.0) + jnp.where(chosen[1], gates[:, 1:2], 0.0)
    mixed = jnp.dot(weights_of, returned.astype(jnp.float32), precision=HIGH)
    output = residual + shared_out + mixed
    kept = dict(
        scale_attn=scale_attn, unit_attn=unit_attn, normed_attn=normed_attn, q_all=q_all, kv_all=kv_all, lse=lse,
        attended=attended, scale_ffn=scale_ffn, unit_ffn=unit_ffn, normed_ffn=normed_ffn, gates=gates, taken=taken,
        shared_joined=shared_joined, shared_hidden=shared_hidden, received=received, expert_joined=expert_joined,
        expert_hidden=expert_hidden, returned=returned, picks=picks, weights_of=weights_of,
    )
    return output, kept


def layer_backward(grad_output, kept, weights, geometry, chosen):
    w_wide, w_gu, w_small, w_sd, w_egu, w_ed = weights
    cosine, sine, qidx, qlab, klab = geometry
    gains = w_small[:, :2].astype(jnp.float32)
    router = w_small[:, 2 : 2 + EXPERTS]
    grad_rounded = low(grad_output)
    slot_grads = low(t_dot(kept["weights_of"], grad_output, HIGH))
    (grad_result,) = exchange("exchange_slots", 4, slot_grads.reshape(EXPERTS, PAD_CAP, D))
    grad_result = grad_result.reshape(SLOTS, D)
    grad_expert_joined = low(swiglu_back(kept["expert_joined"], dot_t(grad_result, w_ed)))
    grad_sent = low(dot_t(grad_expert_joined, w_egu))
    (grad_slots,) = exchange("exchange_slots", 4, grad_sent.reshape(EXPERTS, PAD_CAP, D))
    grad_shared_joined = low(swiglu_back(kept["shared_joined"], dot_t(grad_rounded, w_sd)))
    grad_normed = dot_t(grad_shared_joined, w_gu)
    grad_normed = grad_normed + dot(kept["taken"], grad_slots.reshape(SLOTS, D))
    products = dot_t(grad_rounded, kept["returned"])
    grad_gates = jnp.concatenate(
        [jnp.sum(jnp.where(c, products, 0.0), axis=1, keepdims=True) for c in chosen], axis=1
    )
    gates = kept["gates"]
    grad_chosen = gates * (grad_gates - jnp.sum(gates * grad_gates, axis=1, keepdims=True))
    grad_logits = sum(jnp.where(p, grad_chosen[:, c : c + 1], 0.0) for c, p in enumerate(kept["picks"]))
    grad_router = t_dot(kept["normed_ffn"].astype(jnp.float32), grad_logits, HIGH)
    grad_normed = grad_normed + lax.dot_general(
        grad_logits, router.astype(jnp.float32), (((1,), (1,)), ((), ())), precision=HIGH
    )
    grad_residual, grad_gain_ffn = rms_back(grad_normed, gains[:, 1], kept["scale_ffn"], kept["unit_ffn"])
    grad_residual = grad_output + grad_residual
    grad_projected = low(grad_residual)
    grad_attended = low(dot_t(grad_projected, w_wide[:, 3 * D :]))
    (grad_heads,) = exchange("exchange_heads", 2, None, jnp.stack(heads_out(grad_attended, 4)))
    dq, dkv = attend_back(
        kept["q_all"], kept["kv_all"], grad_heads.reshape(512, 192), kept["lse"], qidx, qlab, klab
    )
    dkv_all, dq_all = exchange("exchange_grads", 3, dkv.reshape(8, ROWS, 384), dq.reshape(4, ROWS, 192))
    dkv_all = dkv_all.astype(jnp.float32)
    dkv_all = dkv_all[:4] + dkv_all[4:]
    grad_queries = jnp.concatenate([dq_all[g] for g in range(4)], axis=1).astype(jnp.float32)
    grad_keys = jnp.concatenate([dkv_all[g, :, :192] for g in range(4)], axis=1)
    grad_values = jnp.concatenate([dkv_all[g, :, 192:] for g in range(4)], axis=1)
    grad_joined = low(
        jnp.concatenate([rotate(grad_queries, cosine, -sine), rotate(grad_keys, cosine, -sine), grad_values], axis=1)
    )
    grad_normed_attn = dot_t(grad_joined, w_wide[:, : 3 * D])
    grad_state, grad_gain_attn = rms_back(grad_normed_attn, gains[:, 0], kept["scale_attn"], kept["unit_attn"])
    grad_input = grad_residual + grad_state
    operands = [
        kept["normed_attn"].T, kept["attended"].T, kept["normed_ffn"].T, kept["shared_hidden"].T,
        kept["received"].T, kept["expert_hidden"].T,
        grad_joined, grad_projected, grad_shared_joined, grad_rounded, grad_expert_joined, grad_result,
    ]
    small = jnp.concatenate(
        [grad_gain_attn[:, None], grad_gain_ffn[:, None], grad_router, jnp.zeros((D, SMALL - 2 - EXPERTS), jnp.float32)],
        axis=1,
    )
    return grad_input, operands, small


def swap_cores(value):
    return lax.ppermute(value, "section", [(0, 1), (1, 0)])


def on_device(
    x_in, cotangent, group_ids, routes, priority,
    gains, w_qkv, w_out, router, shared_gate_up, shared_down, expert_gate_up, expert_down,
):
    section = lax.axis_index("section")
    ctx = lax.axis_index("ctx")
    first = section == 0

    pack = jnp.concatenate(
        [w_qkv[0], w_out[0], shared_gate_up[0], gains[0], router[0], jnp.zeros((OWN, SMALL - 2 - EXPERTS), jnp.bfloat16)],
        axis=1,
    )
    gathered = gather_weights(
        jnp.pad(pack, ((0, 16 - OWN), (0, 0))), shared_down[0], expert_gate_up[0, 0], expert_down[0, 0]
    )
    weights = [tuple(w[layer] for w in gathered) for layer in range(2)]

    def mine(value):
        return jnp.where(first, value[0], value[1])

    def other(value):
        return jnp.where(first, value[1], value[0])

    picked = jnp.stack([routes[0, :, 0], priority[0, :, 0]], axis=1)
    passed = swap_cores(other(picked))
    own = mine(picked)
    plans = [jnp.where(first, own, passed), jnp.where(first, passed, own)]
    chosen = [slot_tables(plan[0], plan[1]) for plan in plans]

    group_row = mine(group_ids[:, 0])
    positions = token_positions(group_row)
    cosine, sine = rotation_tables(lax.dynamic_slice_in_dim(positions, ctx * ROWS, ROWS))
    half_start = ctx // 4 * 512
    qlab = lax.dynamic_slice_in_dim(group_row, half_start, 512)[:, None]
    qidx = (half_start + jnp.arange(512, dtype=jnp.int32))[:, None]
    geometry = (cosine, sine, qidx, qlab, group_row[None, :])

    state = mine(x_in[:, 0]).astype(jnp.float32)
    output, kept_lower = layer_forward(state, weights[0], geometry, plans[0][0], chosen[0])
    hidden = low(output)
    output, kept_upper = layer_forward(hidden.astype(jnp.float32), weights[1], geometry, plans[1][0], chosen[1])
    final = low(output)

    grad_final = mine(cotangent[:, 0]).astype(jnp.float32)
    hidden_grad, operands_upper, small_upper = layer_backward(grad_final, kept_upper, weights[1], geometry, chosen[1])
    input_grad, operands_lower, small_lower = layer_backward(
        low(hidden_grad).astype(jnp.float32), kept_lower, weights[0], geometry, chosen[0]
    )
    small = jnp.where(first, small_lower, small_upper) + swap_cores(jnp.where(first, small_upper, small_lower))
    pack_grad, sd_grad, egu_grad, ed_grad = weight_grads(operands_lower, operands_upper, small)

    def per_layer(lower, upper):
        kept_here = jnp.where(first, lower, upper)
        arrived = swap_cores(jnp.where(first, upper, lower))
        both = jnp.stack([jnp.where(first, kept_here, arrived), jnp.where(first, arrived, kept_here)])
        return both.reshape(1, 2, 1, ROWS, D)

    pack_grad = pack_grad[None, :OWN]
    tail = WIDE + 2 * FF
    return (
        per_layer(hidden, final),
        per_layer(input_grad, hidden_grad),
        pack_grad[:, :, tail : tail + 2],
        pack_grad[:, :, : 3 * D],
        pack_grad[:, :, 3 * D : WIDE],
        pack_grad[:, :, tail + 2 : tail + 2 + EXPERTS],
        pack_grad[:, :, WIDE:tail],
        sd_grad[None],
        egu_grad[None, None],
        ed_grad[None, None],
    )


def solution(mesh):
    dense = P("section", ("ctx", "fsdp"), None)
    expert = P("section", "ctx", "fsdp", None)
    tokens = P("section", None, "fsdp", "ctx", None)
    rows = P(None, "fsdp", "ctx", None)
    return jax.shard_map(
        on_device,
        mesh=mesh,
        in_specs=(rows, rows, P(None, "fsdp", None), tokens, tokens) + (dense,) * 6 + (expert,) * 2,
        out_specs=(tokens, tokens) + (dense,) * 6 + (expert,) * 2,
        check_vma=False,
    )
```

```python
import functools
import math

import jax
import jax.numpy as jnp
from jax import lax
from jax.experimental import pallas as pl
from jax.experimental.pallas import tpu as pltpu
from jax.sharding import PartitionSpec as P

MESH = pl.DeviceIdType.MESH
ANY = pl.BlockSpec(memory_space=pl.ANY)
VMEM = pl.BlockSpec(memory_space=pltpu.VMEM)
DMA = pltpu.SemaphoreType.DMA

D = 768
FF = 2048
WIDE = 3072
SMALL = 128
PACK = WIDE + 2 * FF + SMALL
OWN = 12
HEADS = 12
HEAD_DIM = 64
TOP = 2
CONT = 8
EXPERTS = 8
SEQ = 1024
ROWS = 128
CAP = 40
PAD_CAP = 48
SLOTS = EXPERTS * PAD_CAP
SCALE = 1.0 / math.sqrt(HEAD_DIM)
EPS = 1e-06
NEG = -1e30


def place_ids():
    section = lax.axis_index("section")
    ctx = lax.axis_index("ctx")
    fsdp = lax.axis_index("fsdp")
    return section, ctx // 4, lax.rem(ctx, 4), fsdp // 2, lax.rem(fsdp, 2)


def ctx_of(half, ring):
    return lax.rem(half + 2, 2) * 4 + lax.rem(ring + 4, 4)


def fsdp_of(ring, half):
    return lax.rem(ring + 4, 4) * 2 + lax.rem(half + 2, 2)


def neighbours():
    section, a, z, y, h = place_ids()
    ctx, fsdp = ctx_of(a, z), fsdp_of(y, h)
    return dict(
        core=(1 - section, ctx, fsdp),
        zp=(section, ctx_of(a, z + 1), fsdp),
        zm=(section, ctx_of(a, z - 1), fsdp),
        zx=(section, ctx_of(a + 1, z), fsdp),
        yp=(section, ctx, fsdp_of(y + 1, h)),
        ym=(section, ctx, fsdp_of(y - 1, h)),
        yx=(section, ctx, fsdp_of(y, h + 1)),
    )


def greet(devices):
    barrier = pltpu.get_barrier_semaphore()
    for device in devices:
        pl.semaphore_signal(barrier, inc=1, device_id=device, device_id_type=MESH)
    pl.semaphore_wait(barrier, len(devices))


def rows_at(ref, block, rows, part=None):
    if part is None:
        return ref.at[pl.ds(pl.multiple_of(block * rows, 16), rows)]
    half = rows // 2
    return ref.at[pl.ds(pl.multiple_of(block * rows + part * half, 16), half)]


class Hop:
    def __init__(self, sources, targets, device, send, recv):
        self.copies = [
            pltpu.make_async_remote_copy(s, t, send.at[i], recv.at[i], device_id=device, device_id_type=MESH)
            for i, (s, t) in enumerate(zip(sources, targets))
        ]

    def start(self):
        for copy in self.copies:
            copy.start()
        return self

    def wait_recv(self):
        for copy in self.copies:
            copy.wait_recv()

    def wait_send(self):
        for copy in self.copies:
            copy.wait_send()


def gather_kernel(
    pack, sd, egu, ed, sel,
    w_wide, w_gu, w_small, w_sd, w_egu, w_ed,
    packs, own_wide, own_gu, own_small, own_sd,
    s_send, s_recv, d_send, d_recv, e_send, e_recv, c_send, c_recv, l_sem,
):
    section, a, z, y, h = place_ids()
    ctx, fsdp = ctx_of(a, z), fsdp_of(y, h)
    near = neighbours()
    others = [(dy, dh) for dy in (1, 3, 2, 0) for dh in (0, 1) if (dy, dh) != (0, 0)]
    f_peers = [(section, ctx, fsdp_of(y + dy, h + dh)) for dy, dh in others]
    greet([near["core"], near["zp"], near["zm"], near["zx"]] + f_peers)

    first = []
    for k, device in enumerate(f_peers):
        hop = Hop(
            [pack, sd], [rows_at(packs, fsdp, 16), rows_at(own_sd, fsdp, 32)], device, s_send.at[k], s_recv.at[k]
        )
        first.append(hop.start())
    locals_ = [
        pltpu.make_async_copy(pack, rows_at(packs, fsdp, 16), l_sem.at[0]),
        pltpu.make_async_copy(sd, rows_at(own_sd, fsdp, 32), l_sem.at[1]),
    ]
    for copy in locals_:
        copy.start()

    me_w = [w.at[section] for w in (w_wide, w_gu, w_small, w_sd)]
    me_e = [w.at[section] for w in (w_egu, w_ed)]
    d_rows = (96, 96, 96, 256)
    e_rows = (96, 256)

    def dense(block, part=None):
        return [rows_at(w, block, r, part) for w, r in zip(me_w, d_rows)]

    def expert(block, part=None):
        return [rows_at(w, block, r, part) for w, r in zip(me_e, e_rows)]

    cores = []

    def to_core(refs, block_refs, index):
        cores.append(Hop(refs, block_refs, near["core"], c_send.at[index], c_recv.at[index]).start())

    for hop in first:
        hop.wait_recv()
    for copy in locals_:
        copy.wait()

    e_own = [egu, ed]
    e_hops = {}

    def e_hop(index, refs, block_refs, device):
        e_hops[index] = Hop(refs, block_refs, near[device], e_send.at[index], e_recv.at[index]).start()

    for index, device in ((0, "yp"), (1, "ym"), (2, "yx")):
        e_hop(index, e_own, expert(fsdp), device)

    for target, start, width in ((own_wide, 0, WIDE), (own_gu, WIDE, 2 * FF), (own_small, WIDE + 2 * FF, SMALL)):
        step = min(width, 512)

        @pl.loop(0, width // step)
        def _(j, target=target, start=start, step=step):
            off = pl.multiple_of(j * step, 128)
            block = packs[:, pl.ds(start + off, step)]
            target[:, pl.ds(off, step)] = jnp.dot(sel[...], block, preferred_element_type=jnp.float32).astype(jnp.bfloat16)

    d_own = [own_wide, own_gu, own_small, own_sd]
    d_hops = {}

    def d_hop(index, refs, block_refs, device):
        d_hops[index] = Hop(refs, block_refs, near[device], d_send.at[index], d_recv.at[index]).start()

    for index, device in ((0, "zp"), (1, "zm"), (2, "zx")):
        d_hop(index, d_own, dense(ctx), device)
    own_copies = [
        pltpu.make_async_copy(s, t, l_sem.at[2 + i])
        for i, (s, t) in enumerate(zip(d_own + e_own, dense(ctx) + expert(fsdp)))
    ]
    for copy in own_copies:
        copy.start()
    to_core(d_own + e_own, dense(ctx) + expert(fsdp), 0)

    def e_block(dy, dh):
        return fsdp_of(y + dy, h + dh)

    def d_block(dz, da):
        return ctx_of(a + da, z + dz)

    def e_pass(index, block, part, device):
        e_hop(index, expert(block, part), expert(block, part), device)

    def d_pass(index, block, part, device):
        d_hop(index, dense(block, part), dense(block, part), device)

    e_hops[0].wait_recv()
    e_pass(3, e_block(-1, 0), 0, "yp")
    e_hops[1].wait_recv()
    e_pass(4, e_block(1, 0), 1, "ym")
    d_hops[0].wait_recv()
    d_pass(3, d_block(-1, 0), 0, "zp")
    d_hops[1].wait_recv()
    d_pass(4, d_block(1, 0), 1, "zm")
    e_hops[2].wait_recv()
    e_pass(5, e_block(0, 1), None, "yp")
    e_pass(6, e_block(0, 1), None, "ym")
    d_hops[2].wait_recv()
    d_pass(5, d_block(0, 1), None, "zp")
    d_pass(6, d_block(0, 1), None, "zm")
    to_core(dense(d_block(-1, 0)) + expert(e_block(-1, 0)), dense(d_block(-1, 0)) + expert(e_block(-1, 0)), 1)
    to_core(dense(d_block(1, 0)) + expert(e_block(1, 0)), dense(d_block(1, 0)) + expert(e_block(1, 0)), 2)
    to_core(dense(d_block(0, 1)) + expert(e_block(0, 1)), dense(d_block(0, 1)) + expert(e_block(0, 1)), 3)
    d_hops[3].wait_recv()
    d_hops[4].wait_recv()
    d_pass(7, d_block(2, 0), None, "zx")
    e_hops[3].wait_recv()
    e_hops[4].wait_recv()
    to_core(dense(d_block(2, 0)) + expert(e_block(2, 0)), dense(d_block(2, 0)) + expert(e_block(2, 0)), 4)
    e_hops[5].wait_recv()
    e_pass(7, e_block(-1, 1), 0, "yp")
    e_hops[6].wait_recv()
    e_pass(8, e_block(1, 1), 1, "ym")
    d_hops[5].wait_recv()
    to_core(dense(d_block(-1, 1)) + expert(e_block(-1, 1)), dense(d_block(-1, 1)) + expert(e_block(-1, 1)), 5)
    d_hops[6].wait_recv()
    to_core(dense(d_block(1, 1)) + expert(e_block(1, 1)), dense(d_block(1, 1)) + expert(e_block(1, 1)), 6)
    d_hops[7].wait_recv()
    e_hops[7].wait_recv()
    e_hops[8].wait_recv()
    to_core(dense(d_block(2, 1)) + expert(e_block(2, 1)), dense(d_block(2, 1)) + expert(e_block(2, 1)), 7)
    for copy in own_copies:
        copy.wait()
    for hop in first + list(d_hops.values()) + list(e_hops.values()):
        hop.wait_send()
    for hop in cores:
        hop.wait_recv()
        hop.wait_send()


def gather_weights(pack, sd, egu, ed):
    rows = jnp.arange(96)
    cols = jnp.arange(128)
    sel = ((rows[:, None] // OWN == cols[None, :] // 16) & (rows[:, None] % OWN == cols[None, :] % 16)).astype(jnp.bfloat16)
    bf = jnp.bfloat16
    shapes = [(2, D, WIDE), (2, D, 2 * FF), (2, D, SMALL), (2, FF, D), (2, D, 2 * FF), (2, FF, D)]
    return pl.pallas_call(
        gather_kernel,
        out_shape=[jax.ShapeDtypeStruct(s, bf) for s in shapes],
        in_specs=[ANY, ANY, ANY, ANY, VMEM],
        out_specs=[ANY] * 6,
        scratch_shapes=[
            pltpu.VMEM((128, PACK), bf),
            pltpu.VMEM((96, WIDE), bf),
            pltpu.VMEM((96, 2 * FF), bf),
            pltpu.VMEM((96, SMALL), bf),
            pltpu.VMEM((256, D), bf),
            DMA((7, 2)), DMA((7, 2)),
            DMA((8, 4)), DMA((8, 4)),
            DMA((9, 2)), DMA((9, 2)),
            DMA((8, 6)), DMA((8, 6)),
            DMA((8,)),
        ],
        compiler_params=pltpu.CompilerParams(collective_id=0, has_side_effects=True, vmem_limit_bytes=48 << 20),
        name="gather_weights",
    )(pack, sd, egu, ed, sel)


LEFT = (("na", D, 128), ("at", D, 128), ("nf", D, 128), ("sh", FF, 128), ("rc", D, SLOTS), ("hd", FF, SLOTS))
RIGHT = (("qkv", 128, 3 * D), ("pr", 128, D), ("gu", 128, 2 * FF), ("sd", 128, D), ("j", SLOTS, 2 * FF), ("er", SLOTS, D))
N_OPS = len(LEFT) + len(RIGHT)
DENSE = (("wide", "na", "qkv", 96, 0, 3 * D), ("wide", "at", "pr", 96, 3 * D, D), ("gu", "nf", "gu", 96, 0, 2 * FF), ("sd", "sh", "sd", 256, 0, D))
EXPERT = (("egu", "rc", "j", 96, 0, 2 * FF), ("ed", "hd", "er", 256, 0, D))


def grads_kernel(*refs):
    lower, upper = refs[:N_OPS], refs[N_OPS : 2 * N_OPS]
    small, sel_t = refs[2 * N_OPS : 2 * N_OPS + 2]
    out_pack, out_sd, out_egu, out_ed = refs[2 * N_OPS + 2 : 2 * N_OPS + 6]
    rest = refs[2 * N_OPS + 6 :]
    held = rest[:N_OPS]
    (b_wide, b_gu, b_small, b_sd, c_gu, c_sd, packs, in_pack, in_sd,
     o_send, o_recv, o_local, d_send, d_recv, e_send, e_recv, s_send, s_recv) = rest[N_OPS:]
    names = [n for n, _, _ in LEFT] + [n for n, _, _ in RIGHT]
    ops = dict(zip(names, held))
    section, a, z, y, h = place_ids()
    ctx, fsdp = ctx_of(a, z), fsdp_of(y, h)
    near = neighbours()
    others = [(dy, dh) for dy in (1, 3, 2, 0) for dh in (0, 1) if (dy, dh) != (0, 0)]
    f_peers = [(section, ctx, fsdp_of(y + dy, h + dh)) for dy, dh in others]
    greet([near["core"], near["zp"], near["zm"], near["zx"]] + f_peers)

    def slot_of(i, which):
        n, r, c = (LEFT + RIGHT)[i]
        if i < len(LEFT):
            return held[i].at[:, pl.ds(which * c, c)]
        return held[i].at[pl.ds(which * r, r)]

    def bring(mine, theirs):
        for i in range(N_OPS):
            pltpu.make_async_remote_copy(
                theirs[i], slot_of(i, 1), o_send.at[i], o_recv.at[i], device_id=near["core"], device_id_type=MESH
            ).start()
            pltpu.make_async_copy(mine[i], slot_of(i, 0), o_local.at[i]).start()

    @pl.when(section == 0)
    def _():
        bring(lower, upper)

    @pl.when(section == 1)
    def _():
        bring(upper, lower)

    def ready(wanted):
        for i, n in enumerate(names):
            if n in wanted:
                pltpu.make_async_copy(lower[i], slot_of(i, 0), o_local.at[i]).wait()
                pltpu.make_async_remote_copy(
                    lower[i], slot_of(i, 1), o_send.at[i], o_recv.at[i], device_id=near["core"], device_id_type=MESH
                ).wait_recv()

    kinds = dict(wide=b_wide, gu=b_gu, small=b_small, sd=b_sd, egu=c_gu, ed=c_sd)

    def combine(pieces, block, slot, adds=(), part=None, target=None):
        for kind, left, right, rows, first, width in pieces:
            n = rows if part is None else rows // 2
            off = 0 if part is None else part * n
            lhs_rows = pl.ds(pl.multiple_of(block * rows + off, 16), n)

            @pl.loop(0, width // 256)
            def _(j, kind=kind, left=left, right=right, first=first, n=n, off=off, lhs_rows=lhs_rows):
                at = pl.ds(pl.multiple_of(j * 256, 256), 256)
                to = pl.ds(pl.multiple_of(first + j * 256, 256), 256)
                total = jnp.dot(ops[left][lhs_rows, :], ops[right][:, at], preferred_element_type=jnp.float32)
                for other in adds:
                    total += kinds[kind][other, off : off + n, to].astype(jnp.float32)
                if target is None:
                    kinds[kind][slot, off : off + n, to] = total.astype(jnp.bfloat16)
                else:
                    target[kind][off : off + n, to] = total

        if pieces is DENSE:
            n = 96 if part is None else 48
            off = 0 if part is None else part * n
            total = small[pl.ds(pl.multiple_of(block * 96 + off, 16), n), :]
            for other in adds:
                total += b_small[other, off : off + n, :].astype(jnp.float32)
            b_small[slot, off : off + n, :] = total.astype(jnp.bfloat16)

    def views(pieces, slot, part):
        if pieces is DENSE:
            bufs = ((b_wide, 96), (b_gu, 96), (b_small, 96), (b_sd, 256))
        else:
            bufs = ((c_gu, 96), (c_sd, 256))
        return [rows_at(b.at[slot], 0, r, part) for b, r in bufs]

    hops = {}

    def send(pieces, index, slot, to_slot, device, part=None):
        sems = (d_send, d_recv) if pieces is DENSE else (e_send, e_recv)
        tag = "d" if pieces is DENSE else "e"
        hops[tag, index] = Hop(
            views(pieces, slot, part), views(pieces, to_slot, part), near[device], sems[0].at[index], sems[1].at[index]
        ).start()

    def d_block(dz, da):
        return ctx_of(a + da, z + dz)

    def e_block(dy, dh):
        return fsdp_of(y + dy, h + dh)

    ready(("na", "qkv", "at", "pr", "nf", "gu", "sh", "sd"))
    combine(DENSE, d_block(2, 1), 0)
    send(DENSE, 0, 0, 1, "zx")
    combine(DENSE, d_block(-1, 1), 2)
    send(DENSE, 1, 2, 5, "zm")
    combine(DENSE, d_block(1, 1), 3)
    send(DENSE, 2, 3, 6, "zp")
    ready(("rc", "j", "hd", "er"))
    combine(EXPERT, e_block(2, 1), 0)
    send(EXPERT, 0, 0, 4, "ym", 0)
    send(EXPERT, 1, 0, 4, "yp", 1)
    combine(EXPERT, e_block(2, 0), 1)
    send(EXPERT, 2, 1, 5, "ym", 0)
    send(EXPERT, 3, 1, 5, "yp", 1)
    hops["d", 0].wait_recv()
    combine(DENSE, d_block(2, 0), 1, (1,))
    send(DENSE, 3, 1, 4, "zm", 0)
    send(DENSE, 4, 1, 4, "zp", 1)
    combine(EXPERT, e_block(-1, 1), 2, (), 1)
    combine(EXPERT, e_block(1, 1), 3, (), 0)
    hops["e", 0].wait_recv()
    combine_half(combine, EXPERT, e_block(-1, 1), 2, 4, 0)
    send(EXPERT, 4, 2, 6, "ym")
    hops["e", 1].wait_recv()
    combine_half(combine, EXPERT, e_block(1, 1), 3, 4, 1)
    send(EXPERT, 5, 3, 7, "yp")
    hops["d", 0].wait_send()
    combine(DENSE, d_block(-1, 0), 0, (), 1)
    hops["d", 3].wait_recv()
    combine_half(combine, DENSE, d_block(-1, 0), 0, 4, 0)
    send(DENSE, 5, 0, 7, "zm")
    hops["d", 3].wait_send()
    hops["d", 4].wait_send()
    combine(DENSE, d_block(1, 0), 1, (), 0)
    hops["d", 4].wait_recv()
    combine_half(combine, DENSE, d_block(1, 0), 1, 4, 1)
    send(DENSE, 6, 1, 8, "zp")
    hops["e", 0].wait_send()
    hops["e", 1].wait_send()
    combine(EXPERT, e_block(-1, 0), 0, (), 1)
    hops["e", 2].wait_recv()
    combine_half(combine, EXPERT, e_block(-1, 0), 0, 5, 0)
    send(EXPERT, 6, 0, 8, "ym")
    hops["e", 2].wait_send()
    hops["e", 3].wait_send()
    combine(EXPERT, e_block(1, 0), 1, (), 0)
    hops["e", 3].wait_recv()
    combine_half(combine, EXPERT, e_block(1, 0), 1, 5, 1)
    send(EXPERT, 7, 1, 9, "yp")
    hops["d", 1].wait_recv()
    hops["d", 2].wait_recv()
    combine(DENSE, d_block(0, 1), 5, (5, 6))
    send(DENSE, 7, 5, 9, "zx")
    hops["e", 4].wait_recv()
    hops["e", 5].wait_recv()
    combine(EXPERT, e_block(0, 1), 6, (6, 7))
    send(EXPERT, 8, 6, 10, "yx")
    for index in (5, 6, 7):
        hops["d", index].wait_recv()
    combine(DENSE, ctx, 7, (7, 8, 9))

    for kind, start, width in (("wide", 0, WIDE), ("gu", WIDE, 2 * FF), ("small", WIDE + 2 * FF, SMALL)):
        step = min(width, 512)

        @pl.loop(0, width // step)
        def _(j, kind=kind, start=start, step=step):
            off = pl.multiple_of(j * step, 128)
            block = kinds[kind][7, :, pl.ds(off, step)]
            packs[:, pl.ds(start + off, step)] = jnp.dot(sel_t[...], block, preferred_element_type=jnp.float32).astype(jnp.bfloat16)

    last = []
    for k, ((dy, dh), device) in enumerate(zip(others, f_peers)):
        block = e_block(dy, dh)
        last.append(
            Hop(
                [rows_at(packs, block, 16), rows_at(b_sd.at[7], block, 32)],
                [in_pack.at[k], in_sd.at[k]],
                device, s_send.at[k], s_recv.at[k],
            ).start()
        )
    for index in (6, 7, 8):
        hops["e", index].wait_recv()
    combine(EXPERT, fsdp, 0, (8, 9, 10), None, dict(egu=out_egu, ed=out_ed))
    for hop in last:
        hop.wait_recv()

    @pl.loop(0, PACK // 128)
    def _(j):
        at = pl.ds(pl.multiple_of(j * 128, 128), 128)
        total = packs[pl.ds(pl.multiple_of(fsdp * 16, 16), 16), at].astype(jnp.float32)
        for k in range(7):
            total += in_pack[k, :, at].astype(jnp.float32)
        out_pack[:, at] = total

    total = b_sd[7, pl.ds(pl.multiple_of(fsdp * 32, 16), 32), :].astype(jnp.float32)
    for k in range(7):
        total += in_sd[k].astype(jnp.float32)
    out_sd[...] = total
    for hop in list(hops.values())[:]:
        pass
    for key in (("d", 1), ("d", 2), ("d", 5), ("d", 6), ("d", 7), ("e", 4), ("e", 5), ("e", 6), ("e", 7), ("e", 8)):
        hops[key].wait_send()
    for hop in last:
        hop.wait_send()
    for i in range(N_OPS):
        pltpu.make_async_remote_copy(
            lower[i], slot_of(i, 1), o_send.at[i], o_recv.at[i], device_id=near["core"], device_id_type=MESH
        ).wait_send()


def combine_half(combine, pieces, block, slot, half_slot, part):
    combine(pieces, block, slot, (half_slot,), part)


def weight_grads(lower, upper, small):
    rows = jnp.arange(128)
    cols = jnp.arange(96)
    sel_t = ((cols[None, :] // OWN == rows[:, None] // 16) & (cols[None, :] % OWN == rows[:, None] % 16)).astype(jnp.bfloat16)
    bf, f32 = jnp.bfloat16, jnp.float32
    held = [pltpu.VMEM((r, 2 * c), bf) for _, r, c in LEFT] + [pltpu.VMEM((2 * r, c), bf) for _, r, c in RIGHT]
    return pl.pallas_call(
        grads_kernel,
        out_shape=[
            jax.ShapeDtypeStruct((16, PACK), f32),
            jax.ShapeDtypeStruct((32, D), f32),
            jax.ShapeDtypeStruct((96, 2 * FF), f32),
            jax.ShapeDtypeStruct((256, D), f32),
        ],
        in_specs=[ANY] * (2 * N_OPS) + [VMEM, VMEM],
        out_specs=[VMEM] * 4,
        scratch_shapes=held + [
            pltpu.VMEM((10, 96, WIDE), bf),
            pltpu.VMEM((10, 96, 2 * FF), bf),
            pltpu.VMEM((10, 96, SMALL), bf),
            pltpu.VMEM((10, 256, D), bf),
            pltpu.VMEM((11, 96, 2 * FF), bf),
            pltpu.VMEM((11, 256, D), bf),
            pltpu.VMEM((128, PACK), bf),
            pltpu.VMEM((7, 16, PACK), bf),
            pltpu.VMEM((7, 32, D), bf),
            DMA((N_OPS,)), DMA((N_OPS,)), DMA((N_OPS,)),
            DMA((8, 4)), DMA((8, 4)),
            DMA((9, 2)), DMA((9, 2)),
            DMA((7, 2)), DMA((7, 2)),
        ],
        compiler_params=pltpu.CompilerParams(collective_id=5, has_side_effects=True, vmem_limit_bytes=62 << 20),
        name="weight_grads",
    )(*lower, *upper, small, sel_t)


def split(values):
    high = low(values)
    return high, low(values - high.astype(jnp.float32))


def rms_parts(values):
    scale = lax.rsqrt(jnp.mean(values * values, axis=-1, keepdims=True) + EPS)
    return scale, values * scale


def rms_back(grad, gain, scale, unit):
    inner = grad * gain
    grad_values = scale * (inner - unit * jnp.mean(inner * unit, axis=-1, keepdims=True))
    return grad_values, jnp.sum(grad * unit, axis=0, keepdims=True)


def dot(left, right):
    return jnp.dot(left, right, preferred_element_type=jnp.float32)


def dot_t(left, right):
    return lax.dot_general(left, right, (((1,), (1,)), ((), ())), preferred_element_type=jnp.float32)


def t_dot(left, right):
    return lax.dot_general(left, right, (((0,), (0,)), ((), ())), preferred_element_type=jnp.float32)


def low(values):
    return values.astype(jnp.bfloat16)


def rotate(values, cosine, sine):
    half = HEAD_DIM // 2
    lower = lax.broadcasted_iota(jnp.int32, (values.shape[0], 128), 1) % HEAD_DIM < half
    parts = []
    for start in range(0, values.shape[1], 128):
        span = slice(start, start + 128)
        part = values[:, span]
        other = jnp.where(lower, pltpu.roll(part, 128 - half, 1), pltpu.roll(part, half, 1))
        parts.append(part * cosine[:, span] + other * sine[:, span])
    return jnp.concatenate(parts, axis=1)


def visible_keys(qidx, qlab, klab):
    kidx = lax.broadcasted_iota(jnp.int32, (qidx.shape[0], klab.shape[1]), 1)
    return (kidx <= qidx) & ((klab == 0) | (klab == qlab))


def pair_gates(logits, route):
    lane = lax.broadcasted_iota(jnp.int32, logits.shape, 1)
    picks = [lane == route[:, c : c + 1] + 2 for c in range(TOP)]
    first, second = [jnp.sum(jnp.where(p, logits, 0.0), axis=1, keepdims=True) for p in picks]
    top = jnp.maximum(first, second)
    first, second = jnp.exp(first - top), jnp.exp(second - top)
    total = first + second
    return picks, [first / total, second / total]


class Exchange:
    def __init__(self, source, target, send, recv, everyone, block_of=None):
        section, a, z, y, h = place_ids()
        fsdp = fsdp_of(y, h)
        offsets = [(1, 0), (1, 1), (1, 3), (1, 2)] if everyone else []
        self.copies = []
        for k, (da, dz) in enumerate(offsets + [(0, 1), (0, 3), (0, 2)]):
            c, zz = ctx_of(a + da, z + dz), lax.rem(z + dz, 4)
            block = zz if block_of == "ring" or not everyone else c
            to = ctx_of(a, z) if everyone else z
            self.copies.append(
                pltpu.make_async_remote_copy(
                    source.at[block], target.at[to], send.at[k], recv.at[k], device_id=(section, c, fsdp), device_id_type=MESH
                )
            )

    def start(self):
        for copy in self.copies:
            copy.start()

    def wait_recv(self):
        for copy in self.copies:
            copy.wait_recv()

    def wait_send(self):
        for copy in self.copies:
            copy.wait_send()


def ctx_peers():
    section, a, z, y, h = place_ids()
    fsdp = fsdp_of(y, h)
    return [(section, ctx_of(a + da, z + dz), fsdp) for da in range(2) for dz in range(4) if (da, dz) != (0, 0)]


def forward_kernel(
    layer,
    state, cosine, sine, qidx, qlab, klab, route, first_table, second_table, taken_t, small_t,
    g_wide, g_gu, g_small, g_sd, g_egu, g_ed,
    out, k_q, k_kv, k_lse, k_att, k_res, k_sj, k_rc, k_ej, k_ret,
    wide, gu, small, sd, egu, ed, w_sem,
    kv_pack, q_pack, kv_all, q_all, o_pack, o_in, lse, att, res, sj, sh, sent, rc, ej, eh, result, ret, k_sem,
    kv_send, kv_recv, q_send, q_recv, o_send, o_recv, s_send, s_recv, r_send, r_recv,
):
    section, a, z, y, h = place_ids()
    ctx = ctx_of(a, z)
    loads = [
        pltpu.make_async_copy(s.at[layer], t, w_sem.at[i])
        for i, (s, t) in enumerate(((g_wide, wide), (g_gu, gu), (g_small, small), (g_sd, sd), (g_egu, egu), (g_ed, ed)))
    ]
    for load in (0, 2, 1, 3, 4, 5):
        loads[load].start()
    greet(ctx_peers())
    saves = []

    def save(source, target):
        copy = pltpu.make_async_copy(source, target, k_sem.at[len(saves)])
        copy.start()
        saves.append(copy)

    x = state[...].astype(jnp.float32)
    scale, unit = rms_parts(x)
    normed = low(unit * small_t[0:1, :])
    loads[0].wait()
    keys = low(rotate(dot(normed, wide[:, D : 2 * D]), cosine[...], sine[...]))
    values = low(dot(normed, wide[:, 2 * D : 3 * D]))
    for g in range(4):
        kv_pack[g, :, 0:192] = keys[:, 192 * g : 192 * g + 192]
        kv_pack[g, :, 192:384] = values[:, 192 * g : 192 * g + 192]
    ex_kv = Exchange(kv_pack, kv_all, kv_send, kv_recv, True, "ring")
    ex_kv.start()
    queries = low(rotate(dot(normed, wide[:, 0:D]), cosine[...], sine[...]))
    for g in range(4):
        q_pack[g] = queries[:, 192 * g : 192 * g + 192]
    ex_q = Exchange(q_pack, q_all, q_send, q_recv, False)
    ex_q.start()
    kv_all[ctx] = kv_pack[z]
    q_all[z] = q_pack[z]
    ex_q.wait_recv()
    ex_kv.wait_recv()
    save(kv_all, k_kv)
    save(q_all, k_q)

    @pl.loop(0, 4)
    def _(d):
        block = lax.rem(z + d + 1, 4)
        seen = visible_keys(qidx[block], qlab[block], klab[...])
        for head in range(3):
            span = slice(64 * head, 64 * head + 64)
            vspan = slice(192 + 64 * head, 256 + 64 * head)
            k = kv_all[:, :, span].reshape(SEQ, HEAD_DIM)
            v = kv_all[:, :, vspan].reshape(SEQ, HEAD_DIM)
            scores = jnp.where(seen, dot_t(q_all[block, :, span], k) * SCALE, NEG)
            top = jnp.max(scores, axis=-1, keepdims=True)
            weights = jnp.exp(scores - top)
            total = jnp.sum(weights, axis=-1, keepdims=True)
            o_pack[block, :, span] = low(dot(low(weights / total), v))
            lse[block, :, head : head + 1] = top + jnp.log(total)

    ex_o = Exchange(o_pack, o_in, o_send, o_recv, False)
    ex_o.start()
    save(lse, k_lse)
    o_in[z] = o_pack[z]
    ex_o.wait_recv()
    for g in range(4):
        att[:, 192 * g : 192 * g + 192] = o_in[g]
    save(att, k_att)
    res[...] = x + dot(att[...], wide[:, 3 * D :])
    save(res, k_res)
    scale, unit = rms_parts(res[...])
    normed = low(unit * small_t[1:2, :])
    sent[...] = low(dot(taken_t[...], normed)).reshape(EXPERTS, PAD_CAP, D)
    ex_s = Exchange(sent, rc, s_send, s_recv, True)
    ex_s.start()
    rc[ctx] = sent[ctx]
    loads[2].wait()
    _, gates = pair_gates(dot(normed, small[...]), route[...])
    mix = first_table[...].astype(jnp.float32) * gates[0] + second_table[...].astype(jnp.float32) * gates[1]
    loads[1].wait()

    @pl.loop(0, FF // 256)
    def _(j):
        at = pl.ds(pl.multiple_of(j * 256, 256), 256)
        up_at = pl.ds(pl.multiple_of(FF + j * 256, 256), 256)
        gate, up = dot(normed, gu[:, at]), dot(normed, gu[:, up_at])
        sj[:, at] = gate
        sj[:, up_at] = up
        sh[:, at] = low(gate * jax.nn.sigmoid(gate) * up)

    save(sj, k_sj)
    loads[3].wait()
    shared_out = dot(sh[...], sd[...])
    loads[4].wait()
    ex_s.wait_recv()
    save(rc, k_rc)

    @pl.loop(0, FF // 256)
    def _(j):
        at = pl.ds(pl.multiple_of(j * 256, 256), 256)
        up_at = pl.ds(pl.multiple_of(FF + j * 256, 256), 256)
        gate, up = dot(rc[...].reshape(SLOTS, D), egu[:, at]), dot(rc[...].reshape(SLOTS, D), egu[:, up_at])
        ej[:, at] = gate
        ej[:, up_at] = up
        eh[:, at] = low(gate * jax.nn.sigmoid(gate) * up)

    save(ej, k_ej)
    loads[5].wait()
    for j in range(D // 256):
        span = slice(256 * j, 256 * j + 256)
        result[:, :, span] = low(dot(eh[...], ed[:, span])).reshape(EXPERTS, PAD_CAP, 256)
    ex_r = Exchange(result, ret, r_send, r_recv, True)
    ex_r.start()
    ret[ctx] = result[ctx]
    ex_r.wait_recv()
    save(ret, k_ret)
    high, rest = split(mix)
    returned = ret[...].reshape(SLOTS, D)
    mixed = dot(high, returned) + dot(rest, returned)
    out[...] = low(res[...] + shared_out + mixed)
    for ex in (ex_kv, ex_q, ex_o, ex_s, ex_r):
        ex.wait_send()
    for copy in saves:
        copy.wait()


def weight_scratch():
    bf = jnp.bfloat16
    return [
        pltpu.VMEM((D, WIDE), bf), pltpu.VMEM((D, 2 * FF), bf), pltpu.VMEM((D, SMALL), bf),
        pltpu.VMEM((FF, D), bf), pltpu.VMEM((D, 2 * FF), bf), pltpu.VMEM((FF, D), bf), DMA((6,)),
    ]


KEPT = (
    ((4, ROWS, 192), jnp.bfloat16), ((8, ROWS, 384), jnp.bfloat16), ((4, ROWS, 128), jnp.float32), ((ROWS, D), jnp.bfloat16),
    ((ROWS, D), jnp.float32), ((ROWS, 2 * FF), jnp.float32), ((EXPERTS, PAD_CAP, D), jnp.bfloat16),
    ((SLOTS, 2 * FF), jnp.float32), ((EXPERTS, PAD_CAP, D), jnp.bfloat16),
)


def layer_forward(layer, state, geometry, plan, small_t, weights):
    bf, f32 = jnp.bfloat16, jnp.float32
    cosine, sine, qidx, qlab, klab = geometry
    route, first_table, second_table, taken_t = plan
    slots = pltpu.VMEM((EXPERTS, PAD_CAP, D), bf)
    outs = pl.pallas_call(
        functools.partial(forward_kernel, layer),
        out_shape=[jax.ShapeDtypeStruct((ROWS, D), bf)] + [jax.ShapeDtypeStruct(s, t) for s, t in KEPT],
        in_specs=[VMEM] * 11 + [ANY] * 6,
        out_specs=[VMEM] + [ANY] * len(KEPT),
        scratch_shapes=weight_scratch() + [
            pltpu.VMEM((4, ROWS, 384), bf), pltpu.VMEM((4, ROWS, 192), bf),
            pltpu.VMEM((8, ROWS, 384), bf), pltpu.VMEM((4, ROWS, 192), bf),
            pltpu.VMEM((4, ROWS, 192), bf), pltpu.VMEM((4, ROWS, 192), bf),
            pltpu.VMEM((4, ROWS, 128), f32), pltpu.VMEM((ROWS, D), bf), pltpu.VMEM((ROWS, D), f32),
            pltpu.VMEM((ROWS, 2 * FF), f32), pltpu.VMEM((ROWS, FF), bf),
            slots, slots, pltpu.VMEM((SLOTS, 2 * FF), f32), pltpu.VMEM((SLOTS, FF), bf), slots, slots, DMA((len(KEPT),)),
            DMA((7,)), DMA((7,)), DMA((3,)), DMA((3,)), DMA((3,)), DMA((3,)), DMA((7,)), DMA((7,)), DMA((7,)), DMA((7,)),
        ],
        compiler_params=pltpu.CompilerParams(collective_id=1 + layer, has_side_effects=True, vmem_limit_bytes=60 << 20),
        name="layer_forward",
    )(state, cosine, sine, qidx, qlab, klab, route, first_table, second_table, taken_t, small_t, *weights)
    return outs[0], outs[1:]


def backward_kernel(
    layer,
    grad, state, cosine, sine, qidx, qlab, klab, route, first_table, second_table, taken, small_t,
    g_wide, g_gu, g_small, g_sd, g_egu, g_ed,
    k_q, k_kv, k_lse, k_att, k_res, k_sj, k_rc, k_ej, k_ret,
    out, grad_small,
    p_na, p_at, p_nf, p_sh, p_rc, p_hd, p_qkv, p_pr, p_gu, p_sd, p_j, p_er,
    wide, gu, small, sd, egu, ed, w_sem,
    q_all, kv_all, lse, att, res, sj, rc, ej, ret, i_sem,
    t_na, t_at, t_nf, t_sh, t_rc, t_hd, m_qkv, m_pr, m_gu, m_sd, m_j, p_sem,
    sent, er, back, slots, o_pack, o_in, dq_pack, dq_in, dkv_pack, dkv_in, dkv_sum, normed_grad, sh, eh,
    s_send, s_recv, r_send, r_recv, o_send, o_recv, q_send, q_recv, kv_send, kv_recv,
):
    section, a, z, y, h = place_ids()
    ctx = ctx_of(a, z)
    loads = [
        pltpu.make_async_copy(s.at[layer], t, w_sem.at[i])
        for i, (s, t) in enumerate(((g_wide, wide), (g_gu, gu), (g_small, small), (g_sd, sd), (g_egu, egu), (g_ed, ed)))
    ]
    reads = [
        pltpu.make_async_copy(s, t, i_sem.at[i])
        for i, (s, t) in enumerate(zip((k_q, k_kv, k_lse, k_att, k_res, k_sj, k_rc, k_ej, k_ret), (q_all, kv_all, lse, att, res, sj, rc, ej, ret)))
    ]
    loads[2].start()
    reads[4].start()
    loads[3].start()
    reads[5].start()
    loads[1].start()
    reads[8].start()
    loads[5].start()
    reads[7].start()
    loads[4].start()
    for i in (6, 3, 0, 1, 2):
        reads[i].start()
    loads[0].start()
    greet(ctx_peers())
    saves = []

    def save(source, target):
        copy = pltpu.make_async_copy(source, target, p_sem.at[len(saves)])
        copy.start()
        saves.append(copy)

    grad_out = grad[...].astype(jnp.float32)
    m_sd[...] = low(grad_out)
    save(m_sd, p_sd)
    loads[2].wait()
    reads[4].wait()
    scale_ffn, unit_ffn = rms_parts(res[...])
    normed = low(unit_ffn * small_t[1:2, :])
    picks, gates = pair_gates(dot(normed, small[...]), route[...])
    first, second = first_table[...].astype(jnp.float32), second_table[...].astype(jnp.float32)
    mix_high, mix_rest = split(first * gates[0] + second * gates[1])
    out_high, out_rest = split(grad_out)
    slot_grads = t_dot(mix_high, out_high) + t_dot(mix_rest, out_high) + t_dot(mix_high, out_rest)
    sent[...] = low(slot_grads).reshape(EXPERTS, PAD_CAP, D)
    ex_s = Exchange(sent, er, s_send, s_recv, True)
    ex_s.start()
    er[ctx] = sent[ctx]

    loads[3].wait()
    reads[5].wait()

    @pl.loop(0, FF // 256)
    def _(j):
        at = pl.ds(pl.multiple_of(j * 256, 256), 256)
        up_at = pl.ds(pl.multiple_of(FF + j * 256, 256), 256)
        hidden_grad = dot_t(m_sd[...], sd[at, :])
        gate, up = sj[:, at], sj[:, up_at]
        sig = jax.nn.sigmoid(gate)
        m_gu[:, at] = low(hidden_grad * up * sig * (1.0 + gate * (1.0 - sig)))
        m_gu[:, up_at] = low(hidden_grad * gate * sig)
        sh[:, at] = low(gate * sig * up)
        t_sh[at, :] = low(jnp.transpose(gate * sig * up))

    save(m_gu, p_gu)
    save(t_sh, p_sh)
    t_nf[...] = low(jnp.transpose(unit_ffn * small_t[1:2, :]))
    save(t_nf, p_nf)
    loads[1].wait()

    @pl.loop(0, D // 256)
    def _(j):
        at = pl.ds(pl.multiple_of(j * 256, 256), 256)
        normed_grad[:, at] = dot_t(m_gu[...], gu[at, :])

    reads[8].wait()
    products = dot_t(m_sd[...], ret[...].reshape(SLOTS, D))
    gate_grads = [jnp.sum(products * first, axis=1, keepdims=True), jnp.sum(products * second, axis=1, keepdims=True)]
    inner = gates[0] * gate_grads[0] + gates[1] * gate_grads[1]
    chosen = [g * (d - inner) for g, d in zip(gates, gate_grads)]
    logit_grads = jnp.where(picks[0], chosen[0], 0.0) + jnp.where(picks[1], chosen[1], 0.0)
    logit_high, logit_rest = split(logit_grads)
    grad_small[...] = t_dot(normed, logit_high) + t_dot(normed, logit_rest)
    normed_grad[...] += dot_t(logit_high, small[...]) + dot_t(logit_rest, small[...])

    loads[5].wait()
    reads[7].wait()
    ex_s.wait_recv()
    save(er, p_er)

    @pl.loop(0, FF // 256)
    def _(j):
        at = pl.ds(pl.multiple_of(j * 256, 256), 256)
        up_at = pl.ds(pl.multiple_of(FF + j * 256, 256), 256)
        hidden_grad = dot_t(er[...].reshape(SLOTS, D), ed[at, :])
        gate, up = ej[:, at], ej[:, up_at]
        sig = jax.nn.sigmoid(gate)
        m_j[:, at] = low(hidden_grad * up * sig * (1.0 + gate * (1.0 - sig)))
        m_j[:, up_at] = low(hidden_grad * gate * sig)
        eh[:, at] = low(gate * sig * up)

    save(m_j, p_j)
    loads[4].wait()

    @pl.loop(0, D // 256)
    def _(j):
        at = pl.ds(pl.multiple_of(j * 256, 256), 256)
        back[:, :, at] = low(dot_t(m_j[...], egu[at, :])).reshape(EXPERTS, PAD_CAP, 256)

    ex_r = Exchange(back, slots, r_send, r_recv, True)
    ex_r.start()
    slots[ctx] = back[ctx]
    reads[6].wait()
    t_hd[...] = jnp.transpose(eh[...])
    save(t_hd, p_hd)
    t_rc[...] = jnp.transpose(rc[...].reshape(SLOTS, D))
    save(t_rc, p_rc)
    reads[3].wait()
    t_at[...] = jnp.transpose(att[...])
    save(t_at, p_at)
    loads[0].wait()
    ex_r.wait_recv()
    grad_normed = normed_grad[...] + dot(taken[...], slots[...].reshape(SLOTS, D))
    grad_values, gain_ffn = rms_back(grad_normed, small_t[1:2, :], scale_ffn, unit_ffn)
    grad_res = grad_out + grad_values
    m_pr[...] = low(grad_res)
    save(m_pr, p_pr)
    grad_att = low(dot_t(m_pr[...], wide[:, 3 * D :]))
    for g in range(4):
        o_pack[g] = grad_att[:, 192 * g : 192 * g + 192]
    ex_o = Exchange(o_pack, o_in, o_send, o_recv, False)
    ex_o.start()
    o_in[z] = o_pack[z]
    scale_attn, unit_attn = rms_parts(state[...].astype(jnp.float32))
    t_na[...] = low(jnp.transpose(unit_attn * small_t[0:1, :]))
    save(t_na, p_na)
    dkv_sum[...] = jnp.zeros_like(dkv_sum)
    for i in (0, 1, 2):
        reads[i].wait()
    ex_o.wait_recv()

    @pl.loop(0, 4)
    def _(d):
        block = lax.rem(z + d + 1, 4)
        seen = visible_keys(qidx[block], qlab[block], klab[...])
        for head in range(3):
            span = slice(64 * head, 64 * head + 64)
            vspan = slice(192 + 64 * head, 256 + 64 * head)
            q, do = q_all[block, :, span], o_in[block, :, span]
            k = kv_all[:, :, span].reshape(SEQ, HEAD_DIM)
            v = kv_all[:, :, vspan].reshape(SEQ, HEAD_DIM)
            scores = dot_t(q, k) * SCALE
            probs = jnp.where(seen, jnp.exp(scores - lse[block, :, head : head + 1]), 0.0)
            dprobs = dot_t(do, v)
            delta = jnp.sum(probs * dprobs, axis=-1, keepdims=True)
            dscores = low(probs * (dprobs - delta))
            dq_pack[block, :, span] = low(dot(dscores, k) * SCALE)
            dkv_sum[:, span] += t_dot(dscores, q) * SCALE
            dkv_sum[:, vspan] += t_dot(low(probs), do)

    ex_q = Exchange(dq_pack, dq_in, q_send, q_recv, False)
    ex_q.start()
    dkv_pack[...] = low(dkv_sum[...]).reshape(8, ROWS, 384)
    ex_kv = Exchange(dkv_pack, dkv_in, kv_send, kv_recv, True)
    ex_kv.start()
    dq_in[z] = dq_pack[z]
    dkv_in[ctx] = dkv_pack[ctx]
    ex_q.wait_recv()
    ex_kv.wait_recv()
    dq = jnp.concatenate([dq_in[g].astype(jnp.float32) for g in range(4)], axis=1)
    both = [dkv_in[g].astype(jnp.float32) + dkv_in[4 + g].astype(jnp.float32) for g in range(4)]
    dk = jnp.concatenate([v[:, :192] for v in both], axis=1)
    dv = jnp.concatenate([v[:, 192:] for v in both], axis=1)
    m_qkv[:, 0:D] = low(rotate(dq, cosine[...], -sine[...]))
    m_qkv[:, D : 2 * D] = low(rotate(dk, cosine[...], -sine[...]))
    m_qkv[:, 2 * D :] = low(dv)
    save(m_qkv, p_qkv)
    grad_normed = dot_t(m_qkv[...], wide[:, 0 : 3 * D])
    grad_values, gain_attn = rms_back(grad_normed, small_t[0:1, :], scale_attn, unit_attn)
    out[...] = grad_res + grad_values
    lane = lax.broadcasted_iota(jnp.int32, (D, SMALL), 1)
    gains_t = jnp.transpose(jnp.concatenate([gain_attn, gain_ffn, jnp.zeros((SMALL - 2, D), jnp.float32)], axis=0))
    grad_small[...] = jnp.where(lane < 2, gains_t, grad_small[...])
    for ex in (ex_s, ex_r, ex_o, ex_q, ex_kv):
        ex.wait_send()
    for copy in saves:
        copy.wait()


def layer_backward(layer, grad, state, geometry, plan, taken, small_t, weights, kept):
    bf, f32 = jnp.bfloat16, jnp.float32
    cosine, sine, qidx, qlab, klab = geometry
    route, first_table, second_table, _ = plan
    slots = pltpu.VMEM((EXPERTS, PAD_CAP, D), bf)
    shapes = [(r, c) for _, r, c in LEFT + RIGHT]
    shapes[-1] = (EXPERTS, PAD_CAP, D)
    outs = pl.pallas_call(
        functools.partial(backward_kernel, layer),
        out_shape=[jax.ShapeDtypeStruct((ROWS, D), f32), jax.ShapeDtypeStruct((D, SMALL), f32)]
        + [jax.ShapeDtypeStruct(s, bf) for s in shapes],
        in_specs=[VMEM] * 12 + [ANY] * (6 + len(KEPT)),
        out_specs=[VMEM, VMEM] + [ANY] * N_OPS,
        scratch_shapes=weight_scratch()
        + [pltpu.VMEM(s, t) for s, t in KEPT] + [DMA((len(KEPT),))]
        + [pltpu.VMEM(s, bf) for s in shapes[:-1]] + [DMA((N_OPS,))]
        + [
            slots, slots, slots, slots,
            pltpu.VMEM((4, ROWS, 192), bf), pltpu.VMEM((4, ROWS, 192), bf),
            pltpu.VMEM((4, ROWS, 192), bf), pltpu.VMEM((4, ROWS, 192), bf),
            pltpu.VMEM((8, ROWS, 384), bf), pltpu.VMEM((8, ROWS, 384), bf), pltpu.VMEM((SEQ, 384), f32),
            pltpu.VMEM((ROWS, D), f32), pltpu.VMEM((ROWS, FF), bf), pltpu.VMEM((SLOTS, FF), bf),
            DMA((7,)), DMA((7,)), DMA((7,)), DMA((7,)), DMA((3,)), DMA((3,)), DMA((3,)), DMA((3,)), DMA((7,)), DMA((7,)),
        ],
        compiler_params=pltpu.CompilerParams(collective_id=3 + layer, has_side_effects=True, vmem_limit_bytes=62 << 20),
        name="layer_backward",
    )(grad, state, cosine, sine, qidx, qlab, klab, route, first_table, second_table, taken, small_t, *weights, *kept)
    operands = list(outs[2:])
    operands[-1] = operands[-1].reshape(SLOTS, D)
    return outs[0], operands, outs[1]


def token_positions(group_row):
    labels = jnp.arange(CONT + 1, dtype=jnp.int32)
    member = (group_row[:, None] == labels[None, :]).astype(jnp.int32)
    run_sizes = jnp.sum(member, axis=0)
    run_starts = jnp.cumsum(run_sizes) - run_sizes
    first_index = jnp.sum(member * run_starts[None, :], axis=1)
    token_index = jnp.arange(group_row.shape[0], dtype=jnp.int32)
    return jnp.where(group_row == 0, token_index, run_sizes[0] + token_index - first_index)


def rotation_tables(positions):
    half = HEAD_DIM // 2
    frequency = jnp.exp(-math.log(10000.0) * jnp.arange(half, dtype=jnp.float32) / half)
    angles = positions.astype(jnp.float32)[:, None] * frequency[None, :]
    cosine, sine = jnp.cos(angles), jnp.sin(angles)
    cosine = jnp.tile(jnp.concatenate([cosine, cosine], axis=1), (1, HEADS))
    sine = jnp.tile(jnp.concatenate([-sine, sine], axis=1), (1, HEADS))
    return cosine, sine


def slot_tables(route, rank):
    pairs = ROWS * TOP
    expert = route.reshape(-1)
    key = rank.reshape(-1) * pairs + jnp.arange(pairs, dtype=jnp.int32)
    earlier = (expert[None, :] == expert[:, None]) & (key[None, :] < key[:, None])
    slot = jnp.sum(earlier.astype(jnp.int32), axis=1)
    place = jnp.where(slot < CAP, expert * PAD_CAP + slot, -1).reshape(ROWS, TOP)
    every = jnp.arange(SLOTS, dtype=jnp.int32)
    first, second = [place[:, c : c + 1] == every[None, :] for c in range(TOP)]
    both = low(first | second)
    return (route, low(first), low(second), both.T), both


def swap_cores(value):
    return lax.ppermute(value, "section", [(0, 1), (1, 0)])


def on_device(
    x_in, cotangent, group_ids, routes, priority,
    gains, w_qkv, w_out, router, shared_gate_up, shared_down, expert_gate_up, expert_down,
):
    section = lax.axis_index("section")
    ctx = lax.axis_index("ctx")
    first = section == 0

    pack = jnp.concatenate(
        [w_qkv[0], w_out[0], shared_gate_up[0], gains[0], router[0], jnp.zeros((OWN, SMALL - 2 - EXPERTS), jnp.bfloat16)],
        axis=1,
    )
    gathered = gather_weights(
        jnp.pad(pack, ((0, 16 - OWN), (0, 0))), shared_down[0], expert_gate_up[0, 0], expert_down[0, 0]
    )
    small_t = [gathered[2][layer, :, :8].astype(jnp.float32).T for layer in range(2)]

    def mine(value):
        return jnp.where(first, value[0], value[1])

    def other(value):
        return jnp.where(first, value[1], value[0])

    picked = jnp.stack([routes[0, :, 0], priority[0, :, 0]], axis=1)
    passed = swap_cores(other(picked))
    own = mine(picked)
    plans = [jnp.where(first, own, passed), jnp.where(first, passed, own)]
    plans, taken = zip(*[slot_tables(plan[0], plan[1]) for plan in plans])

    group_row = mine(group_ids[:, 0])
    positions = token_positions(group_row)
    cosine, sine = rotation_tables(lax.dynamic_slice_in_dim(positions, ctx * ROWS, ROWS))
    half_start = ctx // 4 * 512
    qlab = lax.dynamic_slice_in_dim(group_row, half_start, 512).reshape(4, ROWS, 1)
    qidx = (half_start + jnp.arange(512, dtype=jnp.int32)).reshape(4, ROWS, 1)
    geometry = (cosine, sine, qidx, qlab, group_row[None, :])

    state = mine(x_in[:, 0])
    hidden, kept_lower = layer_forward(0, state, geometry, plans[0], small_t[0], gathered)
    final, kept_upper = layer_forward(1, hidden, geometry, plans[1], small_t[1], gathered)
    hidden_grad, operands_upper, small_upper = layer_backward(
        1, mine(cotangent[:, 0]), hidden, geometry, plans[1], taken[1], small_t[1], gathered, kept_upper
    )
    input_grad, operands_lower, small_lower = layer_backward(
        0, low(hidden_grad), state, geometry, plans[0], taken[0], small_t[0], gathered, kept_lower
    )
    small = jnp.where(first, small_lower, small_upper) + swap_cores(jnp.where(first, small_upper, small_lower))
    pack_grad, sd_grad, egu_grad, ed_grad = weight_grads(operands_lower, operands_upper, small)

    def per_layer(lower, upper):
        kept_here = jnp.where(first, lower, upper)
        arrived = swap_cores(jnp.where(first, upper, lower))
        both = jnp.stack([jnp.where(first, kept_here, arrived), jnp.where(first, arrived, kept_here)])
        return both.reshape(1, 2, 1, ROWS, D)

    pack_grad = pack_grad[None, :OWN]
    tail = WIDE + 2 * FF
    return (
        per_layer(hidden, final),
        per_layer(input_grad, hidden_grad),
        pack_grad[:, :, tail : tail + 2],
        pack_grad[:, :, : 3 * D],
        pack_grad[:, :, 3 * D : WIDE],
        pack_grad[:, :, tail + 2 : tail + 2 + EXPERTS],
        pack_grad[:, :, WIDE:tail],
        sd_grad[None],
        egu_grad[None, None],
        ed_grad[None, None],
    )


def solution(mesh):
    dense = P("section", ("ctx", "fsdp"), None)
    expert = P("section", "ctx", "fsdp", None)
    tokens = P("section", None, "fsdp", "ctx", None)
    rows = P(None, "fsdp", "ctx", None)
    return jax.shard_map(
        on_device,
        mesh=mesh,
        in_specs=(rows, rows, P(None, "fsdp", None), tokens, tokens) + (dense,) * 6 + (expert,) * 2,
        out_specs=(tokens, tokens) + (dense,) * 6 + (expert,) * 2,
        check_vma=False,
    )
```

```python
import functools
import math

import jax
import jax.numpy as jnp
from jax import lax
from jax.experimental import pallas as pl
from jax.experimental.pallas import tpu as pltpu
from jax.sharding import PartitionSpec as P

MESH = pl.DeviceIdType.MESH
ANY = pl.BlockSpec(memory_space=pl.ANY)
VMEM = pl.BlockSpec(memory_space=pltpu.VMEM)
DMA = pltpu.SemaphoreType.DMA

D = 768
FF = 2048
WIDE = 3072
SMALL = 128
PACK = WIDE + 2 * FF + SMALL
OWN = 12
HEADS = 12
HEAD_DIM = 64
TOP = 2
CONT = 8
EXPERTS = 8
SEQ = 1024
ROWS = 128
CAP = 40
PAD_CAP = 48
SLOTS = EXPERTS * PAD_CAP
SCALE = 1.0 / math.sqrt(HEAD_DIM)
EPS = 1e-06
NEG = -1e30


def place_ids():
    section = lax.axis_index("section")
    ctx = lax.axis_index("ctx")
    fsdp = lax.axis_index("fsdp")
    return section, ctx // 4, lax.rem(ctx, 4), fsdp // 2, lax.rem(fsdp, 2)


def ctx_of(half, ring):
    return lax.rem(half + 2, 2) * 4 + lax.rem(ring + 4, 4)


def fsdp_of(ring, half):
    return lax.rem(ring + 4, 4) * 2 + lax.rem(half + 2, 2)


def neighbours():
    section, a, z, y, h = place_ids()
    ctx, fsdp = ctx_of(a, z), fsdp_of(y, h)
    return dict(
        core=(1 - section, ctx, fsdp),
        zp=(section, ctx_of(a, z + 1), fsdp),
        zm=(section, ctx_of(a, z - 1), fsdp),
        zx=(section, ctx_of(a + 1, z), fsdp),
        yp=(section, ctx, fsdp_of(y + 1, h)),
        ym=(section, ctx, fsdp_of(y - 1, h)),
        yx=(section, ctx, fsdp_of(y, h + 1)),
    )


def greet(devices):
    barrier = pltpu.get_barrier_semaphore()
    for device in devices:
        pl.semaphore_signal(barrier, inc=1, device_id=device, device_id_type=MESH)
    pl.semaphore_wait(barrier, len(devices))


def rows_at(ref, block, rows, part=None):
    if part is None:
        return ref.at[pl.ds(pl.multiple_of(block * rows, 16), rows)]
    half = rows // 2
    return ref.at[pl.ds(pl.multiple_of(block * rows + part * half, 16), half)]


class Hop:
    def __init__(self, sources, targets, device, send, recv):
        self.copies = [
            pltpu.make_async_remote_copy(s, t, send.at[i], recv.at[i], device_id=device, device_id_type=MESH)
            for i, (s, t) in enumerate(zip(sources, targets))
        ]

    def start(self):
        for copy in self.copies:
            copy.start()
        return self

    def wait_recv(self):
        for copy in self.copies:
            copy.wait_recv()

    def wait_send(self):
        for copy in self.copies:
            copy.wait_send()


class Tree:
    def __init__(self, over_ctx, layer, own, whole, rows, send, recv, c_send, c_recv, l_sem):
        section, a, z, y, h = place_ids()
        near = neighbours()
        self.over_ctx = over_ctx
        ring, pair = ("z", "zx") if over_ctx else ("y", "yx")
        plus, minus, across = near[ring + "p"], near[ring + "m"], near[pair]

        def block(step, side):
            return ctx_of(a + side, z + step) if over_ctx else fsdp_of(y + step, h + side)

        def views(step, side, part=None):
            return [rows_at(w, block(step, side), r, part) for w, r in zip(whole, rows)]

        def hop(index, sources, targets, device):
            return Hop(sources, targets, device, send.at[index], recv.at[index])

        mine = views(0, 0)
        self.hops = [
            hop(0, own, mine, plus),
            hop(1, own, mine, minus),
            hop(2, own, mine, across),
            hop(3, views(-1, 0, 0), views(-1, 0, 0), plus),
            hop(4, views(1, 0, 1), views(1, 0, 1), minus),
            hop(5, views(0, 1), views(0, 1), plus),
            hop(6, views(0, 1), views(0, 1), minus),
        ]
        if over_ctx:
            self.hops.append(hop(7, views(2, 0), views(2, 0), across))
        else:
            self.hops.append(hop(7, views(-1, 1, 0), views(-1, 1, 0), plus))
            self.hops.append(hop(8, views(1, 1, 1), views(1, 1, 1), minus))
        places = [(0, 0), (-1, 0), (1, 0), (0, 1), (2, 0), (-1, 1), (1, 1), (2, 1)]
        self.cores = [
            Hop(own if k == 0 else views(*p), views(*p), near["core"], c_send.at[k], c_recv.at[k]) for k, p in enumerate(places)
        ]
        self.stays = [pltpu.make_async_copy(o, m, l_sem.at[i]) for i, (o, m) in enumerate(zip(own, mine))]

    def start_own(self):
        for index in (0, 1, 2):
            self.hops[index].start()
        self.cores[0].start()
        for copy in self.stays:
            copy.start()

    def forward1(self):
        for index, starts, core in ((0, (3,), 1), (1, (4,), 2), (2, (5, 6), 3)):
            self.hops[index].wait_recv()
            for later in starts:
                self.hops[later].start()
            self.cores[core].start()

    def forward2(self):
        self.hops[3].wait_recv()
        self.hops[4].wait_recv()
        if self.over_ctx:
            self.hops[7].start()
        self.cores[4].start()
        if not self.over_ctx:
            for index, later, core in ((5, 7, 5), (6, 8, 6)):
                self.hops[index].wait_recv()
                self.hops[later].start()
                self.cores[core].start()

    def finish(self):
        if self.over_ctx:
            for index, core in ((5, 5), (6, 6), (7, 7)):
                self.hops[index].wait_recv()
                self.cores[core].start()
        else:
            self.hops[7].wait_recv()
            self.hops[8].wait_recv()
            self.cores[7].start()
        for copy in self.stays:
            copy.wait()

    def receive(self):
        for hop in self.cores:
            hop.wait_recv()

    def drain(self):
        for hop in self.hops + self.cores:
            hop.wait_send()


class Shards:
    def __init__(self, pack, sd, packs, own_sd, send, recv, l_sem):
        section, a, z, y, h = place_ids()
        ctx, fsdp = ctx_of(a, z), fsdp_of(y, h)
        wide = slice(0, WIDE + SMALL)
        rest = slice(WIDE + SMALL, PACK)
        mine = packs.at[pl.ds(pl.multiple_of(fsdp * 16, 16), 16)]
        pieces = [(pack.at[:, wide], mine.at[:, wide]), (pack.at[:, rest], mine.at[:, rest]), (sd, rows_at(own_sd, fsdp, 32))]
        self.hops = [
            [
                Hop([s], [t], device, send.at[k, pl.ds(i, 1)], recv.at[k, pl.ds(i, 1)])
                for k, device in enumerate(fsdp_peers())
            ]
            for i, (s, t) in enumerate(pieces)
        ]
        self.stays = [pltpu.make_async_copy(s, t, l_sem.at[i]) for i, (s, t) in enumerate(pieces)]

    def start(self, pieces):
        for i in pieces:
            for hop in self.hops[i]:
                hop.start()
            self.stays[i].start()

    def wait(self, pieces):
        for i in pieces:
            for hop in self.hops[i]:
                hop.wait_recv()
            self.stays[i].wait()

    def drain(self):
        for hops in self.hops:
            for hop in hops:
                hop.wait_send()


FSDP_STEPS = [(dy, dh) for dy in (1, 3, 2, 0) for dh in (0, 1) if (dy, dh) != (0, 0)]


def fsdp_peers():
    section, a, z, y, h = place_ids()
    ctx = ctx_of(a, z)
    return [(section, ctx, fsdp_of(y + dy, h + dh)) for dy, dh in FSDP_STEPS]


def close_rows(sel, packs, target, start):
    width = target.shape[1]
    step = min(width, 512)

    @pl.loop(0, width // step)
    def _(j):
        off = pl.multiple_of(j * step, 128)
        block = packs[:, pl.ds(pl.multiple_of(start + off, 128), step)]
        target[:, pl.ds(off, step)] = low(dot(sel[...], block))


def close_table(rows_from, rows_to):
    cols, rows = jnp.arange(rows_from), jnp.arange(rows_to)
    return low((rows[:, None] // OWN == cols[None, :] // 16) & (rows[:, None] % OWN == cols[None, :] % 16))


LEFT = (("na", (D, 128)), ("at", (D, 128)), ("nf", (D, 128)), ("sh", (FF, 128)), ("rc", (D, SLOTS)), ("hd", (FF, SLOTS)))
RIGHT = (
    ("qkv", (128, 3 * D)), ("pr", (128, D)), ("gu", (128, 2 * FF)), ("sd", (128, D)), ("j", (SLOTS, 2 * FF)),
    ("er", (EXPERTS, PAD_CAP, D)), ("small", (D, SMALL)),
)
OPERANDS = LEFT + RIGHT
N_OPS = len(OPERANDS)


def operand_type(name):
    return jnp.float32 if name == "small" else jnp.bfloat16


ATTENTION = (("wide", "na", "qkv", 96, 0, 3 * D, D), ("wide", "at", "pr", 96, 3 * D, D, D))
SHARED = (("gu", "nf", "gu", 96, 0, 2 * FF, 1024), ("sd", "sh", "sd", 256, 0, D, D))
EXPERT = (("egu", "rc", "j", 96, 0, 2 * FF, 1024), ("ed", "hd", "er", 256, 0, D, D))


def grads_kernel(*refs):
    lower, upper = refs[:N_OPS], refs[N_OPS : 2 * N_OPS]
    sel_t = refs[2 * N_OPS]
    out_qkv, out_out, out_small, out_gu, out_sd, out_egu, out_ed = refs[2 * N_OPS + 1 : 2 * N_OPS + 8]
    rest = refs[2 * N_OPS + 8 :]
    held = rest[:N_OPS]
    (b_wide, b_gu, b_small, b_sd, c_gu, c_sd, packs, in_pack, in_sd,
     o_local, w_send, w_recv, r_send, r_recv, e_send, e_recv, s_send, s_recv) = rest[N_OPS:]
    names = [n for n, _ in OPERANDS]
    ops = dict(zip(names, held))
    section, a, z, y, h = place_ids()
    ctx, fsdp = ctx_of(a, z), fsdp_of(y, h)
    near = neighbours()

    def bring(source, i, which):
        n, shape = OPERANDS[i]
        if i < len(LEFT):
            target = held[i].at[:, pl.ds(which * shape[1], shape[1])]
        elif n in ("er", "small"):
            target = held[i].at[which]
        else:
            target = held[i].at[pl.ds(which * shape[0], shape[0])]
        return pltpu.make_async_copy(source[i].at[which], target, o_local.at[i, which])

    order = [names.index(n) for n in ("na", "qkv", "at", "pr", "small", "nf", "gu", "sh", "sd", "rc", "j", "hd", "er")]
    for layer, source in enumerate((lower, upper)):

        @pl.when(section == layer)
        def _(source=source):
            for i in order:
                for which in range(2):
                    bring(source, i, which).start()

    greet([near["zp"], near["zm"], near["zx"]] + fsdp_peers())

    def ready(*wanted):
        for n in wanted:
            for which in range(2):
                bring(lower, names.index(n), which).wait()

    kinds = dict(wide=b_wide, gu=b_gu, small=b_small, sd=b_sd, egu=c_gu, ed=c_sd)
    buffers = {
        ATTENTION: ((b_wide, 96), (b_small, 96)),
        SHARED: ((b_gu, 96), (b_sd, 256)),
        EXPERT: ((c_gu, 96), (c_sd, 256)),
    }
    semaphores = {ATTENTION: (w_send, w_recv), SHARED: (r_send, r_recv), EXPERT: (e_send, e_recv)}

    def combine(pieces, block, slot, adds=(), part=None, target=None):
        for kind, left, right, rows, first, width, step in pieces:
            n = rows if part is None else rows // 2
            off = 0 if part is None else part * n
            lhs_rows = pl.ds(pl.multiple_of(block * rows + off, 16), n)

            @pl.loop(0, width // step)
            def _(j, kind=kind, left=left, right=right, first=first, n=n, off=off, lhs_rows=lhs_rows, step=step):
                at = pl.ds(pl.multiple_of(j * step, 256), step)
                to = pl.ds(pl.multiple_of(first + j * step, 256), step)
                if right == "er":
                    right_part = ops[right][:, :, :, at].reshape(2 * SLOTS, step)
                else:
                    right_part = ops[right][:, at]
                total = dot(ops[left][lhs_rows, :], right_part)
                for other in adds:
                    total += kinds[kind][other, off : off + n, to].astype(jnp.float32)
                if target is None:
                    kinds[kind][slot, off : off + n, to] = low(total)
                else:
                    target[kind][off : off + n, to] = total

        if pieces is ATTENTION:
            n = 96 if part is None else 48
            off = 0 if part is None else part * n
            at = pl.ds(pl.multiple_of(block * 96 + off, 16), n)
            total = ops["small"][0, at, :] + ops["small"][1, at, :]
            for other in adds:
                total += b_small[other, off : off + n, :].astype(jnp.float32)
            b_small[slot, off : off + n, :] = low(total)

    hops = {}

    def send(pieces, index, slot, to_slot, device, part=None):
        def views(which):
            return [rows_at(b.at[which], 0, r, part) for b, r in buffers[pieces]]

        sems = semaphores[pieces]
        hops[pieces, index] = Hop(views(slot), views(to_slot), near[device], sems[0].at[index], sems[1].at[index]).start()

    def arrived(pieces, *indices):
        for index in indices:
            hops[pieces, index].wait_recv()

    def sent(pieces, *indices):
        for index in indices:
            hops[pieces, index].wait_send()

    def d_block(dz, da):
        return ctx_of(a + da, z + dz)

    def e_block(dy, dh):
        return fsdp_of(y + dy, h + dh)

    def spread(pieces):
        combine(pieces, d_block(2, 1), 0)
        send(pieces, 0, 0, 1, "zx")
        combine(pieces, d_block(-1, 1), 2)
        send(pieces, 1, 2, 5, "zm")
        combine(pieces, d_block(1, 1), 3)
        send(pieces, 2, 3, 6, "zp")

    def halves(pieces):
        arrived(pieces, 0)
        combine(pieces, d_block(2, 0), 1, (1,))
        send(pieces, 3, 1, 4, "zm", 0)
        send(pieces, 4, 1, 4, "zp", 1)

    def next_ones(pieces):
        sent(pieces, 0)
        combine(pieces, d_block(-1, 0), 0, (), 1)
        arrived(pieces, 3)
        combine(pieces, d_block(-1, 0), 0, (4,), 0)
        send(pieces, 5, 0, 7, "zm")
        sent(pieces, 3, 4)
        combine(pieces, d_block(1, 0), 1, (), 0)
        arrived(pieces, 4)
        combine(pieces, d_block(1, 0), 1, (4,), 1)
        send(pieces, 6, 1, 8, "zp")

    def pair(pieces):
        arrived(pieces, 1, 2)
        combine(pieces, d_block(0, 1), 5, (5, 6))
        send(pieces, 7, 5, 9, "zx")

    def own(pieces):
        arrived(pieces, 5, 6, 7)
        combine(pieces, ctx, 7, (7, 8, 9))

    def open_rows(kind, start, width):
        step = min(width, 1024)

        @pl.loop(0, width // step)
        def _(j):
            off = pl.multiple_of(j * step, 128)
            block = kinds[kind][7, :, pl.ds(off, step)]
            packs[:, pl.ds(pl.multiple_of(start + off, 128), step)] = low(dot(sel_t[...], block))

    last = [[], [], []]
    split_at = WIDE + SMALL

    def to_owners(which):
        for k, device in enumerate(fsdp_peers()):
            dy, dh = FSDP_STEPS[k]
            block = e_block(dy, dh)
            rows = packs.at[pl.ds(pl.multiple_of(block * 16, 16), 16)]
            source, target = (
                (rows.at[:, :split_at], in_pack.at[k, :, :split_at]),
                (rows.at[:, split_at:], in_pack.at[k, :, split_at:]),
                (rows_at(b_sd.at[7], block, 32), in_sd.at[k]),
            )[which]
            last[which].append(
                Hop([source], [target], device, s_send.at[k, pl.ds(which, 1)], s_recv.at[k, pl.ds(which, 1)]).start()
            )

    def total_of(which, start, width, out):
        step = min(width, 256)

        @pl.loop(0, width // step)
        def _(j):
            at = pl.ds(pl.multiple_of(start + j * step, 128), step)
            total = packs[pl.ds(pl.multiple_of(fsdp * 16, 16), 16), at].astype(jnp.float32)
            for k in range(7):
                total += in_pack[k, :, at].astype(jnp.float32)
            out[:, pl.ds(pl.multiple_of(j * step, 128), step)] = total[:OWN]

    ready("na", "qkv", "at", "pr", "small")
    spread(ATTENTION)
    ready("nf", "gu", "sh", "sd")
    spread(SHARED)
    ready("rc", "j", "hd", "er")
    combine(EXPERT, e_block(2, 1), 0)
    send(EXPERT, 0, 0, 4, "ym", 0)
    send(EXPERT, 1, 0, 4, "yp", 1)
    halves(ATTENTION)
    combine(EXPERT, e_block(2, 0), 1)
    send(EXPERT, 2, 1, 5, "ym", 0)
    send(EXPERT, 3, 1, 5, "yp", 1)
    combine(EXPERT, e_block(-1, 1), 2, (), 1)
    combine(EXPERT, e_block(1, 1), 3, (), 0)
    arrived(EXPERT, 0)
    combine(EXPERT, e_block(-1, 1), 2, (4,), 0)
    send(EXPERT, 4, 2, 6, "ym")
    arrived(EXPERT, 1)
    combine(EXPERT, e_block(1, 1), 3, (4,), 1)
    send(EXPERT, 5, 3, 7, "yp")
    pair(ATTENTION)
    halves(SHARED)
    next_ones(ATTENTION)
    pair(SHARED)
    sent(EXPERT, 0, 1)
    combine(EXPERT, e_block(-1, 0), 0, (), 1)
    arrived(EXPERT, 2)
    combine(EXPERT, e_block(-1, 0), 0, (5,), 0)
    send(EXPERT, 6, 0, 8, "ym")
    sent(EXPERT, 2, 3)
    combine(EXPERT, e_block(1, 0), 1, (), 0)
    arrived(EXPERT, 3)
    combine(EXPERT, e_block(1, 0), 1, (5,), 1)
    send(EXPERT, 7, 1, 9, "yp")
    next_ones(SHARED)
    arrived(EXPERT, 4, 5)
    combine(EXPERT, e_block(0, 1), 6, (6, 7))
    send(EXPERT, 8, 6, 10, "yx")
    own(ATTENTION)
    open_rows("wide", 0, WIDE)
    open_rows("small", WIDE, SMALL)
    to_owners(0)
    own(SHARED)
    open_rows("gu", split_at, 2 * FF)
    to_owners(1)
    to_owners(2)
    for hop in last[0]:
        hop.wait_recv()
    total_of(0, 0, 3 * D, out_qkv)
    total_of(0, 3 * D, D, out_out)
    total_of(0, WIDE, SMALL, out_small)
    arrived(EXPERT, 6, 7, 8)
    combine(EXPERT, fsdp, 0, (8, 9, 10), None, dict(egu=out_egu, ed=out_ed))
    for hop in last[1] + last[2]:
        hop.wait_recv()
    total_of(1, split_at, 2 * FF, out_gu)
    total = b_sd[7, pl.ds(pl.multiple_of(fsdp * 32, 16), 32), :].astype(jnp.float32)
    for k in range(7):
        total += in_sd[k].astype(jnp.float32)
    out_sd[...] = total
    for pieces in (ATTENTION, SHARED):
        sent(pieces, 1, 2, 5, 6, 7)
    sent(EXPERT, 4, 5, 6, 7, 8)
    for hop in last[0] + last[1] + last[2]:
        hop.wait_send()


def weight_grads(lower, upper):
    bf, f32 = jnp.bfloat16, jnp.float32
    held = [pltpu.VMEM((shape[0], 2 * shape[1]), bf) for _, shape in LEFT]
    for name, shape in RIGHT:
        whole = (2,) + shape if name in ("er", "small") else (2 * shape[0], shape[1])
        held.append(pltpu.VMEM(whole, operand_type(name)))
    shapes = [(OWN, 3 * D), (OWN, D), (OWN, SMALL), (OWN, 2 * FF), (32, D), (96, 2 * FF), (256, D)]
    return pl.pallas_call(
        grads_kernel,
        out_shape=[jax.ShapeDtypeStruct(shape, f32) for shape in shapes],
        in_specs=[ANY] * (2 * N_OPS) + [VMEM],
        out_specs=[VMEM] * len(shapes),
        scratch_shapes=held + [
            pltpu.VMEM((10, 96, WIDE), bf),
            pltpu.VMEM((10, 96, 2 * FF), bf),
            pltpu.VMEM((10, 96, SMALL), bf),
            pltpu.VMEM((10, 256, D), bf),
            pltpu.VMEM((11, 96, 2 * FF), bf),
            pltpu.VMEM((11, 256, D), bf),
            pltpu.VMEM((128, PACK), bf),
            pltpu.VMEM((7, 16, PACK), bf),
            pltpu.VMEM((7, 32, D), bf),
            DMA((N_OPS, 2)),
            DMA((8, 2)), DMA((8, 2)), DMA((8, 2)), DMA((8, 2)),
            DMA((9, 2)), DMA((9, 2)),
            DMA((7, 3)), DMA((7, 3)),
        ],
        compiler_params=pltpu.CompilerParams(collective_id=5, has_side_effects=True, vmem_limit_bytes=62 << 20),
        name="weight_grads",
    )(*lower, *upper, close_table(128, 96).T)


def split(values):
    high = low(values)
    return high, low(values - high.astype(jnp.float32))


def rms_parts(values):
    scale = lax.rsqrt(jnp.mean(values * values, axis=-1, keepdims=True) + EPS)
    return scale, values * scale


def rms_back(grad, gain, scale, unit):
    inner = grad * gain
    grad_values = scale * (inner - unit * jnp.mean(inner * unit, axis=-1, keepdims=True))
    return grad_values, jnp.sum(grad * unit, axis=0, keepdims=True)


def dot(left, right):
    return jnp.dot(left, right, preferred_element_type=jnp.float32)


def dot_t(left, right):
    return lax.dot_general(left, right, (((1,), (1,)), ((), ())), preferred_element_type=jnp.float32)


def t_dot(left, right):
    return lax.dot_general(left, right, (((0,), (0,)), ((), ())), preferred_element_type=jnp.float32)


def low(values):
    return values.astype(jnp.bfloat16)


def rotate(values, cosine, sine):
    half = HEAD_DIM // 2
    lower = lax.broadcasted_iota(jnp.int32, (values.shape[0], 128), 1) % HEAD_DIM < half
    parts = []
    for start in range(0, values.shape[1], 128):
        span = slice(start, start + 128)
        part = values[:, span]
        other = jnp.where(lower, pltpu.roll(part, 128 - half, 1), pltpu.roll(part, half, 1))
        parts.append(part * cosine[:, span] + other * sine[:, span])
    return jnp.concatenate(parts, axis=1)


def visible_keys(qidx, qlab, klab):
    kidx = lax.broadcasted_iota(jnp.int32, (qidx.shape[0], klab.shape[1]), 1)
    return (kidx <= qidx) & ((klab == 0) | (klab == qlab))


def pair_gates(logits, route):
    lane = lax.broadcasted_iota(jnp.int32, logits.shape, 1)
    picks = [lane == route[:, c : c + 1] + 2 for c in range(TOP)]
    first, second = [jnp.sum(jnp.where(p, logits, 0.0), axis=1, keepdims=True) for p in picks]
    top = jnp.maximum(first, second)
    first, second = jnp.exp(first - top), jnp.exp(second - top)
    total = first + second
    return picks, [first / total, second / total]


class Exchange:
    def __init__(self, source, target, send, recv, everyone, block_of=None):
        section, a, z, y, h = place_ids()
        fsdp = fsdp_of(y, h)
        offsets = [(1, 0), (1, 1), (1, 3), (1, 2)] if everyone else []
        self.copies = []
        for k, (da, dz) in enumerate(offsets + [(0, 1), (0, 3), (0, 2)]):
            c, zz = ctx_of(a + da, z + dz), lax.rem(z + dz, 4)
            block = zz if block_of == "ring" or not everyone else c
            to = ctx_of(a, z) if everyone else z
            self.copies.append(
                pltpu.make_async_remote_copy(
                    source.at[block], target.at[to], send.at[k], recv.at[k], device_id=(section, c, fsdp), device_id_type=MESH
                )
            )

    def start(self):
        for copy in self.copies:
            copy.start()

    def wait_recv(self):
        for copy in self.copies:
            copy.wait_recv()

    def wait_send(self):
        for copy in self.copies:
            copy.wait_send()


def ctx_peers():
    section, a, z, y, h = place_ids()
    fsdp = fsdp_of(y, h)
    return [(section, ctx_of(a + da, z + dz), fsdp) for da in range(2) for dz in range(4) if (da, dz) != (0, 0)]


def forward_kernel(
    pack, g_sd, g_egu, g_ed, sel,
    state, cosine, sine, qidx, qlab, klab, route, first_table, second_table, taken_t,
    out_lower, out_upper,
    l_wide, l_gu, l_small, l_sd, l_egu, l_ed, u_wide, u_gu, u_small, u_sd, u_egu, u_ed,
    *rest,
):
    kept = (rest[:9], rest[9:18])
    (wide, gu, small, sd, egu, ed, w_sem,
     packs, own_wide, own_small, own_gu, own_sd, g_stay, sh_send, sh_recv,
     w_send, w_recv, r_send, r_recv, e_send, e_recv, wc_send, wc_recv, rc_send, rc_recv, ec_send, ec_recv,
     kv_pack, q_pack, kv_all, q_all, o_pack, o_in, lse, att, res, sj, sh, sent, rc, ej, eh, result, ret, k_sem,
     x_send, x_recv) = rest[18:]
    section, a, z, y, h = place_ids()
    ctx = ctx_of(a, z)
    wholes = ((l_wide, l_gu, l_small, l_sd, l_egu, l_ed), (u_wide, u_gu, u_small, u_sd, u_egu, u_ed))
    greet([neighbours()["core"]] + ctx_peers() + fsdp_peers())

    shards = Shards(pack, g_sd, packs, own_sd, sh_send, sh_recv, g_stay.at[0])
    trees = []
    for layer in range(2):
        t_wide, t_gu, t_small, t_sd, t_egu, t_ed = wholes[layer]
        trees.append(
            dict(
                w=Tree(True, layer, [own_wide, own_small], [t_wide, t_small], (96, 96),
                       w_send, w_recv, wc_send.at[layer], wc_recv.at[layer], g_stay.at[1]),
                r=Tree(True, layer, [own_gu, own_sd], [t_gu, t_sd], (96, 256),
                       r_send, r_recv, rc_send.at[layer], rc_recv.at[layer], g_stay.at[2]),
                e=Tree(False, layer, [g_egu, g_ed], [t_egu, t_ed], (96, 256),
                       e_send, e_recv, ec_send.at[layer], ec_recv.at[layer], g_stay.at[3]),
            )
        )

    def drive(layer, *steps):
        @pl.when(section == layer)
        def _():
            for step in steps:
                step()

    def close_wide():
        shards.wait((0,))
        close_rows(sel, packs, own_wide, 0)
        close_rows(sel, packs, own_small, WIDE)

    def close_rest():
        shards.wait((1, 2))
        close_rows(sel, packs, own_gu, WIDE + SMALL)

    def arrived(layer, group):
        drive(layer, trees[layer][group].finish)

        @pl.when(section != layer)
        def _():
            trees[layer][group].receive()

    def load(layer, *which):
        for i in which:
            target = (wide.at[layer], gu, small.at[layer], sd, egu, ed)[i]
            pltpu.make_async_copy(wholes[layer][i], target, w_sem.at[layer, i]).start()

    def loaded(layer, *which):
        for i in which:
            target = (wide.at[layer], gu, small.at[layer], sd, egu, ed)[i]
            pltpu.make_async_copy(wholes[layer][i], target, w_sem.at[layer, i]).wait()

    lower, upper = trees
    hooks = {
        (0, "start"): lambda: (
            drive(0, lambda: shards.start((0,)), close_wide, lambda: shards.start((1, 2)), lower["w"].start_own, close_rest,
                  lower["w"].forward1, lower["e"].start_own, lower["w"].forward2, lower["r"].start_own),
            arrived(0, "w"), load(0, 0, 2),
        ),
        (0, "keys"): lambda: (drive(0, lower["e"].forward1), drive(1, lambda: shards.start((0, 1, 2)))),
        (0, "queries"): lambda: drive(0, lower["r"].forward1),
        (0, "block1"): lambda: drive(0, lower["e"].forward2),
        (0, "block2"): lambda: drive(1, close_wide, upper["w"].start_own),
        (0, "attended"): lambda: (drive(0, lower["r"].forward2), drive(1, close_rest)),
        (0, "sent"): lambda: (arrived(0, "r"), load(0, 1, 3)),
        (0, "shared0"): lambda: (drive(1, upper["w"].forward1, upper["e"].start_own),),
        (0, "shared"): lambda: (arrived(0, "e"), load(0, 4, 5)),
        (0, "expert1"): lambda: drive(1, upper["r"].start_own),
        (0, "expert2"): lambda: drive(1, upper["w"].forward2),
        (0, "expert3"): lambda: drive(1, upper["e"].forward1),
        (0, "returned"): lambda: drive(1, upper["r"].forward1),
        (1, "start"): lambda: (arrived(1, "w"), load(1, 0, 2)),
        (1, "keys"): lambda: drive(1, upper["e"].forward2),
        (1, "block0"): lambda: drive(1, upper["r"].forward2),
        (1, "sent"): lambda: (arrived(1, "r"), load(1, 1, 3)),
        (1, "shared"): lambda: (arrived(1, "e"), load(1, 4, 5)),
    }

    def one_layer(layer, x, out):
        def hook(name):
            if (layer, name) in hooks:
                hooks[layer, name]()

        k_q, k_kv, k_lse, k_att, k_res, k_sj, k_rc, k_ej, k_ret = kept[layer]
        saves = []

        def save(source, target):
            copy = pltpu.make_async_copy(source, target, k_sem.at[len(saves)])
            copy.start()
            saves.append(copy)

        def exchange(index, source, target, everyone, block_of=None):
            sems = x_send.at[layer, index], x_recv.at[layer, index]
            return Exchange(source, target, *sems, everyone, block_of)

        scale, unit = rms_parts(x)
        hook("start")
        loaded(layer, 0, 2)
        wide_l, small_l = wide.at[layer], small.at[layer]
        gains = jnp.transpose(small_l[...].astype(jnp.float32))
        normed = low(unit * gains[0:1, :])
        keys = low(rotate(dot(normed, wide_l[:, D : 2 * D]), cosine[...], sine[...]))
        values = low(dot(normed, wide_l[:, 2 * D : 3 * D]))
        for g in range(4):
            kv_pack[g, :, 0:192] = keys[:, 192 * g : 192 * g + 192]
            kv_pack[g, :, 192:384] = values[:, 192 * g : 192 * g + 192]
        ex_kv = exchange(0, kv_pack, kv_all, True, "ring")
        ex_kv.start()
        hook("keys")
        queries = low(rotate(dot(normed, wide_l[:, 0:D]), cosine[...], sine[...]))
        for g in range(4):
            q_pack[g] = queries[:, 192 * g : 192 * g + 192]
        ex_q = exchange(1, q_pack, q_all, False)
        ex_q.start()
        kv_all[ctx] = kv_pack[z]
        q_all[z] = q_pack[z]
        hook("queries")
        ex_q.wait_recv()
        ex_kv.wait_recv()
        save(kv_all, k_kv)
        save(q_all, k_q)

        def attend(d):
            block = lax.rem(z + d + 1, 4)
            seen = visible_keys(qidx[block], qlab[block], klab[...])
            for head in range(3):
                span = slice(64 * head, 64 * head + 64)
                vspan = slice(192 + 64 * head, 256 + 64 * head)
                k = kv_all[:, :, span].reshape(SEQ, HEAD_DIM)
                v = kv_all[:, :, vspan].reshape(SEQ, HEAD_DIM)
                scores = jnp.where(seen, dot_t(q_all[block, :, span], k) * SCALE, NEG)
                top = jnp.max(scores, axis=-1, keepdims=True)
                weights = jnp.exp(scores - top)
                total = jnp.sum(weights, axis=-1, keepdims=True)
                o_pack[block, :, span] = low(dot(low(weights / total), v))
                lse[block, :, head : head + 1] = top + jnp.log(total)

        for d in range(4):
            pl.loop(d, d + 1)(attend)
            hook(f"block{d}")

        ex_o = exchange(2, o_pack, o_in, False)
        ex_o.start()
        save(lse, k_lse)
        o_in[z] = o_pack[z]
        hook("attended")
        ex_o.wait_recv()
        for g in range(4):
            att[:, 192 * g : 192 * g + 192] = o_in[g]
        save(att, k_att)
        res[...] = x + dot(att[...], wide_l[:, 3 * D :])
        save(res, k_res)
        scale, unit = rms_parts(res[...])
        normed = low(unit * gains[1:2, :])
        sent[...] = low(dot(taken_t[layer], normed)).reshape(EXPERTS, PAD_CAP, D)
        ex_s = exchange(3, sent, rc, True)
        ex_s.start()
        rc[ctx] = sent[ctx]
        _, gates = pair_gates(dot(normed, small_l[...]), route[layer])
        mix = first_table[layer].astype(jnp.float32) * gates[0] + second_table[layer].astype(jnp.float32) * gates[1]
        hook("sent")
        loaded(layer, 1)

        def shared_part(j):
            at = pl.ds(pl.multiple_of(j * 256, 256), 256)
            up_at = pl.ds(pl.multiple_of(FF + j * 256, 256), 256)
            gate, up = dot(normed, gu[:, at]), dot(normed, gu[:, up_at])
            sj[:, at] = gate
            sj[:, up_at] = up
            sh[:, at] = low(gate * jax.nn.sigmoid(gate) * up)

        for d in range(2):
            pl.loop(4 * d, 4 * d + 4)(shared_part)
            hook(f"shared{d}")

        save(sj, k_sj)
        hook("shared")
        loaded(layer, 3)
        shared_out = dot(sh[...], sd[...])
        ex_s.wait_recv()
        save(rc, k_rc)
        loaded(layer, 4)

        def expert_part(j):
            at = pl.ds(pl.multiple_of(j * 256, 256), 256)
            up_at = pl.ds(pl.multiple_of(FF + j * 256, 256), 256)
            gate, up = dot(rc[...].reshape(SLOTS, D), egu[:, at]), dot(rc[...].reshape(SLOTS, D), egu[:, up_at])
            ej[:, at] = gate
            ej[:, up_at] = up
            eh[:, at] = low(gate * jax.nn.sigmoid(gate) * up)

        for d in range(4):
            pl.loop(2 * d, 2 * d + 2)(expert_part)
            hook(f"expert{d}")

        save(ej, k_ej)
        loaded(layer, 5)
        for j in range(D // 256):
            span = slice(256 * j, 256 * j + 256)
            result[:, :, span] = low(dot(eh[...], ed[:, span])).reshape(EXPERTS, PAD_CAP, 256)
        ex_r = exchange(4, result, ret, True)
        for copy in saves[:2]:
            copy.wait()
        ex_r.start()
        ret[ctx] = result[ctx]
        hook("returned")
        ex_r.wait_recv()
        save(ret, k_ret)
        high, rest_of = split(mix)
        returned = ret[...].reshape(SLOTS, D)
        mixed = dot(high, returned) + dot(rest_of, returned)
        out[...] = low(res[...] + shared_out + mixed)
        for ex in (ex_kv, ex_q, ex_o, ex_s, ex_r):
            ex.wait_send()
        for copy in saves[2:]:
            copy.wait()

    one_layer(0, state[...].astype(jnp.float32), out_lower)
    one_layer(1, out_lower[...].astype(jnp.float32), out_upper)
    for layer in range(2):
        drive(layer, shards.drain, *[tree.drain for tree in trees[layer].values()])


def weight_scratch():
    bf = jnp.bfloat16
    return [
        pltpu.VMEM((D, WIDE), bf), pltpu.VMEM((D, 2 * FF), bf), pltpu.VMEM((D, SMALL), bf),
        pltpu.VMEM((FF, D), bf), pltpu.VMEM((D, 2 * FF), bf), pltpu.VMEM((FF, D), bf), DMA((6,)),
    ]


KEPT = (
    ((4, ROWS, 192), jnp.bfloat16), ((8, ROWS, 384), jnp.bfloat16), ((4, ROWS, 128), jnp.float32), ((ROWS, D), jnp.bfloat16),
    ((ROWS, D), jnp.float32), ((ROWS, 2 * FF), jnp.float32), ((EXPERTS, PAD_CAP, D), jnp.bfloat16),
    ((SLOTS, 2 * FF), jnp.float32), ((EXPERTS, PAD_CAP, D), jnp.bfloat16),
)


WEIGHTS = ((D, WIDE), (D, 2 * FF), (D, SMALL), (FF, D), (D, 2 * FF), (FF, D))


def forward(pack, sd, egu, ed, state, geometry, plans):
    bf, f32 = jnp.bfloat16, jnp.float32
    slots = pltpu.VMEM((EXPERTS, PAD_CAP, D), bf)
    tables = [jnp.stack(pair) for pair in zip(*plans)]
    outs = pl.pallas_call(
        forward_kernel,
        out_shape=[jax.ShapeDtypeStruct((ROWS, D), bf)] * 2
        + [jax.ShapeDtypeStruct(s, bf) for s in WEIGHTS] * 2
        + [jax.ShapeDtypeStruct(s, t) for s, t in KEPT] * 2,
        in_specs=[ANY] * 4 + [VMEM] * 11,
        out_specs=[VMEM] * 2 + [ANY] * (2 * len(WEIGHTS) + 2 * len(KEPT)),
        scratch_shapes=[
            pltpu.VMEM((2, D, WIDE), bf), pltpu.VMEM((D, 2 * FF), bf), pltpu.VMEM((2, D, SMALL), bf),
            pltpu.VMEM((FF, D), bf), pltpu.VMEM((D, 2 * FF), bf), pltpu.VMEM((FF, D), bf), DMA((2, 6)),
            pltpu.VMEM((128, PACK), bf), pltpu.VMEM((96, WIDE), bf), pltpu.VMEM((96, SMALL), bf),
            pltpu.VMEM((96, 2 * FF), bf), pltpu.VMEM((256, D), bf), DMA((4, 3)), DMA((7, 3)), DMA((7, 3)),
            DMA((8, 2)), DMA((8, 2)), DMA((8, 2)), DMA((8, 2)), DMA((9, 2)), DMA((9, 2)),
        ]
        + [DMA((2, 8, 2))] * 6
        + [
            pltpu.VMEM((4, ROWS, 384), bf), pltpu.VMEM((4, ROWS, 192), bf),
            pltpu.VMEM((8, ROWS, 384), bf), pltpu.VMEM((4, ROWS, 192), bf),
            pltpu.VMEM((4, ROWS, 192), bf), pltpu.VMEM((4, ROWS, 192), bf),
            pltpu.VMEM((4, ROWS, 128), f32), pltpu.VMEM((ROWS, D), bf), pltpu.VMEM((ROWS, D), f32),
            pltpu.VMEM((ROWS, 2 * FF), f32), pltpu.VMEM((ROWS, FF), bf),
            slots, slots, pltpu.VMEM((SLOTS, 2 * FF), f32), pltpu.VMEM((SLOTS, FF), bf), slots, slots, DMA((len(KEPT),)),
            DMA((2, 5, 7)), DMA((2, 5, 7)),
        ],
        compiler_params=pltpu.CompilerParams(collective_id=1, has_side_effects=True, vmem_limit_bytes=60 << 20),
        name="forward",
    )(pack, sd, egu, ed, close_table(128, 96), state, *geometry, *tables)
    weights, kept = outs[2 : 2 + 2 * len(WEIGHTS)], outs[2 + 2 * len(WEIGHTS) :]
    return outs[:2], (weights[: len(WEIGHTS)], weights[len(WEIGHTS) :]), (kept[: len(KEPT)], kept[len(KEPT) :])


def backward_kernel(
    layer,
    grad, state, cosine, sine, qidx, qlab, klab, route, first_table, second_table, taken, small_t,
    g_wide, g_gu, g_small, g_sd, g_egu, g_ed,
    k_q, k_kv, k_lse, k_att, k_res, k_sj, k_rc, k_ej, k_ret,
    out, out_both,
    p_na, p_at, p_nf, p_sh, p_rc, p_hd, p_qkv, p_pr, p_gu, p_sd, p_j, p_er, p_small,
    wide, gu, small, sd, egu, ed, w_sem,
    q_all, kv_all, lse, att, res, sj, rc, ej, ret, i_sem,
    t_na, t_at, t_nf, t_sh, t_rc, t_hd, m_qkv, m_pr, m_gu, m_sd, m_j, grad_small, p_sem, p_send, p_recv,
    sent, er, back, slots, o_pack, o_in, dq_pack, dq_in, dkv_pack, dkv_in, dkv_sum, normed_grad, sh, eh,
    s_send, s_recv, r_send, r_recv, o_send, o_recv, q_send, q_recv, kv_send, kv_recv,
):
    section, a, z, y, h = place_ids()
    ctx = ctx_of(a, z)
    loads = [
        pltpu.make_async_copy(s, t, w_sem.at[i])
        for i, (s, t) in enumerate(((g_wide, wide), (g_gu, gu), (g_small, small), (g_sd, sd), (g_egu, egu), (g_ed, ed)))
    ]
    reads = [
        pltpu.make_async_copy(s, t, i_sem.at[i])
        for i, (s, t) in enumerate(zip((k_q, k_kv, k_lse, k_att, k_res, k_sj, k_rc, k_ej, k_ret), (q_all, kv_all, lse, att, res, sj, rc, ej, ret)))
    ]
    loads[2].start()
    reads[4].start()
    loads[3].start()
    reads[5].start()
    loads[1].start()
    reads[8].start()
    loads[5].start()
    reads[7].start()
    loads[4].start()
    for i in (6, 3, 0, 1, 2):
        reads[i].start()
    loads[0].start()
    near = neighbours()
    greet([near["core"]] + ctx_peers())
    saves = []

    def save(source, target):
        i = len(saves)
        here = pltpu.make_async_copy(source, target.at[0], p_sem.at[i])
        away = pltpu.make_async_remote_copy(
            source, target.at[1], p_send.at[i], p_recv.at[i], device_id=near["core"], device_id_type=MESH
        )
        saves.append((here, away))

        @pl.when(section == layer)
        def _():
            here.start()

        @pl.when(section != layer)
        def _():
            away.start()

    grad_out = grad[...].astype(jnp.float32)
    m_sd[...] = low(grad_out)
    save(m_sd, p_sd)
    loads[2].wait()
    reads[4].wait()
    scale_ffn, unit_ffn = rms_parts(res[...])
    normed = low(unit_ffn * small_t[1:2, :])
    picks, gates = pair_gates(dot(normed, small[...]), route[...])
    first, second = first_table[...].astype(jnp.float32), second_table[...].astype(jnp.float32)
    mix_high, mix_rest = split(first * gates[0] + second * gates[1])
    out_high, out_rest = split(grad_out)
    slot_grads = t_dot(mix_high, out_high) + t_dot(mix_rest, out_high) + t_dot(mix_high, out_rest)
    sent[...] = low(slot_grads).reshape(EXPERTS, PAD_CAP, D)
    ex_s = Exchange(sent, er, s_send, s_recv, True)
    ex_s.start()
    er[ctx] = sent[ctx]

    loads[3].wait()
    reads[5].wait()

    @pl.loop(0, FF // 256)
    def _(j):
        at = pl.ds(pl.multiple_of(j * 256, 256), 256)
        up_at = pl.ds(pl.multiple_of(FF + j * 256, 256), 256)
        hidden_grad = dot_t(m_sd[...], sd[at, :])
        gate, up = sj[:, at], sj[:, up_at]
        sig = jax.nn.sigmoid(gate)
        m_gu[:, at] = low(hidden_grad * up * sig * (1.0 + gate * (1.0 - sig)))
        m_gu[:, up_at] = low(hidden_grad * gate * sig)
        sh[:, at] = low(gate * sig * up)
        t_sh[at, :] = low(jnp.transpose(gate * sig * up))

    save(m_gu, p_gu)
    save(t_sh, p_sh)
    t_nf[...] = low(jnp.transpose(unit_ffn * small_t[1:2, :]))
    save(t_nf, p_nf)
    loads[1].wait()

    @pl.loop(0, D // 256)
    def _(j):
        at = pl.ds(pl.multiple_of(j * 256, 256), 256)
        normed_grad[:, at] = dot_t(m_gu[...], gu[at, :])

    reads[8].wait()
    products = dot_t(m_sd[...], ret[...].reshape(SLOTS, D))
    gate_grads = [jnp.sum(products * first, axis=1, keepdims=True), jnp.sum(products * second, axis=1, keepdims=True)]
    inner = gates[0] * gate_grads[0] + gates[1] * gate_grads[1]
    chosen = [g * (d - inner) for g, d in zip(gates, gate_grads)]
    logit_grads = jnp.where(picks[0], chosen[0], 0.0) + jnp.where(picks[1], chosen[1], 0.0)
    logit_high, logit_rest = split(logit_grads)
    grad_small[...] = t_dot(normed, logit_high) + t_dot(normed, logit_rest)
    normed_grad[...] += dot_t(logit_high, small[...]) + dot_t(logit_rest, small[...])

    loads[5].wait()
    reads[7].wait()
    ex_s.wait_recv()
    save(er, p_er)

    @pl.loop(0, FF // 256)
    def _(j):
        at = pl.ds(pl.multiple_of(j * 256, 256), 256)
        up_at = pl.ds(pl.multiple_of(FF + j * 256, 256), 256)
        hidden_grad = dot_t(er[...].reshape(SLOTS, D), ed[at, :])
        gate, up = ej[:, at], ej[:, up_at]
        sig = jax.nn.sigmoid(gate)
        m_j[:, at] = low(hidden_grad * up * sig * (1.0 + gate * (1.0 - sig)))
        m_j[:, up_at] = low(hidden_grad * gate * sig)
        eh[:, at] = low(gate * sig * up)

    save(m_j, p_j)
    loads[4].wait()

    @pl.loop(0, D // 256)
    def _(j):
        at = pl.ds(pl.multiple_of(j * 256, 256), 256)
        back[:, :, at] = low(dot_t(m_j[...], egu[at, :])).reshape(EXPERTS, PAD_CAP, 256)

    ex_r = Exchange(back, slots, r_send, r_recv, True)
    ex_r.start()
    slots[ctx] = back[ctx]
    reads[6].wait()
    t_hd[...] = jnp.transpose(eh[...])
    save(t_hd, p_hd)
    t_rc[...] = jnp.transpose(rc[...].reshape(SLOTS, D))
    save(t_rc, p_rc)
    reads[3].wait()
    t_at[...] = jnp.transpose(att[...])
    save(t_at, p_at)
    loads[0].wait()
    ex_r.wait_recv()
    grad_normed = normed_grad[...] + dot(taken[...], slots[...].reshape(SLOTS, D))
    grad_values, gain_ffn = rms_back(grad_normed, small_t[1:2, :], scale_ffn, unit_ffn)
    grad_res = grad_out + grad_values
    m_pr[...] = low(grad_res)
    save(m_pr, p_pr)
    grad_att = low(dot_t(m_pr[...], wide[:, 3 * D :]))
    for g in range(4):
        o_pack[g] = grad_att[:, 192 * g : 192 * g + 192]
    ex_o = Exchange(o_pack, o_in, o_send, o_recv, False)
    ex_o.start()
    o_in[z] = o_pack[z]
    scale_attn, unit_attn = rms_parts(state[...].astype(jnp.float32))
    t_na[...] = low(jnp.transpose(unit_attn * small_t[0:1, :]))
    save(t_na, p_na)
    dkv_sum[...] = jnp.zeros_like(dkv_sum)
    for i in (0, 1, 2):
        reads[i].wait()
    ex_o.wait_recv()

    @pl.loop(0, 4)
    def _(d):
        block = lax.rem(z + d + 1, 4)
        seen = visible_keys(qidx[block], qlab[block], klab[...])
        for head in range(3):
            span = slice(64 * head, 64 * head + 64)
            vspan = slice(192 + 64 * head, 256 + 64 * head)
            q, do = q_all[block, :, span], o_in[block, :, span]
            k = kv_all[:, :, span].reshape(SEQ, HEAD_DIM)
            v = kv_all[:, :, vspan].reshape(SEQ, HEAD_DIM)
            scores = dot_t(q, k) * SCALE
            probs = jnp.where(seen, jnp.exp(scores - lse[block, :, head : head + 1]), 0.0)
            dprobs = dot_t(do, v)
            delta = jnp.sum(probs * dprobs, axis=-1, keepdims=True)
            dscores = low(probs * (dprobs - delta))
            dq_pack[block, :, span] = low(dot(dscores, k) * SCALE)
            dkv_sum[:, span] += t_dot(dscores, q) * SCALE
            dkv_sum[:, vspan] += t_dot(low(probs), do)

    ex_q = Exchange(dq_pack, dq_in, q_send, q_recv, False)
    ex_q.start()
    dkv_pack[...] = low(dkv_sum[...]).reshape(8, ROWS, 384)
    ex_kv = Exchange(dkv_pack, dkv_in, kv_send, kv_recv, True)
    ex_kv.start()
    dq_in[z] = dq_pack[z]
    dkv_in[ctx] = dkv_pack[ctx]
    ex_q.wait_recv()
    ex_kv.wait_recv()
    dq = jnp.concatenate([dq_in[g].astype(jnp.float32) for g in range(4)], axis=1)
    both = [dkv_in[g].astype(jnp.float32) + dkv_in[4 + g].astype(jnp.float32) for g in range(4)]
    dk = jnp.concatenate([v[:, :192] for v in both], axis=1)
    dv = jnp.concatenate([v[:, 192:] for v in both], axis=1)
    m_qkv[:, 0:D] = low(rotate(dq, cosine[...], -sine[...]))
    m_qkv[:, D : 2 * D] = low(rotate(dk, cosine[...], -sine[...]))
    m_qkv[:, 2 * D :] = low(dv)
    save(m_qkv, p_qkv)
    grad_normed = dot_t(m_qkv[...], wide[:, 0 : 3 * D])
    grad_values, gain_attn = rms_back(grad_normed, small_t[0:1, :], scale_attn, unit_attn)
    out[...] = grad_res + grad_values
    lane = lax.broadcasted_iota(jnp.int32, (D, SMALL), 1)
    gains_t = jnp.transpose(jnp.concatenate([gain_attn, gain_ffn, jnp.zeros((SMALL - 2, D), jnp.float32)], axis=0))
    grad_small[...] = jnp.where(lane < 2, gains_t, grad_small[...])
    save(grad_small, p_small)
    save(out, out_both)
    for ex in (ex_s, ex_r, ex_o, ex_q, ex_kv):
        ex.wait_send()

    @pl.when(section == layer)
    def _():
        for here, away in saves:
            here.wait()
            away.wait_recv()

    @pl.when(section != layer)
    def _():
        for here, away in saves:
            away.wait_send()


def layer_backward(layer, grad, state, geometry, plan, taken, small_t, weights, kept):
    bf, f32 = jnp.bfloat16, jnp.float32
    cosine, sine, qidx, qlab, klab = geometry
    route, first_table, second_table, _ = plan
    slots = pltpu.VMEM((EXPERTS, PAD_CAP, D), bf)
    shapes = dict(OPERANDS)
    order = ("na", "at", "nf", "sh", "rc", "hd", "qkv", "pr", "gu", "sd", "j", "er", "small")
    outs = pl.pallas_call(
        functools.partial(backward_kernel, layer),
        out_shape=[jax.ShapeDtypeStruct((ROWS, D), f32), jax.ShapeDtypeStruct((2, ROWS, D), f32)]
        + [jax.ShapeDtypeStruct((2,) + shapes[n], operand_type(n)) for n in order],
        in_specs=[VMEM] * 12 + [ANY] * (6 + len(KEPT)),
        out_specs=[VMEM, ANY] + [ANY] * N_OPS,
        scratch_shapes=weight_scratch()
        + [pltpu.VMEM(s, t) for s, t in KEPT] + [DMA((len(KEPT),))]
        + [pltpu.VMEM(shapes[n], operand_type(n)) for n in order if n != "er"] + [DMA((N_OPS + 1,))] * 3
        + [
            slots, slots, slots, slots,
            pltpu.VMEM((4, ROWS, 192), bf), pltpu.VMEM((4, ROWS, 192), bf),
            pltpu.VMEM((4, ROWS, 192), bf), pltpu.VMEM((4, ROWS, 192), bf),
            pltpu.VMEM((8, ROWS, 384), bf), pltpu.VMEM((8, ROWS, 384), bf), pltpu.VMEM((SEQ, 384), f32),
            pltpu.VMEM((ROWS, D), f32), pltpu.VMEM((ROWS, FF), bf), pltpu.VMEM((SLOTS, FF), bf),
            DMA((7,)), DMA((7,)), DMA((7,)), DMA((7,)), DMA((3,)), DMA((3,)), DMA((3,)), DMA((3,)), DMA((7,)), DMA((7,)),
        ],
        compiler_params=pltpu.CompilerParams(collective_id=3 + layer, has_side_effects=True, vmem_limit_bytes=62 << 20),
        name="layer_backward",
    )(grad, state, cosine, sine, qidx, qlab, klab, route, first_table, second_table, taken, small_t, *weights, *kept)
    return outs[0], outs[1], outs[2:]


def token_positions(group_row):
    labels = jnp.arange(CONT + 1, dtype=jnp.int32)
    member = (group_row[:, None] == labels[None, :]).astype(jnp.int32)
    run_sizes = jnp.sum(member, axis=0)
    run_starts = jnp.cumsum(run_sizes) - run_sizes
    first_index = jnp.sum(member * run_starts[None, :], axis=1)
    token_index = jnp.arange(group_row.shape[0], dtype=jnp.int32)
    return jnp.where(group_row == 0, token_index, run_sizes[0] + token_index - first_index)


def rotation_tables(positions):
    half = HEAD_DIM // 2
    frequency = jnp.exp(-math.log(10000.0) * jnp.arange(half, dtype=jnp.float32) / half)
    angles = positions.astype(jnp.float32)[:, None] * frequency[None, :]
    cosine, sine = jnp.cos(angles), jnp.sin(angles)
    cosine = jnp.tile(jnp.concatenate([cosine, cosine], axis=1), (1, HEADS))
    sine = jnp.tile(jnp.concatenate([-sine, sine], axis=1), (1, HEADS))
    return cosine, sine


def slot_tables(route, rank):
    pairs = ROWS * TOP
    expert = route.reshape(-1)
    key = rank.reshape(-1) * pairs + jnp.arange(pairs, dtype=jnp.int32)
    earlier = (expert[None, :] == expert[:, None]) & (key[None, :] < key[:, None])
    slot = jnp.sum(earlier.astype(jnp.int32), axis=1)
    place = jnp.where(slot < CAP, expert * PAD_CAP + slot, -1).reshape(ROWS, TOP)
    every = jnp.arange(SLOTS, dtype=jnp.int32)
    first, second = [place[:, c : c + 1] == every[None, :] for c in range(TOP)]
    both = low(first | second)
    return (route, low(first), low(second), both.T), both


def swap_cores(value):
    return lax.ppermute(value, "section", [(0, 1), (1, 0)])


def on_device(
    x_in, cotangent, group_ids, routes, priority,
    gains, w_qkv, w_out, router, shared_gate_up, shared_down, expert_gate_up, expert_down,
):
    section = lax.axis_index("section")
    ctx = lax.axis_index("ctx")
    first = section == 0

    pack = jnp.concatenate(
        [w_qkv[0], w_out[0], gains[0], router[0], jnp.zeros((OWN, SMALL - 2 - EXPERTS), jnp.bfloat16), shared_gate_up[0]],
        axis=1,
    )
    pack = jnp.pad(pack, ((0, 16 - OWN), (0, 0)))

    def mine(value):
        return jnp.where(first, value[0], value[1])

    def other(value):
        return jnp.where(first, value[1], value[0])

    picked = jnp.stack([routes[0, :, 0], priority[0, :, 0]], axis=1)
    passed = swap_cores(other(picked))
    own = mine(picked)
    plans = [jnp.where(first, own, passed), jnp.where(first, passed, own)]
    plans, taken = zip(*[slot_tables(plan[0], plan[1]) for plan in plans])

    group_row = mine(group_ids[:, 0])
    positions = token_positions(group_row)
    cosine, sine = rotation_tables(lax.dynamic_slice_in_dim(positions, ctx * ROWS, ROWS))
    half_start = ctx // 4 * 512
    qlab = lax.dynamic_slice_in_dim(group_row, half_start, 512).reshape(4, ROWS, 1)
    qidx = (half_start + jnp.arange(512, dtype=jnp.int32)).reshape(4, ROWS, 1)
    geometry = (cosine, sine, qidx, qlab, group_row[None, :])

    state = mine(x_in[:, 0])
    (hidden, final), weights, kept = forward(
        pack, shared_down[0], expert_gate_up[0, 0], expert_down[0, 0], state, geometry, plans
    )
    small_t = [weights[layer][2][:, :8].astype(jnp.float32).T for layer in range(2)]
    hidden_grad, hidden_grads, operands_upper = layer_backward(
        1, mine(cotangent[:, 0]), hidden, geometry, plans[1], taken[1], small_t[1], weights[1], kept[1]
    )
    _, input_grads, operands_lower = layer_backward(
        0, low(hidden_grad), state, geometry, plans[0], taken[0], small_t[0], weights[0], kept[0]
    )
    qkv_grad, out_grad, small_grad, gu_grad, sd_grad, egu_grad, ed_grad = weight_grads(operands_lower, operands_upper)

    outputs = jnp.where(first, hidden, final)
    arrived = swap_cores(jnp.where(first, final, hidden))
    outputs = jnp.stack([jnp.where(first, outputs, arrived), jnp.where(first, arrived, outputs)])
    grads = jnp.where(first, input_grads, hidden_grads[::-1])
    return (
        outputs.reshape(1, 2, 1, ROWS, D),
        grads.reshape(1, 2, 1, ROWS, D),
        small_grad[None, :, :2],
        qkv_grad[None],
        out_grad[None],
        small_grad[None, :, 2 : 2 + EXPERTS],
        gu_grad[None],
        sd_grad[None],
        egu_grad[None, None],
        ed_grad[None, None],
    )


def solution(mesh):
    dense = P("section", ("ctx", "fsdp"), None)
    expert = P("section", "ctx", "fsdp", None)
    tokens = P("section", None, "fsdp", "ctx", None)
    rows = P(None, "fsdp", "ctx", None)
    return jax.shard_map(
        on_device,
        mesh=mesh,
        in_specs=(rows, rows, P(None, "fsdp", None), tokens, tokens) + (dense,) * 6 + (expert,) * 2,
        out_specs=(tokens, tokens) + (dense,) * 6 + (expert,) * 2,
        check_vma=False,
    )
```

```python
import functools
import math

import jax
import jax.numpy as jnp
from jax import lax
from jax.experimental import pallas as pl
from jax.experimental.pallas import tpu as pltpu
from jax.sharding import PartitionSpec as P

MESH = pl.DeviceIdType.MESH
ANY = pl.BlockSpec(memory_space=pl.ANY)
VMEM = pl.BlockSpec(memory_space=pltpu.VMEM)
DMA = pltpu.SemaphoreType.DMA

D = 768
FF = 2048
WIDE = 3072
SMALL = 128
PACK = WIDE + 2 * FF + SMALL
OWN = 12
HEADS = 12
HEAD_DIM = 64
TOP = 2
CONT = 8
EXPERTS = 8
SEQ = 1024
ROWS = 128
CAP = 40
PAD_CAP = 48
SLOTS = EXPERTS * PAD_CAP
SCALE = 1.0 / math.sqrt(HEAD_DIM)
EPS = 1e-06
NEG = -1e30


def place_ids():
    section = lax.axis_index("section")
    ctx = lax.axis_index("ctx")
    fsdp = lax.axis_index("fsdp")
    return section, ctx // 4, lax.rem(ctx, 4), fsdp // 2, lax.rem(fsdp, 2)


def ctx_of(half, ring):
    return lax.rem(half + 2, 2) * 4 + lax.rem(ring + 4, 4)


def fsdp_of(ring, half):
    return lax.rem(ring + 4, 4) * 2 + lax.rem(half + 2, 2)


def neighbours():
    section, a, z, y, h = place_ids()
    ctx, fsdp = ctx_of(a, z), fsdp_of(y, h)
    return dict(
        core=(1 - section, ctx, fsdp),
        zp=(section, ctx_of(a, z + 1), fsdp),
        zm=(section, ctx_of(a, z - 1), fsdp),
        zx=(section, ctx_of(a + 1, z), fsdp),
        yp=(section, ctx, fsdp_of(y + 1, h)),
        ym=(section, ctx, fsdp_of(y - 1, h)),
        yx=(section, ctx, fsdp_of(y, h + 1)),
    )


def greet(devices):
    barrier = pltpu.get_barrier_semaphore()
    for device in devices:
        pl.semaphore_signal(barrier, inc=1, device_id=device, device_id_type=MESH)
    pl.semaphore_wait(barrier, len(devices))


def rows_at(ref, block, rows, part=None):
    if part is None:
        return ref.at[pl.ds(pl.multiple_of(block * rows, 16), rows)]
    half = rows // 2
    return ref.at[pl.ds(pl.multiple_of(block * rows + part * half, 16), half)]


class Hop:
    def __init__(self, sources, targets, device, send, recv):
        self.copies = [
            pltpu.make_async_remote_copy(s, t, send.at[i], recv.at[i], device_id=device, device_id_type=MESH)
            for i, (s, t) in enumerate(zip(sources, targets))
        ]

    def start(self):
        for copy in self.copies:
            copy.start()
        return self

    def wait_recv(self):
        for copy in self.copies:
            copy.wait_recv()

    def wait_send(self):
        for copy in self.copies:
            copy.wait_send()


def row_view(rows):
    return lambda whole, block, part: rows_at(whole, block, rows, part)


def shard_view(whole, block, part):
    if part is None:
        return whole.at[:, block]
    return whole.at[4 * part : 4 * part + 4, block]


class Tree:
    def __init__(self, over_ctx, halves, own, whole, view, send, recv, c_send, c_recv, l_sem):
        section, a, z, y, h = place_ids()
        near = neighbours()
        self.halves = halves
        ring, pair = ("z", "zx") if over_ctx else ("y", "yx")
        plus, minus, across = near[ring + "p"], near[ring + "m"], near[pair]

        def views(step, side, part=None):
            block = ctx_of(a + side, z + step) if over_ctx else fsdp_of(y + step, h + side)
            return [v(w, block, part) for w, v in zip(whole, view)]

        def hop(index, sources, targets, device):
            return Hop(sources, targets, device, send.at[index], recv.at[index])

        mine = views(0, 0)
        self.stays = [] if own is None else [pltpu.make_async_copy(o, m, l_sem.at[i]) for i, (o, m) in enumerate(zip(own, mine))]
        own = mine if own is None else own
        self.hops = [
            hop(0, own, mine, plus),
            hop(1, own, mine, minus),
            hop(2, own, mine, across),
            hop(3, views(-1, 0, 0), views(-1, 0, 0), plus),
            hop(4, views(1, 0, 1), views(1, 0, 1), minus),
            hop(5, views(0, 1), views(0, 1), plus),
            hop(6, views(0, 1), views(0, 1), minus),
        ]
        if halves:
            self.hops.append(hop(7, views(-1, 1, 0), views(-1, 1, 0), plus))
            self.hops.append(hop(8, views(1, 1, 1), views(1, 1, 1), minus))
        else:
            self.hops.append(hop(7, views(2, 0), views(2, 0), across))
        places = [(0, 0), (-1, 0), (1, 0), (0, 1), (2, 0), (-1, 1), (1, 1), (2, 1)]
        self.cores = [
            Hop(own if k == 0 else views(*p), views(*p), near["core"], c_send.at[k], c_recv.at[k]) for k, p in enumerate(places)
        ]

    def start_own(self):
        for index in (0, 1, 2):
            self.hops[index].start()
        self.cores[0].start()
        for copy in self.stays:
            copy.start()

    def pass_ring(self):
        for index, later, core in ((0, 3, 1), (1, 4, 2)):
            self.hops[index].wait_recv()
            self.hops[later].start()
            self.cores[core].start()

    def pass_pair(self):
        self.hops[2].wait_recv()
        self.hops[5].start()
        self.hops[6].start()
        self.cores[3].start()

    def pass_far(self):
        if self.halves:
            for index, later, core in ((5, 7, 5), (6, 8, 6)):
                self.hops[index].wait_recv()
                self.hops[later].start()
                self.cores[core].start()
        self.hops[3].wait_recv()
        self.hops[4].wait_recv()
        if not self.halves:
            self.hops[7].start()
        self.cores[4].start()

    def finish(self):
        if self.halves:
            self.hops[7].wait_recv()
            self.hops[8].wait_recv()
            self.cores[7].start()
        else:
            for index, core in ((5, 5), (6, 6), (7, 7)):
                self.hops[index].wait_recv()
                self.cores[core].start()
        for copy in self.stays:
            copy.wait()

    def receive(self):
        for hop in self.cores:
            hop.wait_recv()

    def drain(self):
        for hop in self.hops + self.cores:
            hop.wait_send()


class Shards:
    def __init__(self, pack, packs, sd, whole_sd, send, recv, l_sem):
        section, a, z, y, h = place_ids()
        ctx, fsdp = ctx_of(a, z), fsdp_of(y, h)
        wide = slice(0, WIDE + SMALL)
        rest = slice(WIDE + SMALL, PACK)
        mine = packs.at[pl.ds(pl.multiple_of(fsdp * 16, 16), 16)]
        pieces = [
            (pack.at[:, wide], mine.at[:, wide], fsdp_peers()),
            (pack.at[:, rest], mine.at[:, rest], fsdp_peers()),
            (sd, whole_sd.at[ctx, fsdp], ctx_peers()),
        ]
        self.hops = [
            [Hop([s], [t], device, send.at[k, pl.ds(i, 1)], recv.at[k, pl.ds(i, 1)]) for k, device in enumerate(peers)]
            for i, (s, t, peers) in enumerate(pieces)
        ]
        self.stays = [pltpu.make_async_copy(s, t, l_sem.at[i]) for i, (s, t, _) in enumerate(pieces)]

    def start(self, *pieces):
        for i in pieces:
            for hop in self.hops[i]:
                hop.start()
            self.stays[i].start()

    def wait(self, *pieces):
        for i in pieces:
            for hop in self.hops[i]:
                hop.wait_recv()
            self.stays[i].wait()

    def drain(self):
        for hops in self.hops:
            for hop in hops:
                hop.wait_send()


FSDP_STEPS = [(dy, dh) for dy in (1, 3, 2, 0) for dh in (0, 1) if (dy, dh) != (0, 0)]


def fsdp_peers():
    section, a, z, y, h = place_ids()
    ctx = ctx_of(a, z)
    return [(section, ctx, fsdp_of(y + dy, h + dh)) for dy, dh in FSDP_STEPS]


def close_rows(sel, packs, target, start):
    width = target.shape[1]
    step = min(width, 512)

    @pl.loop(0, width // step)
    def _(j):
        off = pl.multiple_of(j * step, 128)
        block = packs[:, pl.ds(pl.multiple_of(start + off, 128), step)]
        target[:, pl.ds(off, step)] = low(dot(sel[...], block))


def close_table(rows_from, rows_to):
    cols, rows = jnp.arange(rows_from), jnp.arange(rows_to)
    return low((rows[:, None] // OWN == cols[None, :] // 16) & (rows[:, None] % OWN == cols[None, :] % 16))


LEFT = (("na", (D, 128)), ("at", (D, 128)), ("nf", (D, 128)), ("sh", (FF, 128)), ("rc", (D, SLOTS)), ("hd", (FF, SLOTS)))
RIGHT = (
    ("qkv", (128, 3 * D)), ("pr", (128, D)), ("gu", (128, 2 * FF)), ("sd", (128, D)), ("j", (SLOTS, 2 * FF)),
    ("er", (EXPERTS, PAD_CAP, D)), ("small", (D, SMALL)),
)
OPERANDS = LEFT + RIGHT
N_OPS = len(OPERANDS)


def operand_type(name):
    return jnp.float32 if name == "small" else jnp.bfloat16


ATTENTION = (("wide", "na", "qkv", 96, 0, 3 * D, D), ("wide", "at", "pr", 96, 3 * D, D, D))
SHARED = (("gu", "nf", "gu", 96, 0, 2 * FF, 1024), ("sd", "sh", "sd", 256, 0, D, D))
EXPERT = (("egu", "rc", "j", 96, 0, 2 * FF, 1024), ("ed", "hd", "er", 256, 0, D, D))


def grads_kernel(*refs):
    lower, upper = refs[:N_OPS], refs[N_OPS : 2 * N_OPS]
    sel_t = refs[2 * N_OPS]
    out_qkv, out_out, out_small, out_gu, out_sd, out_egu, out_ed = refs[2 * N_OPS + 1 : 2 * N_OPS + 8]
    rest = refs[2 * N_OPS + 8 :]
    held = rest[:N_OPS]
    (b_wide, b_gu, b_small, b_sd, c_gu, c_sd, packs, in_pack, in_sd,
     o_local, w_send, w_recv, r_send, r_recv, e_send, e_recv, s_send, s_recv) = rest[N_OPS:]
    names = [n for n, _ in OPERANDS]
    ops = dict(zip(names, held))
    section, a, z, y, h = place_ids()
    ctx, fsdp = ctx_of(a, z), fsdp_of(y, h)
    near = neighbours()

    def bring(source, i, which):
        n, shape = OPERANDS[i]
        if i < len(LEFT):
            target = held[i].at[:, pl.ds(which * shape[1], shape[1])]
        elif n in ("er", "small"):
            target = held[i].at[which]
        else:
            target = held[i].at[pl.ds(which * shape[0], shape[0])]
        return pltpu.make_async_copy(source[i].at[which], target, o_local.at[i, which])

    order = [names.index(n) for n in ("na", "qkv", "at", "pr", "small", "nf", "gu", "sh", "sd", "rc", "j", "hd", "er")]
    for layer, source in enumerate((lower, upper)):

        @pl.when(section == layer)
        def _(source=source):
            for i in order:
                for which in range(2):
                    bring(source, i, which).start()

    greet([near["zp"], near["zm"], near["zx"]] + fsdp_peers())

    def ready(*wanted):
        for n in wanted:
            for which in range(2):
                bring(lower, names.index(n), which).wait()

    kinds = dict(wide=b_wide, gu=b_gu, small=b_small, sd=b_sd, egu=c_gu, ed=c_sd)
    buffers = {
        ATTENTION: ((b_wide, 96), (b_small, 96)),
        SHARED: ((b_gu, 96), (b_sd, 256)),
        EXPERT: ((c_gu, 96), (c_sd, 256)),
    }
    semaphores = {ATTENTION: (w_send, w_recv), SHARED: (r_send, r_recv), EXPERT: (e_send, e_recv)}

    def combine(pieces, block, slot, adds=(), part=None, target=None):
        for kind, left, right, rows, first, width, step in pieces:
            n = rows if part is None else rows // 2
            off = 0 if part is None else part * n
            lhs_rows = pl.ds(pl.multiple_of(block * rows + off, 16), n)

            @pl.loop(0, width // step)
            def _(j, kind=kind, left=left, right=right, first=first, n=n, off=off, lhs_rows=lhs_rows, step=step):
                at = pl.ds(pl.multiple_of(j * step, 256), step)
                to = pl.ds(pl.multiple_of(first + j * step, 256), step)
                if right == "er":
                    right_part = ops[right][:, :, :, at].reshape(2 * SLOTS, step)
                else:
                    right_part = ops[right][:, at]
                total = dot(ops[left][lhs_rows, :], right_part)
                for other in adds:
                    total += kinds[kind][other, off : off + n, to].astype(jnp.float32)
                if target is None:
                    kinds[kind][slot, off : off + n, to] = low(total)
                else:
                    target[kind][off : off + n, to] = total

        if pieces is ATTENTION:
            n = 96 if part is None else 48
            off = 0 if part is None else part * n
            at = pl.ds(pl.multiple_of(block * 96 + off, 16), n)
            total = ops["small"][0, at, :] + ops["small"][1, at, :]
            for other in adds:
                total += b_small[other, off : off + n, :].astype(jnp.float32)
            b_small[slot, off : off + n, :] = low(total)

    hops = {}

    def send(pieces, index, slot, to_slot, device, part=None):
        def views(which):
            return [rows_at(b.at[which], 0, r, part) for b, r in buffers[pieces]]

        sems = semaphores[pieces]
        hops[pieces, index] = Hop(views(slot), views(to_slot), near[device], sems[0].at[index], sems[1].at[index]).start()

    def arrived(pieces, *indices):
        for index in indices:
            hops[pieces, index].wait_recv()

    def sent(pieces, *indices):
        for index in indices:
            hops[pieces, index].wait_send()

    def d_block(dz, da):
        return ctx_of(a + da, z + dz)

    def e_block(dy, dh):
        return fsdp_of(y + dy, h + dh)

    def spread(pieces):
        combine(pieces, d_block(2, 1), 0)
        send(pieces, 0, 0, 1, "zx")
        combine(pieces, d_block(-1, 1), 2)
        send(pieces, 1, 2, 5, "zm")
        combine(pieces, d_block(1, 1), 3)
        send(pieces, 2, 3, 6, "zp")

    def halves(pieces):
        arrived(pieces, 0)
        combine(pieces, d_block(2, 0), 1, (1,))
        send(pieces, 3, 1, 4, "zm", 0)
        send(pieces, 4, 1, 4, "zp", 1)

    def next_ones(pieces):
        sent(pieces, 0)
        combine(pieces, d_block(-1, 0), 0, (), 1)
        arrived(pieces, 3)
        combine(pieces, d_block(-1, 0), 0, (4,), 0)
        send(pieces, 5, 0, 7, "zm")
        sent(pieces, 3, 4)
        combine(pieces, d_block(1, 0), 1, (), 0)
        arrived(pieces, 4)
        combine(pieces, d_block(1, 0), 1, (4,), 1)
        send(pieces, 6, 1, 8, "zp")

    def pair(pieces):
        arrived(pieces, 1, 2)
        combine(pieces, d_block(0, 1), 5, (5, 6))
        send(pieces, 7, 5, 9, "zx")

    def own(pieces):
        arrived(pieces, 5, 6, 7)
        combine(pieces, ctx, 7, (7, 8, 9))

    def open_rows(kind, start, width):
        step = min(width, 1024)

        @pl.loop(0, width // step)
        def _(j):
            off = pl.multiple_of(j * step, 128)
            block = kinds[kind][7, :, pl.ds(off, step)]
            packs[:, pl.ds(pl.multiple_of(start + off, 128), step)] = low(dot(sel_t[...], block))

    last = [[], [], []]
    split_at = WIDE + SMALL

    def to_owners(which):
        for k, device in enumerate(fsdp_peers()):
            dy, dh = FSDP_STEPS[k]
            block = e_block(dy, dh)
            rows = packs.at[pl.ds(pl.multiple_of(block * 16, 16), 16)]
            source, target = (
                (rows.at[:, :split_at], in_pack.at[k, :, :split_at]),
                (rows.at[:, split_at:], in_pack.at[k, :, split_at:]),
                (rows_at(b_sd.at[7], block, 32), in_sd.at[k]),
            )[which]
            last[which].append(
                Hop([source], [target], device, s_send.at[k, pl.ds(which, 1)], s_recv.at[k, pl.ds(which, 1)]).start()
            )

    def total_of(which, start, width, out):
        step = min(width, 256)

        @pl.loop(0, width // step)
        def _(j):
            at = pl.ds(pl.multiple_of(start + j * step, 128), step)
            total = packs[pl.ds(pl.multiple_of(fsdp * 16, 16), 16), at].astype(jnp.float32)
            for k in range(7):
                total += in_pack[k, :, at].astype(jnp.float32)
            out[:, pl.ds(pl.multiple_of(j * step, 128), step)] = total[:OWN]

    ready("na", "qkv", "at", "pr", "small")
    spread(ATTENTION)
    ready("nf", "gu", "sh", "sd")
    spread(SHARED)
    ready("rc", "j", "hd", "er")
    combine(EXPERT, e_block(2, 1), 0)
    send(EXPERT, 0, 0, 4, "ym", 0)
    send(EXPERT, 1, 0, 4, "yp", 1)
    halves(ATTENTION)
    combine(EXPERT, e_block(2, 0), 1)
    send(EXPERT, 2, 1, 5, "ym", 0)
    send(EXPERT, 3, 1, 5, "yp", 1)
    combine(EXPERT, e_block(-1, 1), 2, (), 1)
    combine(EXPERT, e_block(1, 1), 3, (), 0)
    arrived(EXPERT, 0)
    combine(EXPERT, e_block(-1, 1), 2, (4,), 0)
    send(EXPERT, 4, 2, 6, "ym")
    arrived(EXPERT, 1)
    combine(EXPERT, e_block(1, 1), 3, (4,), 1)
    send(EXPERT, 5, 3, 7, "yp")
    pair(ATTENTION)
    halves(SHARED)
    next_ones(ATTENTION)
    pair(SHARED)
    sent(EXPERT, 0, 1)
    combine(EXPERT, e_block(-1, 0), 0, (), 1)
    arrived(EXPERT, 2)
    combine(EXPERT, e_block(-1, 0), 0, (5,), 0)
    send(EXPERT, 6, 0, 8, "ym")
    sent(EXPERT, 2, 3)
    combine(EXPERT, e_block(1, 0), 1, (), 0)
    arrived(EXPERT, 3)
    combine(EXPERT, e_block(1, 0), 1, (5,), 1)
    send(EXPERT, 7, 1, 9, "yp")
    next_ones(SHARED)
    arrived(EXPERT, 4, 5)
    combine(EXPERT, e_block(0, 1), 6, (6, 7))
    send(EXPERT, 8, 6, 10, "yx")
    own(ATTENTION)
    open_rows("wide", 0, WIDE)
    open_rows("small", WIDE, SMALL)
    to_owners(0)
    own(SHARED)
    open_rows("gu", split_at, 2 * FF)
    to_owners(1)
    to_owners(2)
    for hop in last[0]:
        hop.wait_recv()
    total_of(0, 0, 3 * D, out_qkv)
    total_of(0, 3 * D, D, out_out)
    total_of(0, WIDE, SMALL, out_small)
    arrived(EXPERT, 6, 7, 8)
    combine(EXPERT, fsdp, 0, (8, 9, 10), None, dict(egu=out_egu, ed=out_ed))
    for hop in last[1] + last[2]:
        hop.wait_recv()
    total_of(1, split_at, 2 * FF, out_gu)
    total = b_sd[7, pl.ds(pl.multiple_of(fsdp * 32, 16), 32), :].astype(jnp.float32)
    for k in range(7):
        total += in_sd[k].astype(jnp.float32)
    out_sd[...] = total
    for pieces in (ATTENTION, SHARED):
        sent(pieces, 1, 2, 5, 6, 7)
    sent(EXPERT, 4, 5, 6, 7, 8)
    for hop in last[0] + last[1] + last[2]:
        hop.wait_send()


def weight_grads(lower, upper):
    bf, f32 = jnp.bfloat16, jnp.float32
    held = [pltpu.VMEM((shape[0], 2 * shape[1]), bf) for _, shape in LEFT]
    for name, shape in RIGHT:
        whole = (2,) + shape if name in ("er", "small") else (2 * shape[0], shape[1])
        held.append(pltpu.VMEM(whole, operand_type(name)))
    shapes = [(OWN, 3 * D), (OWN, D), (OWN, SMALL), (OWN, 2 * FF), (32, D), (96, 2 * FF), (256, D)]
    return pl.pallas_call(
        grads_kernel,
        out_shape=[jax.ShapeDtypeStruct(shape, f32) for shape in shapes],
        in_specs=[ANY] * (2 * N_OPS) + [VMEM],
        out_specs=[VMEM] * len(shapes),
        scratch_shapes=held + [
            pltpu.VMEM((10, 96, WIDE), bf),
            pltpu.VMEM((10, 96, 2 * FF), bf),
            pltpu.VMEM((10, 96, SMALL), bf),
            pltpu.VMEM((10, 256, D), bf),
            pltpu.VMEM((11, 96, 2 * FF), bf),
            pltpu.VMEM((11, 256, D), bf),
            pltpu.VMEM((128, PACK), bf),
            pltpu.VMEM((7, 16, PACK), bf),
            pltpu.VMEM((7, 32, D), bf),
            DMA((N_OPS, 2)),
            DMA((8, 2)), DMA((8, 2)), DMA((8, 2)), DMA((8, 2)),
            DMA((9, 2)), DMA((9, 2)),
            DMA((7, 3)), DMA((7, 3)),
        ],
        compiler_params=pltpu.CompilerParams(collective_id=5, has_side_effects=True, vmem_limit_bytes=62 << 20),
        name="weight_grads",
    )(*lower, *upper, close_table(128, 96).T)


def split(values):
    high = low(values)
    return high, low(values - high.astype(jnp.float32))


def rms_parts(values):
    scale = lax.rsqrt(jnp.mean(values * values, axis=-1, keepdims=True) + EPS)
    return scale, values * scale


def rms_back(grad, gain, scale, unit):
    inner = grad * gain
    grad_values = scale * (inner - unit * jnp.mean(inner * unit, axis=-1, keepdims=True))
    return grad_values, jnp.sum(grad * unit, axis=0, keepdims=True)


def dot(left, right):
    return jnp.dot(left, right, preferred_element_type=jnp.float32)


def dot_t(left, right):
    return lax.dot_general(left, right, (((1,), (1,)), ((), ())), preferred_element_type=jnp.float32)


def t_dot(left, right):
    return lax.dot_general(left, right, (((0,), (0,)), ((), ())), preferred_element_type=jnp.float32)


def low(values):
    return values.astype(jnp.bfloat16)


def rotate(values, cosine, sine):
    half = HEAD_DIM // 2
    lower = lax.broadcasted_iota(jnp.int32, (values.shape[0], 128), 1) % HEAD_DIM < half
    parts = []
    for start in range(0, values.shape[1], 128):
        span = slice(start, start + 128)
        part = values[:, span]
        other = jnp.where(lower, pltpu.roll(part, 128 - half, 1), pltpu.roll(part, half, 1))
        parts.append(part * cosine[:, span] + other * sine[:, span])
    return jnp.concatenate(parts, axis=1)


def visible_keys(qidx, qlab, klab):
    kidx = lax.broadcasted_iota(jnp.int32, (qidx.shape[0], klab.shape[1]), 1)
    return (kidx <= qidx) & ((klab == 0) | (klab == qlab))


def pair_gates(logits, route):
    lane = lax.broadcasted_iota(jnp.int32, logits.shape, 1)
    picks = [lane == route[:, c : c + 1] + 2 for c in range(TOP)]
    first, second = [jnp.sum(jnp.where(p, logits, 0.0), axis=1, keepdims=True) for p in picks]
    top = jnp.maximum(first, second)
    first, second = jnp.exp(first - top), jnp.exp(second - top)
    total = first + second
    return picks, [first / total, second / total]


class Exchange:
    def __init__(self, source, target, send, recv, everyone, block_of=None):
        section, a, z, y, h = place_ids()
        fsdp = fsdp_of(y, h)
        offsets = [(1, 0), (1, 1), (1, 3), (1, 2)] if everyone else []
        self.copies = []
        for k, (da, dz) in enumerate(offsets + [(0, 1), (0, 3), (0, 2)]):
            c, zz = ctx_of(a + da, z + dz), lax.rem(z + dz, 4)
            block = zz if block_of == "ring" or not everyone else c
            to = ctx_of(a, z) if everyone else z
            self.copies.append(
                pltpu.make_async_remote_copy(
                    source.at[block], target.at[to], send.at[k], recv.at[k], device_id=(section, c, fsdp), device_id_type=MESH
                )
            )

    def start(self):
        for copy in self.copies:
            copy.start()

    def wait_recv(self):
        for copy in self.copies:
            copy.wait_recv()

    def wait_send(self):
        for copy in self.copies:
            copy.wait_send()


CTX_STEPS = [(1, 0), (0, 1), (0, 3), (0, 2), (1, 1), (1, 3), (1, 2)]


def ctx_peers():
    section, a, z, y, h = place_ids()
    fsdp = fsdp_of(y, h)
    return [(section, ctx_of(a + da, z + dz), fsdp) for da, dz in CTX_STEPS]


def forward_kernel(
    pack, i_sd, i_egu, i_ed, sel,
    state, cosine, sine, qidx, qlab, klab, route, first_table, second_table, taken_t,
    out_lower, out_upper,
    l_wide, l_gu, l_small, l_sd, l_egu, l_ed, u_wide, u_gu, u_small, u_sd, u_egu, u_ed,
    *rest,
):
    kept = (rest[:9], rest[9:18])
    (wide, gu, small, sd, egu, ed, w_sem,
     packs, own_wide, own_small, own_gu, g_sd, g_egu, g_ed, g_stay, sh_send, sh_recv,
     w_send, w_recv, g_send, g_recv, d_send, d_recv, e_send, e_recv,
     wc_send, wc_recv, gc_send, gc_recv, dc_send, dc_recv, ec_send, ec_recv,
     kv_pack, q_pack, kv_all, q_all, o_pack, o_in, lse, att, res, sj, sh, sent, rc, ej, eh, result, ret, k_sem,
     x_send, x_recv) = rest[18:]
    section, a, z, y, h = place_ids()
    ctx = ctx_of(a, z)
    wholes = ((l_wide, l_gu, l_small, l_sd, l_egu, l_ed), (u_wide, u_gu, u_small, u_sd, u_egu, u_ed))
    shards_in = [
        pltpu.make_async_copy(s, t, g_stay.at[4, i]) for i, (s, t) in enumerate(((i_sd, g_sd), (i_egu, g_egu), (i_ed, g_ed)))
    ]
    for copy in shards_in:
        copy.start()
    greet([neighbours()["core"]] + ctx_peers() + fsdp_peers())
    for copy in shards_in:
        copy.wait()

    trees, firsts = [], []
    for layer in range(2):
        t_wide, t_gu, t_small, t_sd, t_egu, t_ed = wholes[layer]
        firsts.append(Shards(pack, packs, g_sd, t_sd, sh_send, sh_recv, g_stay.at[0]))
        trees.append(
            dict(
                w=Tree(True, False, [own_wide, own_small], [t_wide, t_small], [row_view(96)] * 2,
                       w_send, w_recv, wc_send.at[layer], wc_recv.at[layer], g_stay.at[1]),
                g=Tree(True, True, [own_gu], [t_gu], [row_view(96)],
                       g_send, g_recv, gc_send.at[layer], gc_recv.at[layer], g_stay.at[2]),
                d=Tree(False, True, None, [t_sd], [shard_view],
                       d_send, d_recv, dc_send.at[layer], dc_recv.at[layer], None),
                e=Tree(False, True, [g_egu, g_ed], [t_egu, t_ed], [row_view(96), row_view(256)],
                       e_send, e_recv, ec_send.at[layer], ec_recv.at[layer], g_stay.at[3]),
            )
        )

    def drive(layer, *steps):
        @pl.when(section == layer)
        def _():
            for step in steps:
                step()

    def close_wide():
        firsts[0].wait(0)
        close_rows(sel, packs, own_wide, 0)
        close_rows(sel, packs, own_small, WIDE)

    def close_gu():
        firsts[0].wait(1)
        close_rows(sel, packs, own_gu, WIDE + SMALL)

    def arrived(layer, group):
        drive(layer, trees[layer][group].finish)

        @pl.when(section != layer)
        def _():
            trees[layer][group].receive()

    def load(layer, *which):
        for i in which:
            target = (wide.at[layer], gu, small.at[layer], sd, egu, ed)[i]
            pltpu.make_async_copy(wholes[layer][i], target, w_sem.at[layer, i]).start()

    def loaded(layer, *which):
        for i in which:
            target = (wide.at[layer], gu, small.at[layer], sd, egu, ed)[i]
            pltpu.make_async_copy(wholes[layer][i], target, w_sem.at[layer, i]).wait()

    def first(layer, *pieces):
        return lambda: firsts[layer].start(*pieces)

    def down(layer):
        def step():
            firsts[layer].wait(2)
            trees[layer]["d"].start_own()

        return step

    lower, upper = trees
    hooks = {
        (0, "start"): lambda: (
            drive(0, first(0, 0, 2), close_wide, lower["w"].start_own, first(0, 1), lower["e"].start_own,
                  lower["w"].pass_ring, lower["w"].pass_pair, close_gu, lower["g"].start_own, lower["w"].pass_far),
            arrived(0, "w"), load(0, 0, 2),
        ),
        (0, "keys"): lambda: (drive(0, lower["e"].pass_ring, lower["e"].pass_pair), drive(1, first(1, 0, 1, 2))),
        (0, "queries"): lambda: drive(0, lower["g"].pass_pair),
        (0, "block1"): lambda: drive(0, down(0)),
        (0, "attended"): lambda: (
            drive(0, lower["g"].pass_ring, lower["e"].pass_far), drive(1, close_wide, upper["w"].start_own),
        ),
        (0, "sent"): lambda: (
            drive(0, lower["g"].pass_far, lower["d"].pass_ring, lower["d"].pass_pair),
            drive(1, upper["w"].pass_ring, upper["w"].pass_pair, close_gu),
            arrived(0, "e"), load(0, 4, 5),
        ),
        (0, "expert0"): lambda: drive(1, upper["e"].start_own),
        (0, "expert1"): lambda: drive(0, lower["d"].pass_far),
        (0, "expert2"): lambda: drive(1, upper["w"].pass_far),
        (0, "returned"): lambda: (
            arrived(0, "g"), load(0, 1), drive(1, upper["g"].start_own, upper["e"].pass_ring, upper["e"].pass_pair),
            arrived(0, "d"), load(0, 3),
        ),
        (1, "start"): lambda: (arrived(1, "w"), load(1, 0, 2)),
        (1, "queries"): lambda: drive(1, upper["g"].pass_pair),
        (1, "block1"): lambda: drive(1, down(1), upper["e"].pass_far),
        (1, "attended"): lambda: drive(1, upper["g"].pass_ring),
        (1, "sent"): lambda: (
            drive(1, upper["g"].pass_far, upper["d"].pass_ring, upper["d"].pass_pair), arrived(1, "e"), load(1, 4, 5),
        ),
        (1, "expert1"): lambda: drive(1, upper["d"].pass_far),
        (1, "returned"): lambda: (arrived(1, "g"), load(1, 1), arrived(1, "d"), load(1, 3)),
    }

    def one_layer(layer, x, out):
        def hook(name):
            if (layer, name) in hooks:
                hooks[layer, name]()

        k_q, k_kv, k_lse, k_att, k_res, k_sj, k_rc, k_ej, k_ret = kept[layer]
        saves = []

        def save(source, target):
            copy = pltpu.make_async_copy(source, target, k_sem.at[len(saves)])
            copy.start()
            saves.append(copy)

        def exchange(index, source, target, everyone, block_of=None):
            sems = x_send.at[layer, index], x_recv.at[layer, index]
            return Exchange(source, target, *sems, everyone, block_of)

        scale, unit = rms_parts(x)
        hook("start")
        loaded(layer, 0, 2)
        wide_l, small_l = wide.at[layer], small.at[layer]
        gains = jnp.transpose(small_l[...].astype(jnp.float32))
        normed = low(unit * gains[0:1, :])
        keys = low(rotate(dot(normed, wide_l[:, D : 2 * D]), cosine[...], sine[...]))
        values = low(dot(normed, wide_l[:, 2 * D : 3 * D]))
        for g in range(4):
            kv_pack[g, :, 0:192] = keys[:, 192 * g : 192 * g + 192]
            kv_pack[g, :, 192:384] = values[:, 192 * g : 192 * g + 192]
        ex_kv = exchange(0, kv_pack, kv_all, True, "ring")
        ex_kv.start()
        hook("keys")
        queries = low(rotate(dot(normed, wide_l[:, 0:D]), cosine[...], sine[...]))
        for g in range(4):
            q_pack[g] = queries[:, 192 * g : 192 * g + 192]
        ex_q = exchange(1, q_pack, q_all, False)
        ex_q.start()
        kv_all[ctx] = kv_pack[z]
        q_all[z] = q_pack[z]
        hook("queries")
        ex_q.wait_recv()
        ex_kv.wait_recv()
        save(kv_all, k_kv)
        save(q_all, k_q)

        def attend(d):
            block = lax.rem(z + d + 1, 4)
            seen = visible_keys(qidx[block], qlab[block], klab[...])
            for head in range(3):
                span = slice(64 * head, 64 * head + 64)
                vspan = slice(192 + 64 * head, 256 + 64 * head)
                k = kv_all[:, :, span].reshape(SEQ, HEAD_DIM)
                v = kv_all[:, :, vspan].reshape(SEQ, HEAD_DIM)
                scores = jnp.where(seen, dot_t(q_all[block, :, span], k) * SCALE, NEG)
                top = jnp.max(scores, axis=-1, keepdims=True)
                weights = jnp.exp(scores - top)
                total = jnp.sum(weights, axis=-1, keepdims=True)
                o_pack[block, :, span] = low(dot(low(weights / total), v))
                lse[block, :, head : head + 1] = top + jnp.log(total)

        for d in range(4):
            pl.loop(d, d + 1)(attend)
            hook(f"block{d}")

        ex_o = exchange(2, o_pack, o_in, False)
        ex_o.start()
        save(lse, k_lse)
        o_in[z] = o_pack[z]
        hook("attended")
        ex_o.wait_recv()
        for g in range(4):
            att[:, 192 * g : 192 * g + 192] = o_in[g]
        save(att, k_att)
        res[...] = x + dot(att[...], wide_l[:, 3 * D :])
        save(res, k_res)
        scale, unit = rms_parts(res[...])
        normed = low(unit * gains[1:2, :])
        sent[...] = low(dot(taken_t[layer], normed)).reshape(EXPERTS, PAD_CAP, D)
        ex_s = exchange(3, sent, rc, True)
        ex_s.start()
        rc[ctx] = sent[ctx]
        _, gates = pair_gates(dot(normed, small_l[...]), route[layer])
        mix = first_table[layer].astype(jnp.float32) * gates[0] + second_table[layer].astype(jnp.float32) * gates[1]
        hook("sent")
        ex_s.wait_recv()
        save(rc, k_rc)
        loaded(layer, 4)

        def expert_part(j):
            at = pl.ds(pl.multiple_of(j * 256, 256), 256)
            up_at = pl.ds(pl.multiple_of(FF + j * 256, 256), 256)
            gate, up = dot(rc[...].reshape(SLOTS, D), egu[:, at]), dot(rc[...].reshape(SLOTS, D), egu[:, up_at])
            ej[:, at] = gate
            ej[:, up_at] = up
            eh[:, at] = low(gate * jax.nn.sigmoid(gate) * up)

        for d in range(4):
            pl.loop(2 * d, 2 * d + 2)(expert_part)
            hook(f"expert{d}")

        save(ej, k_ej)
        loaded(layer, 5)
        for j in range(D // 256):
            span = slice(256 * j, 256 * j + 256)
            result[:, :, span] = low(dot(eh[...], ed[:, span])).reshape(EXPERTS, PAD_CAP, 256)
        ex_r = exchange(4, result, ret, True)
        for copy in saves[:2]:
            copy.wait()
        ex_r.start()
        ret[ctx] = result[ctx]
        hook("returned")
        loaded(layer, 1)

        def shared_part(j):
            at = pl.ds(pl.multiple_of(j * 256, 256), 256)
            up_at = pl.ds(pl.multiple_of(FF + j * 256, 256), 256)
            gate, up = dot(normed, gu[:, at]), dot(normed, gu[:, up_at])
            sj[:, at] = gate
            sj[:, up_at] = up
            sh[:, at] = low(gate * jax.nn.sigmoid(gate) * up)

        pl.loop(0, FF // 256)(shared_part)

        save(sj, k_sj)
        loaded(layer, 3)
        shared_out = dot(sh[...], sd[...].reshape(FF, D))
        ex_r.wait_recv()
        save(ret, k_ret)
        high, rest_of = split(mix)
        returned = ret[...].reshape(SLOTS, D)
        mixed = dot(high, returned) + dot(rest_of, returned)
        out[...] = low(res[...] + shared_out + mixed)
        for ex in (ex_kv, ex_q, ex_o, ex_s, ex_r):
            ex.wait_send()
        for copy in saves[2:]:
            copy.wait()

    one_layer(0, state[...].astype(jnp.float32), out_lower)
    one_layer(1, out_lower[...].astype(jnp.float32), out_upper)
    for layer in range(2):
        drive(layer, firsts[layer].drain, *[tree.drain for tree in trees[layer].values()])


def weight_scratch():
    bf = jnp.bfloat16
    return [
        pltpu.VMEM((D, WIDE), bf), pltpu.VMEM((D, 2 * FF), bf), pltpu.VMEM((D, SMALL), bf),
        pltpu.VMEM((8, 8, 32, D), bf), pltpu.VMEM((D, 2 * FF), bf), pltpu.VMEM((FF, D), bf), DMA((6,)),
    ]


KEPT = (
    ((4, ROWS, 192), jnp.bfloat16), ((8, ROWS, 384), jnp.bfloat16), ((4, ROWS, 128), jnp.float32), ((ROWS, D), jnp.bfloat16),
    ((ROWS, D), jnp.float32), ((ROWS, 2 * FF), jnp.float32), ((EXPERTS, PAD_CAP, D), jnp.bfloat16),
    ((SLOTS, 2 * FF), jnp.float32), ((EXPERTS, PAD_CAP, D), jnp.bfloat16),
)


WEIGHTS = ((D, WIDE), (D, 2 * FF), (D, SMALL), (8, 8, 32, D), (D, 2 * FF), (FF, D))


def forward(pack, sd, egu, ed, state, geometry, plans):
    bf, f32 = jnp.bfloat16, jnp.float32
    slots = pltpu.VMEM((EXPERTS, PAD_CAP, D), bf)
    tables = [jnp.stack(pair) for pair in zip(*plans)]
    outs = pl.pallas_call(
        forward_kernel,
        out_shape=[jax.ShapeDtypeStruct((ROWS, D), bf)] * 2
        + [jax.ShapeDtypeStruct(s, bf) for s in WEIGHTS] * 2
        + [jax.ShapeDtypeStruct(s, t) for s, t in KEPT] * 2,
        in_specs=[ANY] * 4 + [VMEM] * 11,
        out_specs=[VMEM] * 2 + [ANY] * (2 * len(WEIGHTS) + 2 * len(KEPT)),
        scratch_shapes=[
            pltpu.VMEM((2, D, WIDE), bf), pltpu.VMEM((D, 2 * FF), bf), pltpu.VMEM((2, D, SMALL), bf),
            pltpu.VMEM((8, 8, 32, D), bf), pltpu.VMEM((D, 2 * FF), bf), pltpu.VMEM((FF, D), bf), DMA((2, 6)),
            pltpu.VMEM((128, PACK), bf), pltpu.VMEM((96, WIDE), bf), pltpu.VMEM((96, SMALL), bf),
            pltpu.VMEM((96, 2 * FF), bf), pltpu.VMEM((32, D), bf), pltpu.VMEM((96, 2 * FF), bf), pltpu.VMEM((256, D), bf),
            DMA((5, 3)), DMA((7, 3)), DMA((7, 3)),
        ]
        + [DMA((9, 2))] * 8
        + [DMA((2, 8, 2))] * 8
        + [
            pltpu.VMEM((4, ROWS, 384), bf), pltpu.VMEM((4, ROWS, 192), bf),
            pltpu.VMEM((8, ROWS, 384), bf), pltpu.VMEM((4, ROWS, 192), bf),
            pltpu.VMEM((4, ROWS, 192), bf), pltpu.VMEM((4, ROWS, 192), bf),
            pltpu.VMEM((4, ROWS, 128), f32), pltpu.VMEM((ROWS, D), bf), pltpu.VMEM((ROWS, D), f32),
            pltpu.VMEM((ROWS, 2 * FF), f32), pltpu.VMEM((ROWS, FF), bf),
            slots, slots, pltpu.VMEM((SLOTS, 2 * FF), f32), pltpu.VMEM((SLOTS, FF), bf), slots, slots, DMA((len(KEPT),)),
            DMA((2, 5, 7)), DMA((2, 5, 7)),
        ],
        compiler_params=pltpu.CompilerParams(collective_id=1, has_side_effects=True, vmem_limit_bytes=60 << 20),
        name="forward",
    )(pack, sd, egu, ed, close_table(128, 96), state, *geometry, *tables)
    weights, kept = outs[2 : 2 + 2 * len(WEIGHTS)], outs[2 + 2 * len(WEIGHTS) :]
    return outs[:2], (weights[: len(WEIGHTS)], weights[len(WEIGHTS) :]), (kept[: len(KEPT)], kept[len(KEPT) :])


def backward_kernel(
    layer,
    grad, state, cosine, sine, qidx, qlab, klab, route, first_table, second_table, taken, small_t,
    g_wide, g_gu, g_small, g_sd, g_egu, g_ed,
    k_q, k_kv, k_lse, k_att, k_res, k_sj, k_rc, k_ej, k_ret,
    out, out_both,
    p_na, p_at, p_nf, p_sh, p_rc, p_hd, p_qkv, p_pr, p_gu, p_sd, p_j, p_er, p_small,
    wide, gu, small, sd, egu, ed, w_sem,
    q_all, kv_all, lse, att, res, sj, rc, ej, ret, i_sem,
    t_na, t_at, t_nf, t_sh, t_rc, t_hd, m_qkv, m_pr, m_gu, m_sd, m_j, grad_small, p_sem, p_send, p_recv,
    sent, er, back, slots, o_pack, o_in, dq_pack, dq_in, dkv_pack, dkv_in, dkv_sum, normed_grad, sh, eh,
    s_send, s_recv, r_send, r_recv, o_send, o_recv, q_send, q_recv, kv_send, kv_recv,
):
    section, a, z, y, h = place_ids()
    ctx = ctx_of(a, z)
    loads = [
        pltpu.make_async_copy(s, t, w_sem.at[i])
        for i, (s, t) in enumerate(((g_wide, wide), (g_gu, gu), (g_small, small), (g_sd, sd), (g_egu, egu), (g_ed, ed)))
    ]
    reads = [
        pltpu.make_async_copy(s, t, i_sem.at[i])
        for i, (s, t) in enumerate(zip((k_q, k_kv, k_lse, k_att, k_res, k_sj, k_rc, k_ej, k_ret), (q_all, kv_all, lse, att, res, sj, rc, ej, ret)))
    ]
    loads[2].start()
    reads[4].start()
    loads[3].start()
    reads[5].start()
    loads[1].start()
    reads[8].start()
    loads[5].start()
    reads[7].start()
    loads[4].start()
    for i in (6, 3, 0, 1, 2):
        reads[i].start()
    loads[0].start()
    near = neighbours()
    greet([near["core"]] + ctx_peers())
    saves = []

    def save(source, target):
        i = len(saves)
        here = pltpu.make_async_copy(source, target.at[0], p_sem.at[i])
        away = pltpu.make_async_remote_copy(
            source, target.at[1], p_send.at[i], p_recv.at[i], device_id=near["core"], device_id_type=MESH
        )
        saves.append((here, away))

        @pl.when(section == layer)
        def _():
            here.start()

        @pl.when(section != layer)
        def _():
            away.start()

    grad_out = grad[...].astype(jnp.float32)
    m_sd[...] = low(grad_out)
    save(m_sd, p_sd)
    loads[2].wait()
    reads[4].wait()
    scale_ffn, unit_ffn = rms_parts(res[...])
    normed = low(unit_ffn * small_t[1:2, :])
    picks, gates = pair_gates(dot(normed, small[...]), route[...])
    first, second = first_table[...].astype(jnp.float32), second_table[...].astype(jnp.float32)
    mix_high, mix_rest = split(first * gates[0] + second * gates[1])
    out_high, out_rest = split(grad_out)
    slot_grads = t_dot(mix_high, out_high) + t_dot(mix_rest, out_high) + t_dot(mix_high, out_rest)
    sent[...] = low(slot_grads).reshape(EXPERTS, PAD_CAP, D)
    ex_s = Exchange(sent, er, s_send, s_recv, True)
    ex_s.start()
    er[ctx] = sent[ctx]

    loads[3].wait()
    reads[5].wait()

    @pl.loop(0, FF // 1024)
    def _(j):
        at = pl.ds(pl.multiple_of(j * 1024, 256), 1024)
        up_at = pl.ds(pl.multiple_of(FF + j * 1024, 256), 1024)
        hidden_grad = dot_t(m_sd[...], sd[pl.ds(j * 4, 4)].reshape(1024, D))
        gate, up = sj[:, at], sj[:, up_at]
        sig = jax.nn.sigmoid(gate)
        m_gu[:, at] = low(hidden_grad * up * sig * (1.0 + gate * (1.0 - sig)))
        m_gu[:, up_at] = low(hidden_grad * gate * sig)
        sh[:, at] = low(gate * sig * up)
        t_sh[at, :] = low(jnp.transpose(gate * sig * up))

    save(m_gu, p_gu)
    save(t_sh, p_sh)
    t_nf[...] = low(jnp.transpose(unit_ffn * small_t[1:2, :]))
    save(t_nf, p_nf)
    loads[1].wait()

    @pl.loop(0, D // 768)
    def _(j):
        at = pl.ds(pl.multiple_of(j * 768, 256), 768)
        normed_grad[:, at] = dot_t(m_gu[...], gu[at, :])

    reads[8].wait()
    products = dot_t(m_sd[...], ret[...].reshape(SLOTS, D))
    gate_grads = [jnp.sum(products * first, axis=1, keepdims=True), jnp.sum(products * second, axis=1, keepdims=True)]
    inner = gates[0] * gate_grads[0] + gates[1] * gate_grads[1]
    chosen = [g * (d - inner) for g, d in zip(gates, gate_grads)]
    logit_grads = jnp.where(picks[0], chosen[0], 0.0) + jnp.where(picks[1], chosen[1], 0.0)
    logit_high, logit_rest = split(logit_grads)
    grad_small[...] = t_dot(normed, logit_high) + t_dot(normed, logit_rest)
    normed_grad[...] += dot_t(logit_high, small[...]) + dot_t(logit_rest, small[...])

    loads[5].wait()
    reads[7].wait()
    ex_s.wait_recv()
    save(er, p_er)

    @pl.loop(0, FF // 1024)
    def _(j):
        at = pl.ds(pl.multiple_of(j * 1024, 256), 1024)
        up_at = pl.ds(pl.multiple_of(FF + j * 1024, 256), 1024)
        hidden_grad = dot_t(er[...].reshape(SLOTS, D), ed[at, :])
        gate, up = ej[:, at], ej[:, up_at]
        sig = jax.nn.sigmoid(gate)
        m_j[:, at] = low(hidden_grad * up * sig * (1.0 + gate * (1.0 - sig)))
        m_j[:, up_at] = low(hidden_grad * gate * sig)
        eh[:, at] = low(gate * sig * up)

    save(m_j, p_j)
    loads[4].wait()

    @pl.loop(0, D // 768)
    def _(j):
        at = pl.ds(pl.multiple_of(j * 768, 256), 768)
        back[:, :, at] = low(dot_t(m_j[...], egu[at, :])).reshape(EXPERTS, PAD_CAP, 768)

    ex_r = Exchange(back, slots, r_send, r_recv, True)
    ex_r.start()
    slots[ctx] = back[ctx]
    reads[6].wait()
    t_hd[...] = jnp.transpose(eh[...])
    save(t_hd, p_hd)
    t_rc[...] = jnp.transpose(rc[...].reshape(SLOTS, D))
    save(t_rc, p_rc)
    reads[3].wait()
    t_at[...] = jnp.transpose(att[...])
    save(t_at, p_at)
    loads[0].wait()
    ex_r.wait_recv()
    grad_normed = normed_grad[...] + dot(taken[...], slots[...].reshape(SLOTS, D))
    grad_values, gain_ffn = rms_back(grad_normed, small_t[1:2, :], scale_ffn, unit_ffn)
    grad_res = grad_out + grad_values
    m_pr[...] = low(grad_res)
    save(m_pr, p_pr)
    grad_att = low(dot_t(m_pr[...], wide[:, 3 * D :]))
    for g in range(4):
        o_pack[g] = grad_att[:, 192 * g : 192 * g + 192]
    ex_o = Exchange(o_pack, o_in, o_send, o_recv, False)
    ex_o.start()
    o_in[z] = o_pack[z]
    scale_attn, unit_attn = rms_parts(state[...].astype(jnp.float32))
    t_na[...] = low(jnp.transpose(unit_attn * small_t[0:1, :]))
    save(t_na, p_na)
    dkv_sum[...] = jnp.zeros_like(dkv_sum)
    for i in (0, 1, 2):
        reads[i].wait()
    ex_o.wait_recv()

    @pl.loop(0, 4)
    def _(d):
        block = lax.rem(z + d + 1, 4)
        seen = visible_keys(qidx[block], qlab[block], klab[...])
        for head in range(3):
            span = slice(64 * head, 64 * head + 64)
            vspan = slice(192 + 64 * head, 256 + 64 * head)
            q, do = q_all[block, :, span], o_in[block, :, span]
            k = kv_all[:, :, span].reshape(SEQ, HEAD_DIM)
            v = kv_all[:, :, vspan].reshape(SEQ, HEAD_DIM)
            scores = dot_t(q, k) * SCALE
            probs = jnp.where(seen, jnp.exp(scores - lse[block, :, head : head + 1]), 0.0)
            dprobs = dot_t(do, v)
            delta = jnp.sum(probs * dprobs, axis=-1, keepdims=True)
            dscores = low(probs * (dprobs - delta))
            dq_pack[block, :, span] = low(dot(dscores, k) * SCALE)
            dkv_sum[:, span] += t_dot(dscores, q) * SCALE
            dkv_sum[:, vspan] += t_dot(low(probs), do)

    ex_q = Exchange(dq_pack, dq_in, q_send, q_recv, False)
    ex_q.start()
    dkv_pack[...] = low(dkv_sum[...]).reshape(8, ROWS, 384)
    ex_kv = Exchange(dkv_pack, dkv_in, kv_send, kv_recv, True)
    ex_kv.start()
    dq_in[z] = dq_pack[z]
    dkv_in[ctx] = dkv_pack[ctx]
    ex_q.wait_recv()
    ex_kv.wait_recv()
    dq = jnp.concatenate([dq_in[g].astype(jnp.float32) for g in range(4)], axis=1)
    both = [dkv_in[g].astype(jnp.float32) + dkv_in[4 + g].astype(jnp.float32) for g in range(4)]
    dk = jnp.concatenate([v[:, :192] for v in both], axis=1)
    dv = jnp.concatenate([v[:, 192:] for v in both], axis=1)
    m_qkv[:, 0:D] = low(rotate(dq, cosine[...], -sine[...]))
    m_qkv[:, D : 2 * D] = low(rotate(dk, cosine[...], -sine[...]))
    m_qkv[:, 2 * D :] = low(dv)
    save(m_qkv, p_qkv)
    grad_normed = dot_t(m_qkv[...], wide[:, 0 : 3 * D])
    grad_values, gain_attn = rms_back(grad_normed, small_t[0:1, :], scale_attn, unit_attn)
    out[...] = grad_res + grad_values
    lane = lax.broadcasted_iota(jnp.int32, (D, SMALL), 1)
    gains_t = jnp.transpose(jnp.concatenate([gain_attn, gain_ffn, jnp.zeros((SMALL - 2, D), jnp.float32)], axis=0))
    grad_small[...] = jnp.where(lane < 2, gains_t, grad_small[...])
    save(grad_small, p_small)
    save(out, out_both)
    for ex in (ex_s, ex_r, ex_o, ex_q, ex_kv):
        ex.wait_send()

    @pl.when(section == layer)
    def _():
        for here, away in saves:
            here.wait()
            away.wait_recv()

    @pl.when(section != layer)
    def _():
        for here, away in saves:
            away.wait_send()


def layer_backward(layer, grad, state, geometry, plan, taken, small_t, weights, kept):
    bf, f32 = jnp.bfloat16, jnp.float32
    cosine, sine, qidx, qlab, klab = geometry
    route, first_table, second_table, _ = plan
    slots = pltpu.VMEM((EXPERTS, PAD_CAP, D), bf)
    shapes = dict(OPERANDS)
    order = ("na", "at", "nf", "sh", "rc", "hd", "qkv", "pr", "gu", "sd", "j", "er", "small")
    outs = pl.pallas_call(
        functools.partial(backward_kernel, layer),
        out_shape=[jax.ShapeDtypeStruct((ROWS, D), f32), jax.ShapeDtypeStruct((2, ROWS, D), f32)]
        + [jax.ShapeDtypeStruct((2,) + shapes[n], operand_type(n)) for n in order],
        in_specs=[VMEM] * 12 + [ANY] * (6 + len(KEPT)),
        out_specs=[VMEM, ANY] + [ANY] * N_OPS,
        scratch_shapes=weight_scratch()
        + [pltpu.VMEM(s, t) for s, t in KEPT] + [DMA((len(KEPT),))]
        + [pltpu.VMEM(shapes[n], operand_type(n)) for n in order if n != "er"] + [DMA((N_OPS + 1,))] * 3
        + [
            slots, slots, slots, slots,
            pltpu.VMEM((4, ROWS, 192), bf), pltpu.VMEM((4, ROWS, 192), bf),
            pltpu.VMEM((4, ROWS, 192), bf), pltpu.VMEM((4, ROWS, 192), bf),
            pltpu.VMEM((8, ROWS, 384), bf), pltpu.VMEM((8, ROWS, 384), bf), pltpu.VMEM((SEQ, 384), f32),
            pltpu.VMEM((ROWS, D), f32), pltpu.VMEM((ROWS, FF), bf), pltpu.VMEM((SLOTS, FF), bf),
            DMA((7,)), DMA((7,)), DMA((7,)), DMA((7,)), DMA((3,)), DMA((3,)), DMA((3,)), DMA((3,)), DMA((7,)), DMA((7,)),
        ],
        compiler_params=pltpu.CompilerParams(collective_id=3 + layer, has_side_effects=True, vmem_limit_bytes=62 << 20),
        name="layer_backward",
    )(grad, state, cosine, sine, qidx, qlab, klab, route, first_table, second_table, taken, small_t, *weights, *kept)
    return outs[0], outs[1], outs[2:]


def token_positions(group_row):
    labels = jnp.arange(CONT + 1, dtype=jnp.int32)
    member = (group_row[:, None] == labels[None, :]).astype(jnp.int32)
    run_sizes = jnp.sum(member, axis=0)
    run_starts = jnp.cumsum(run_sizes) - run_sizes
    first_index = jnp.sum(member * run_starts[None, :], axis=1)
    token_index = jnp.arange(group_row.shape[0], dtype=jnp.int32)
    return jnp.where(group_row == 0, token_index, run_sizes[0] + token_index - first_index)


def rotation_tables(positions):
    half = HEAD_DIM // 2
    frequency = jnp.exp(-math.log(10000.0) * jnp.arange(half, dtype=jnp.float32) / half)
    angles = positions.astype(jnp.float32)[:, None] * frequency[None, :]
    cosine, sine = jnp.cos(angles), jnp.sin(angles)
    cosine = jnp.tile(jnp.concatenate([cosine, cosine], axis=1), (1, HEADS))
    sine = jnp.tile(jnp.concatenate([-sine, sine], axis=1), (1, HEADS))
    return cosine, sine


def slot_tables(route, rank):
    pairs = ROWS * TOP
    expert = route.reshape(-1)
    key = rank.reshape(-1) * pairs + jnp.arange(pairs, dtype=jnp.int32)
    earlier = (expert[None, :] == expert[:, None]) & (key[None, :] < key[:, None])
    slot = jnp.sum(earlier.astype(jnp.int32), axis=1)
    place = jnp.where(slot < CAP, expert * PAD_CAP + slot, -1).reshape(ROWS, TOP)
    every = jnp.arange(SLOTS, dtype=jnp.int32)
    first, second = [place[:, c : c + 1] == every[None, :] for c in range(TOP)]
    both = low(first | second)
    return (route, low(first), low(second), both.T), both


def swap_cores(value):
    return lax.ppermute(value, "section", [(0, 1), (1, 0)])


def on_device(
    x_in, cotangent, group_ids, routes, priority,
    gains, w_qkv, w_out, router, shared_gate_up, shared_down, expert_gate_up, expert_down,
):
    section = lax.axis_index("section")
    ctx = lax.axis_index("ctx")
    first = section == 0

    pack = jnp.concatenate(
        [w_qkv[0], w_out[0], gains[0], router[0], jnp.zeros((OWN, SMALL - 2 - EXPERTS), jnp.bfloat16), shared_gate_up[0]],
        axis=1,
    )
    pack = jnp.pad(pack, ((0, 16 - OWN), (0, 0)))

    def mine(value):
        return jnp.where(first, value[0], value[1])

    def other(value):
        return jnp.where(first, value[1], value[0])

    picked = jnp.stack([routes[0, :, 0], priority[0, :, 0]], axis=1)
    passed = swap_cores(other(picked))
    own = mine(picked)
    plans = [jnp.where(first, own, passed), jnp.where(first, passed, own)]
    plans, taken = zip(*[slot_tables(plan[0], plan[1]) for plan in plans])

    group_row = mine(group_ids[:, 0])
    positions = token_positions(group_row)
    cosine, sine = rotation_tables(lax.dynamic_slice_in_dim(positions, ctx * ROWS, ROWS))
    half_start = ctx // 4 * 512
    qlab = lax.dynamic_slice_in_dim(group_row, half_start, 512).reshape(4, ROWS, 1)
    qidx = (half_start + jnp.arange(512, dtype=jnp.int32)).reshape(4, ROWS, 1)
    geometry = (cosine, sine, qidx, qlab, group_row[None, :])

    state = mine(x_in[:, 0])
    (hidden, final), weights, kept = forward(
        pack, shared_down[0], expert_gate_up[0, 0], expert_down[0, 0], state, geometry, plans
    )
    small_t = [weights[layer][2][:, :8].astype(jnp.float32).T for layer in range(2)]
    hidden_grad, hidden_grads, operands_upper = layer_backward(
        1, mine(cotangent[:, 0]), hidden, geometry, plans[1], taken[1], small_t[1], weights[1], kept[1]
    )
    _, input_grads, operands_lower = layer_backward(
        0, low(hidden_grad), state, geometry, plans[0], taken[0], small_t[0], weights[0], kept[0]
    )
    qkv_grad, out_grad, small_grad, gu_grad, sd_grad, egu_grad, ed_grad = weight_grads(operands_lower, operands_upper)

    outputs = jnp.where(first, hidden, final)
    arrived = swap_cores(jnp.where(first, final, hidden))
    outputs = jnp.stack([jnp.where(first, outputs, arrived), jnp.where(first, arrived, outputs)])
    grads = jnp.where(first, input_grads, hidden_grads[::-1])
    return (
        outputs.reshape(1, 2, 1, ROWS, D),
        grads.reshape(1, 2, 1, ROWS, D),
        small_grad[None, :, :2],
        qkv_grad[None],
        out_grad[None],
        small_grad[None, :, 2 : 2 + EXPERTS],
        gu_grad[None],
        sd_grad[None],
        egu_grad[None, None],
        ed_grad[None, None],
    )


def solution(mesh):
    dense = P("section", ("ctx", "fsdp"), None)
    expert = P("section", "ctx", "fsdp", None)
    tokens = P("section", None, "fsdp", "ctx", None)
    rows = P(None, "fsdp", "ctx", None)
    return jax.shard_map(
        on_device,
        mesh=mesh,
        in_specs=(rows, rows, P(None, "fsdp", None), tokens, tokens) + (dense,) * 6 + (expert,) * 2,
        out_specs=(tokens, tokens) + (dense,) * 6 + (expert,) * 2,
        check_vma=False,
    )
```

```python
import functools
import math

import jax
import jax.numpy as jnp
from jax import lax
from jax.experimental import pallas as pl
from jax.experimental.pallas import tpu as pltpu
from jax.sharding import PartitionSpec as P

MESH = pl.DeviceIdType.MESH
ANY = pl.BlockSpec(memory_space=pl.ANY)
VMEM = pl.BlockSpec(memory_space=pltpu.VMEM)
DMA = pltpu.SemaphoreType.DMA

D = 768
FF = 2048
WIDE = 3072
SMALL = 128
PACK = WIDE + 2 * FF + SMALL
OWN = 12
HEADS = 12
HEAD_DIM = 64
TOP = 2
CONT = 8
EXPERTS = 8
SEQ = 1024
ROWS = 128
CAP = 40
PAD_CAP = 48
SLOTS = EXPERTS * PAD_CAP
SCALE = 1.0 / math.sqrt(HEAD_DIM)
EPS = 1e-06
NEG = -1e30


def place_ids():
    section = lax.axis_index("section")
    ctx = lax.axis_index("ctx")
    fsdp = lax.axis_index("fsdp")
    return section, ctx // 4, lax.rem(ctx, 4), fsdp // 2, lax.rem(fsdp, 2)


def ctx_of(half, ring):
    return lax.rem(half + 2, 2) * 4 + lax.rem(ring + 4, 4)


def fsdp_of(ring, half):
    return lax.rem(ring + 4, 4) * 2 + lax.rem(half + 2, 2)


def neighbours():
    section, a, z, y, h = place_ids()
    ctx, fsdp = ctx_of(a, z), fsdp_of(y, h)
    return dict(
        core=(1 - section, ctx, fsdp),
        zp=(section, ctx_of(a, z + 1), fsdp),
        zm=(section, ctx_of(a, z - 1), fsdp),
        zx=(section, ctx_of(a + 1, z), fsdp),
        yp=(section, ctx, fsdp_of(y + 1, h)),
        ym=(section, ctx, fsdp_of(y - 1, h)),
        yx=(section, ctx, fsdp_of(y, h + 1)),
    )


def greet(devices):
    barrier = pltpu.get_barrier_semaphore()
    for device in devices:
        pl.semaphore_signal(barrier, inc=1, device_id=device, device_id_type=MESH)
    pl.semaphore_wait(barrier, len(devices))


def rows_at(ref, block, rows, part=None):
    if part is None:
        return ref.at[pl.ds(pl.multiple_of(block * rows, 16), rows)]
    half = rows // 2
    return ref.at[pl.ds(pl.multiple_of(block * rows + part * half, 16), half)]


class Hop:
    def __init__(self, sources, targets, device, send, recv):
        self.copies = [
            pltpu.make_async_remote_copy(s, t, send.at[i], recv.at[i], device_id=device, device_id_type=MESH)
            for i, (s, t) in enumerate(zip(sources, targets))
        ]

    def start(self):
        for copy in self.copies:
            copy.start()
        return self

    def wait_recv(self):
        for copy in self.copies:
            copy.wait_recv()

    def wait_send(self):
        for copy in self.copies:
            copy.wait_send()


def row_view(rows):
    return lambda whole, block, part: rows_at(whole, block, rows, part)


def shard_view(whole, block, part):
    if part is None:
        return whole.at[:, block]
    return whole.at[4 * part : 4 * part + 4, block]


class Tree:
    def __init__(self, over_ctx, halves, own, whole, view, send, recv, c_send, c_recv, l_sem):
        section, a, z, y, h = place_ids()
        near = neighbours()
        self.halves = halves
        ring, pair = ("z", "zx") if over_ctx else ("y", "yx")
        plus, minus, across = near[ring + "p"], near[ring + "m"], near[pair]

        def views(step, side, part=None):
            block = ctx_of(a + side, z + step) if over_ctx else fsdp_of(y + step, h + side)
            return [v(w, block, part) for w, v in zip(whole, view)]

        def hop(index, sources, targets, device):
            return Hop(sources, targets, device, send.at[index], recv.at[index])

        mine = views(0, 0)
        self.stays = [] if own is None else [pltpu.make_async_copy(o, m, l_sem.at[i]) for i, (o, m) in enumerate(zip(own, mine))]
        own = mine if own is None else own
        self.hops = [
            hop(0, own, mine, plus),
            hop(1, own, mine, minus),
            hop(2, own, mine, across),
            hop(3, views(-1, 0, 0), views(-1, 0, 0), plus),
            hop(4, views(1, 0, 1), views(1, 0, 1), minus),
            hop(5, views(0, 1), views(0, 1), plus),
            hop(6, views(0, 1), views(0, 1), minus),
        ]
        if halves:
            self.hops.append(hop(7, views(-1, 1, 0), views(-1, 1, 0), plus))
            self.hops.append(hop(8, views(1, 1, 1), views(1, 1, 1), minus))
        else:
            self.hops.append(hop(7, views(2, 0), views(2, 0), across))
        places = [(0, 0), (-1, 0), (1, 0), (0, 1), (2, 0), (-1, 1), (1, 1), (2, 1)]
        self.cores = [
            Hop(own if k == 0 else views(*p), views(*p), near["core"], c_send.at[k], c_recv.at[k]) for k, p in enumerate(places)
        ]

    def start_own(self):
        for index in (0, 1, 2):
            self.hops[index].start()
        self.cores[0].start()
        for copy in self.stays:
            copy.start()

    def pass_ring(self):
        for index, later, core in ((0, 3, 1), (1, 4, 2)):
            self.hops[index].wait_recv()
            self.hops[later].start()
            self.cores[core].start()

    def pass_pair(self):
        self.hops[2].wait_recv()
        self.hops[5].start()
        self.hops[6].start()
        self.cores[3].start()

    def pass_far(self):
        if self.halves:
            for index, later, core in ((5, 7, 5), (6, 8, 6)):
                self.hops[index].wait_recv()
                self.hops[later].start()
                self.cores[core].start()
        self.hops[3].wait_recv()
        self.hops[4].wait_recv()
        if not self.halves:
            self.hops[7].start()
        self.cores[4].start()

    def finish(self):
        if self.halves:
            self.hops[7].wait_recv()
            self.hops[8].wait_recv()
            self.cores[7].start()
        else:
            for index, core in ((5, 5), (6, 6), (7, 7)):
                self.hops[index].wait_recv()
                self.cores[core].start()
        for copy in self.stays:
            copy.wait()

    def receive(self):
        for hop in self.cores:
            hop.wait_recv()

    def drain(self):
        for hop in self.hops + self.cores:
            hop.wait_send()


class Shards:
    def __init__(self, pack, packs, sd, whole_sd, send, recv, l_sem):
        section, a, z, y, h = place_ids()
        ctx, fsdp = ctx_of(a, z), fsdp_of(y, h)
        wide = slice(0, WIDE + SMALL)
        rest = slice(WIDE + SMALL, PACK)
        mine = packs.at[pl.ds(pl.multiple_of(fsdp * 16, 16), 16)]
        pieces = [
            (pack.at[:, wide], mine.at[:, wide], fsdp_peers()),
            (pack.at[:, rest], mine.at[:, rest], fsdp_peers()),
            (sd, whole_sd.at[ctx, fsdp], ctx_peers()),
        ]
        self.hops = [
            [Hop([s], [t], device, send.at[k, pl.ds(i, 1)], recv.at[k, pl.ds(i, 1)]) for k, device in enumerate(peers)]
            for i, (s, t, peers) in enumerate(pieces)
        ]
        self.stays = [pltpu.make_async_copy(s, t, l_sem.at[i]) for i, (s, t, _) in enumerate(pieces)]

    def start(self, *pieces):
        for i in pieces:
            for hop in self.hops[i]:
                hop.start()
            self.stays[i].start()

    def wait(self, *pieces):
        for i in pieces:
            for hop in self.hops[i]:
                hop.wait_recv()
            self.stays[i].wait()

    def drain(self):
        for hops in self.hops:
            for hop in hops:
                hop.wait_send()


FSDP_STEPS = [(dy, dh) for dy in (1, 3, 2, 0) for dh in (0, 1) if (dy, dh) != (0, 0)]


def fsdp_peers():
    section, a, z, y, h = place_ids()
    ctx = ctx_of(a, z)
    return [(section, ctx, fsdp_of(y + dy, h + dh)) for dy, dh in FSDP_STEPS]


def close_table(transposed=False):
    shape, dims = ((128, 96), (1, 0)) if transposed else ((96, 128), (0, 1))
    closed, padded = [lax.broadcasted_iota(jnp.int32, shape, d) for d in dims]
    within = padded % 16
    return low(jnp.where((within < OWN) & (closed == OWN * (padded // 16) + within), 1.0, 0.0))


def close_rows(packs, target, start):
    width = target.shape[1]
    step = min(width, 512)

    @pl.loop(0, width // step)
    def _(j):
        off = pl.multiple_of(j * step, 128)
        block = packs[:, pl.ds(pl.multiple_of(start + off, 128), step)]
        target[:, pl.ds(off, step)] = low(dot(close_table(), block))


LEFT = (("na", (D, 128)), ("at", (D, 128)), ("nf", (D, 128)), ("sh", (FF, 128)), ("rc", (D, SLOTS)), ("hd", (FF, SLOTS)))
RIGHT = (
    ("qkv", (128, 3 * D)), ("pr", (128, D)), ("gu", (128, 2 * FF)), ("sd", (128, D)), ("j", (SLOTS, 2 * FF)),
    ("er", (EXPERTS, PAD_CAP, D)), ("small", (D, SMALL)),
)
OPERANDS = LEFT + RIGHT
N_OPS = len(OPERANDS)


def operand_type(name):
    return jnp.float32 if name == "small" else jnp.bfloat16


ATTENTION = (("wide", "na", "qkv", 96, 0, 3 * D, D), ("wide", "at", "pr", 96, 3 * D, D, D))
SHARED = (("gu", "nf", "gu", 96, 0, 2 * FF, 1024), ("sd", "sh", "sd", 256, 0, D, D))
EXPERT = (("egu", "rc", "j", 96, 0, 2 * FF, 1024), ("ed", "hd", "er", 256, 0, D, D))


def grads_kernel(*refs):
    lower, upper = refs[:N_OPS], refs[N_OPS : 2 * N_OPS]
    out_qkv, out_out, out_small, out_gu, out_sd, out_egu, out_ed = refs[2 * N_OPS : 2 * N_OPS + 7]
    rest = refs[2 * N_OPS + 7 :]
    held = rest[:N_OPS]
    (b_wide, b_gu, b_small, b_sd, c_gu, c_sd, packs, in_pack, in_sd,
     o_local, w_send, w_recv, r_send, r_recv, e_send, e_recv, s_send, s_recv) = rest[N_OPS:]
    names = [n for n, _ in OPERANDS]
    ops = dict(zip(names, held))
    section, a, z, y, h = place_ids()
    ctx, fsdp = ctx_of(a, z), fsdp_of(y, h)
    near = neighbours()

    def bring(source, i, which):
        n, shape = OPERANDS[i]
        if i < len(LEFT):
            target = held[i].at[:, pl.ds(which * shape[1], shape[1])]
        elif n in ("er", "small"):
            target = held[i].at[which]
        else:
            target = held[i].at[pl.ds(which * shape[0], shape[0])]
        return pltpu.make_async_copy(source[i].at[which], target, o_local.at[i, which])

    order = [names.index(n) for n in ("na", "qkv", "at", "pr", "small", "nf", "gu", "sh", "sd", "rc", "j", "hd", "er")]
    for layer, source in enumerate((lower, upper)):

        @pl.when(section == layer)
        def _(source=source):
            for i in order:
                for which in range(2):
                    bring(source, i, which).start()

    greet([near["zp"], near["zm"], near["zx"]] + fsdp_peers())

    def ready(*wanted):
        for n in wanted:
            for which in range(2):
                bring(lower, names.index(n), which).wait()

    kinds = dict(wide=b_wide, gu=b_gu, small=b_small, sd=b_sd, egu=c_gu, ed=c_sd)
    buffers = {
        ATTENTION: ((b_wide, 96), (b_small, 96)),
        SHARED: ((b_gu, 96), (b_sd, 256)),
        EXPERT: ((c_gu, 96), (c_sd, 256)),
    }
    semaphores = {ATTENTION: (w_send, w_recv), SHARED: (r_send, r_recv), EXPERT: (e_send, e_recv)}

    def combine(pieces, block, slot, adds=(), part=None, target=None):
        for kind, left, right, rows, first, width, step in pieces:
            n = rows if part is None else rows // 2
            off = 0 if part is None else part * n
            lhs_rows = pl.ds(pl.multiple_of(block * rows + off, 16), n)

            @pl.loop(0, width // step)
            def _(j, kind=kind, left=left, right=right, first=first, n=n, off=off, lhs_rows=lhs_rows, step=step):
                at = pl.ds(pl.multiple_of(j * step, 256), step)
                to = pl.ds(pl.multiple_of(first + j * step, 256), step)
                if right == "er":
                    right_part = ops[right][:, :, :, at].reshape(2 * SLOTS, step)
                else:
                    right_part = ops[right][:, at]
                total = dot(ops[left][lhs_rows, :], right_part)
                for other in adds:
                    total += kinds[kind][other, off : off + n, to].astype(jnp.float32)
                if target is None:
                    kinds[kind][slot, off : off + n, to] = low(total)
                else:
                    target[kind][off : off + n, to] = total

        if pieces is ATTENTION:
            n = 96 if part is None else 48
            off = 0 if part is None else part * n
            at = pl.ds(pl.multiple_of(block * 96 + off, 16), n)
            total = ops["small"][0, at, :] + ops["small"][1, at, :]
            for other in adds:
                total += b_small[other, off : off + n, :].astype(jnp.float32)
            b_small[slot, off : off + n, :] = low(total)

    hops = {}

    def send(pieces, index, slot, to_slot, device, part=None):
        def views(which):
            return [rows_at(b.at[which], 0, r, part) for b, r in buffers[pieces]]

        sems = semaphores[pieces]
        hops[pieces, index] = Hop(views(slot), views(to_slot), near[device], sems[0].at[index], sems[1].at[index]).start()

    def arrived(pieces, *indices):
        for index in indices:
            hops[pieces, index].wait_recv()

    def sent(pieces, *indices):
        for index in indices:
            hops[pieces, index].wait_send()

    def d_block(dz, da):
        return ctx_of(a + da, z + dz)

    def e_block(dy, dh):
        return fsdp_of(y + dy, h + dh)

    def spread(pieces):
        combine(pieces, d_block(2, 1), 0)
        send(pieces, 0, 0, 1, "zx")
        combine(pieces, d_block(-1, 1), 2)
        send(pieces, 1, 2, 5, "zm")
        combine(pieces, d_block(1, 1), 3)
        send(pieces, 2, 3, 6, "zp")

    def halves(pieces):
        arrived(pieces, 0)
        combine(pieces, d_block(2, 0), 1, (1,))
        send(pieces, 3, 1, 4, "zm", 0)
        send(pieces, 4, 1, 4, "zp", 1)

    def next_ones(pieces):
        sent(pieces, 0)
        combine(pieces, d_block(-1, 0), 0, (), 1)
        arrived(pieces, 3)
        combine(pieces, d_block(-1, 0), 0, (4,), 0)
        send(pieces, 5, 0, 7, "zm")
        sent(pieces, 3, 4)
        combine(pieces, d_block(1, 0), 1, (), 0)
        arrived(pieces, 4)
        combine(pieces, d_block(1, 0), 1, (4,), 1)
        send(pieces, 6, 1, 8, "zp")

    def pair(pieces):
        arrived(pieces, 1, 2)
        combine(pieces, d_block(0, 1), 5, (5, 6))
        send(pieces, 7, 5, 9, "zx")

    def own(pieces):
        arrived(pieces, 5, 6, 7)
        combine(pieces, ctx, 7, (7, 8, 9))

    def open_rows(kind, start, width):
        step = min(width, 1024)

        @pl.loop(0, width // step)
        def _(j):
            off = pl.multiple_of(j * step, 128)
            block = kinds[kind][7, :, pl.ds(off, step)]
            packs[:, pl.ds(pl.multiple_of(start + off, 128), step)] = low(dot(close_table(True), block))

    last = [[], [], []]
    split_at = WIDE + SMALL

    def to_owners(which):
        for k, device in enumerate(fsdp_peers()):
            dy, dh = FSDP_STEPS[k]
            block = e_block(dy, dh)
            rows = packs.at[pl.ds(pl.multiple_of(block * 16, 16), 16)]
            source, target = (
                (rows.at[:, :split_at], in_pack.at[k, :, :split_at]),
                (rows.at[:, split_at:], in_pack.at[k, :, split_at:]),
                (rows_at(b_sd.at[7], block, 32), in_sd.at[k]),
            )[which]
            last[which].append(
                Hop([source], [target], device, s_send.at[k, pl.ds(which, 1)], s_recv.at[k, pl.ds(which, 1)]).start()
            )

    def total_of(which, start, width, out):
        step = min(width, 256)

        @pl.loop(0, width // step)
        def _(j):
            at = pl.ds(pl.multiple_of(start + j * step, 128), step)
            total = packs[pl.ds(pl.multiple_of(fsdp * 16, 16), 16), at].astype(jnp.float32)
            for k in range(7):
                total += in_pack[k, :, at].astype(jnp.float32)
            out[:, pl.ds(pl.multiple_of(j * step, 128), step)] = total[:OWN]

    ready("na", "qkv", "at", "pr", "small")
    spread(ATTENTION)
    ready("nf", "gu", "sh", "sd")
    spread(SHARED)
    ready("rc", "j", "hd", "er")
    combine(EXPERT, e_block(2, 1), 0)
    send(EXPERT, 0, 0, 4, "ym", 0)
    send(EXPERT, 1, 0, 4, "yp", 1)
    halves(ATTENTION)
    combine(EXPERT, e_block(2, 0), 1)
    send(EXPERT, 2, 1, 5, "ym", 0)
    send(EXPERT, 3, 1, 5, "yp", 1)
    combine(EXPERT, e_block(-1, 1), 2, (), 1)
    combine(EXPERT, e_block(1, 1), 3, (), 0)
    arrived(EXPERT, 0)
    combine(EXPERT, e_block(-1, 1), 2, (4,), 0)
    send(EXPERT, 4, 2, 6, "ym")
    arrived(EXPERT, 1)
    combine(EXPERT, e_block(1, 1), 3, (4,), 1)
    send(EXPERT, 5, 3, 7, "yp")
    pair(ATTENTION)
    halves(SHARED)
    next_ones(ATTENTION)
    pair(SHARED)
    sent(EXPERT, 0, 1)
    combine(EXPERT, e_block(-1, 0), 0, (), 1)
    arrived(EXPERT, 2)
    combine(EXPERT, e_block(-1, 0), 0, (5,), 0)
    send(EXPERT, 6, 0, 8, "ym")
    sent(EXPERT, 2, 3)
    combine(EXPERT, e_block(1, 0), 1, (), 0)
    arrived(EXPERT, 3)
    combine(EXPERT, e_block(1, 0), 1, (5,), 1)
    send(EXPERT, 7, 1, 9, "yp")
    next_ones(SHARED)
    arrived(EXPERT, 4, 5)
    combine(EXPERT, e_block(0, 1), 6, (6, 7))
    send(EXPERT, 8, 6, 10, "yx")
    own(ATTENTION)
    open_rows("wide", 0, WIDE)
    open_rows("small", WIDE, SMALL)
    to_owners(0)
    own(SHARED)
    open_rows("gu", split_at, 2 * FF)
    to_owners(1)
    to_owners(2)
    for hop in last[0]:
        hop.wait_recv()
    total_of(0, 0, 3 * D, out_qkv)
    total_of(0, 3 * D, D, out_out)
    total_of(0, WIDE, SMALL, out_small)
    arrived(EXPERT, 6, 7, 8)
    combine(EXPERT, fsdp, 0, (8, 9, 10), None, dict(egu=out_egu, ed=out_ed))
    for hop in last[1] + last[2]:
        hop.wait_recv()
    total_of(1, split_at, 2 * FF, out_gu)
    total = b_sd[7, pl.ds(pl.multiple_of(fsdp * 32, 16), 32), :].astype(jnp.float32)
    for k in range(7):
        total += in_sd[k].astype(jnp.float32)
    out_sd[...] = total
    for pieces in (ATTENTION, SHARED):
        sent(pieces, 1, 2, 5, 6, 7)
    sent(EXPERT, 4, 5, 6, 7, 8)
    for hop in last[0] + last[1] + last[2]:
        hop.wait_send()


def weight_grads(lower, upper):
    bf, f32 = jnp.bfloat16, jnp.float32
    held = [pltpu.VMEM((shape[0], 2 * shape[1]), bf) for _, shape in LEFT]
    for name, shape in RIGHT:
        whole = (2,) + shape if name in ("er", "small") else (2 * shape[0], shape[1])
        held.append(pltpu.VMEM(whole, operand_type(name)))
    shapes = [(OWN, 3 * D), (OWN, D), (OWN, SMALL), (OWN, 2 * FF), (32, D), (96, 2 * FF), (256, D)]
    return pl.pallas_call(
        grads_kernel,
        out_shape=[jax.ShapeDtypeStruct(shape, f32) for shape in shapes],
        in_specs=[ANY] * (2 * N_OPS),
        out_specs=[VMEM] * len(shapes),
        scratch_shapes=held + [
            pltpu.VMEM((10, 96, WIDE), bf),
            pltpu.VMEM((10, 96, 2 * FF), bf),
            pltpu.VMEM((10, 96, SMALL), bf),
            pltpu.VMEM((10, 256, D), bf),
            pltpu.VMEM((11, 96, 2 * FF), bf),
            pltpu.VMEM((11, 256, D), bf),
            pltpu.VMEM((128, PACK), bf),
            pltpu.VMEM((7, 16, PACK), bf),
            pltpu.VMEM((7, 32, D), bf),
            DMA((N_OPS, 2)),
            DMA((8, 2)), DMA((8, 2)), DMA((8, 2)), DMA((8, 2)),
            DMA((9, 2)), DMA((9, 2)),
            DMA((7, 3)), DMA((7, 3)),
        ],
        compiler_params=pltpu.CompilerParams(collective_id=5, has_side_effects=True, vmem_limit_bytes=62 << 20),
        name="weight_grads",
    )(*lower, *upper)


def split(values):
    high = low(values)
    return high, low(values - high.astype(jnp.float32))


def rms_parts(values):
    scale = lax.rsqrt(jnp.mean(values * values, axis=-1, keepdims=True) + EPS)
    return scale, values * scale


def rms_back(grad, gain, scale, unit):
    inner = grad * gain
    grad_values = scale * (inner - unit * jnp.mean(inner * unit, axis=-1, keepdims=True))
    return grad_values, jnp.sum(grad * unit, axis=0, keepdims=True)


def dot(left, right):
    return jnp.dot(left, right, preferred_element_type=jnp.float32)


def dot_t(left, right):
    return lax.dot_general(left, right, (((1,), (1,)), ((), ())), preferred_element_type=jnp.float32)


def t_dot(left, right):
    return lax.dot_general(left, right, (((0,), (0,)), ((), ())), preferred_element_type=jnp.float32)


def low(values):
    return values.astype(jnp.bfloat16)


def rotate(values, cosine, sine):
    half = HEAD_DIM // 2
    lower = lax.broadcasted_iota(jnp.int32, (values.shape[0], 128), 1) % HEAD_DIM < half
    parts = []
    for start in range(0, values.shape[1], 128):
        span = slice(start, start + 128)
        part = values[:, span]
        other = jnp.where(lower, pltpu.roll(part, 128 - half, 1), pltpu.roll(part, half, 1))
        parts.append(part * cosine[:, span] + other * sine[:, span])
    return jnp.concatenate(parts, axis=1)


def visible_keys(qidx, qlab, klab):
    kidx = lax.broadcasted_iota(jnp.int32, (qidx.shape[0], klab.shape[1]), 1)
    return (kidx <= qidx) & ((klab == 0) | (klab == qlab))


def pair_gates(logits, route):
    lane = lax.broadcasted_iota(jnp.int32, logits.shape, 1)
    picks = [lane == route[:, c : c + 1] + 2 for c in range(TOP)]
    first, second = [jnp.sum(jnp.where(p, logits, 0.0), axis=1, keepdims=True) for p in picks]
    top = jnp.maximum(first, second)
    first, second = jnp.exp(first - top), jnp.exp(second - top)
    total = first + second
    return picks, [first / total, second / total]


class Exchange:
    def __init__(self, source, target, send, recv, everyone, block_of=None):
        section, a, z, y, h = place_ids()
        fsdp = fsdp_of(y, h)
        offsets = [(1, 0), (1, 1), (1, 3), (1, 2)] if everyone else []
        self.copies = []
        for k, (da, dz) in enumerate(offsets + [(0, 1), (0, 3), (0, 2)]):
            c, zz = ctx_of(a + da, z + dz), lax.rem(z + dz, 4)
            block = zz if block_of == "ring" or not everyone else c
            to = ctx_of(a, z) if everyone else z
            self.copies.append(
                pltpu.make_async_remote_copy(
                    source.at[block], target.at[to], send.at[k], recv.at[k], device_id=(section, c, fsdp), device_id_type=MESH
                )
            )

    def start(self):
        for copy in self.copies:
            copy.start()

    def wait_recv(self):
        for copy in self.copies:
            copy.wait_recv()

    def wait_send(self):
        for copy in self.copies:
            copy.wait_send()


CTX_STEPS = [(1, 0), (0, 1), (0, 3), (0, 2), (1, 1), (1, 3), (1, 2)]


def ctx_peers():
    section, a, z, y, h = place_ids()
    fsdp = fsdp_of(y, h)
    return [(section, ctx_of(a + da, z + dz), fsdp) for da, dz in CTX_STEPS]


def forward_kernel(
    pack, i_sd, i_egu, i_ed,
    state, cosine, sine, qidx, qlab, klab, route, first_table, second_table, taken_t,
    out_lower, out_upper,
    l_wide, l_gu, l_small, l_sd, l_egu, l_ed, u_wide, u_gu, u_small, u_sd, u_egu, u_ed,
    *rest,
):
    kept = (rest[:9], rest[9:18])
    (wide, gu, small, sd, egu, ed, w_sem,
     packs, own_wide, own_small, own_gu, g_sd, g_egu, g_ed, g_stay, sh_send, sh_recv,
     w_send, w_recv, g_send, g_recv, d_send, d_recv, e_send, e_recv,
     wc_send, wc_recv, gc_send, gc_recv, dc_send, dc_recv, ec_send, ec_recv,
     kv_pack, q_pack, kv_all, q_all, o_pack, o_in, lse, att, res, sj, sh, sent, rc, ej, eh, result, ret, k_sem,
     x_send, x_recv) = rest[18:]
    section, a, z, y, h = place_ids()
    ctx = ctx_of(a, z)
    wholes = ((l_wide, l_gu, l_small, l_sd, l_egu, l_ed), (u_wide, u_gu, u_small, u_sd, u_egu, u_ed))
    shards_in = [
        pltpu.make_async_copy(s, t, g_stay.at[4, i]) for i, (s, t) in enumerate(((i_sd, g_sd), (i_egu, g_egu), (i_ed, g_ed)))
    ]
    for copy in shards_in:
        copy.start()
    greet([neighbours()["core"]] + ctx_peers() + fsdp_peers())
    for copy in shards_in:
        copy.wait()

    trees, firsts = [], []
    for layer in range(2):
        t_wide, t_gu, t_small, t_sd, t_egu, t_ed = wholes[layer]
        firsts.append(Shards(pack, packs, g_sd, t_sd, sh_send, sh_recv, g_stay.at[0]))
        trees.append(
            dict(
                w=Tree(True, False, [own_wide, own_small], [t_wide, t_small], [row_view(96)] * 2,
                       w_send, w_recv, wc_send.at[layer], wc_recv.at[layer], g_stay.at[1]),
                g=Tree(True, True, [own_gu], [t_gu], [row_view(96)],
                       g_send, g_recv, gc_send.at[layer], gc_recv.at[layer], g_stay.at[2]),
                d=Tree(False, True, None, [t_sd], [shard_view],
                       d_send, d_recv, dc_send.at[layer], dc_recv.at[layer], None),
                e=Tree(False, True, [g_egu, g_ed], [t_egu, t_ed], [row_view(96), row_view(256)],
                       e_send, e_recv, ec_send.at[layer], ec_recv.at[layer], g_stay.at[3]),
            )
        )

    def drive(layer, *steps):
        @pl.when(section == layer)
        def _():
            for step in steps:
                step()

    def close_wide():
        firsts[0].wait(0)
        close_rows(packs, own_wide, 0)
        close_rows(packs, own_small, WIDE)

    def close_gu():
        firsts[0].wait(1)
        close_rows(packs, own_gu, WIDE + SMALL)

    def arrived(layer, group):
        drive(layer, trees[layer][group].finish)

        @pl.when(section != layer)
        def _():
            trees[layer][group].receive()

    def load(layer, *which):
        for i in which:
            target = (wide.at[layer], gu, small.at[layer], sd, egu, ed)[i]
            pltpu.make_async_copy(wholes[layer][i], target, w_sem.at[layer, i]).start()

    def loaded(layer, *which):
        for i in which:
            target = (wide.at[layer], gu, small.at[layer], sd, egu, ed)[i]
            pltpu.make_async_copy(wholes[layer][i], target, w_sem.at[layer, i]).wait()

    def first(layer, *pieces):
        return lambda: firsts[layer].start(*pieces)

    def down(layer):
        def step():
            firsts[layer].wait(2)
            trees[layer]["d"].start_own()

        return step

    lower, upper = trees
    hooks = {
        (0, "start"): lambda: (
            drive(0, first(0, 0), close_wide, lower["w"].start_own, first(0, 1, 2), lower["w"].pass_ring, lower["w"].pass_pair,
                  lower["w"].pass_far, lower["e"].start_own, close_gu, lower["g"].start_own),
            arrived(0, "w"), load(0, 0, 2),
        ),
        (0, "keys"): lambda: (drive(0, lower["e"].pass_ring, lower["e"].pass_pair), drive(1, first(1, 0, 1, 2))),
        (0, "queries"): lambda: drive(0, lower["g"].pass_pair),
        (0, "block1"): lambda: drive(0, down(0)),
        (0, "attended"): lambda: (
            drive(0, lower["g"].pass_ring, lower["e"].pass_far), drive(1, close_wide, upper["w"].start_own),
        ),
        (0, "sent"): lambda: (
            drive(0, lower["g"].pass_far, lower["d"].pass_ring, lower["d"].pass_pair),
            drive(1, upper["w"].pass_ring, upper["w"].pass_pair, close_gu),
            arrived(0, "e"), load(0, 4, 5),
        ),
        (0, "expert0"): lambda: drive(1, upper["e"].start_own),
        (0, "expert1"): lambda: drive(0, lower["d"].pass_far),
        (0, "expert2"): lambda: drive(1, upper["w"].pass_far),
        (0, "returned"): lambda: (
            arrived(0, "g"), load(0, 1), drive(1, upper["g"].start_own, upper["e"].pass_ring, upper["e"].pass_pair),
            arrived(0, "d"), load(0, 3),
        ),
        (1, "start"): lambda: (arrived(1, "w"), load(1, 0, 2)),
        (1, "queries"): lambda: drive(1, upper["g"].pass_pair),
        (1, "block1"): lambda: drive(1, down(1), upper["e"].pass_far),
        (1, "attended"): lambda: drive(1, upper["g"].pass_ring),
        (1, "sent"): lambda: (
            drive(1, upper["g"].pass_far, upper["d"].pass_ring, upper["d"].pass_pair), arrived(1, "e"), load(1, 4, 5),
        ),
        (1, "expert1"): lambda: drive(1, upper["d"].pass_far),
        (1, "returned"): lambda: (arrived(1, "g"), load(1, 1), arrived(1, "d"), load(1, 3)),
    }

    def one_layer(layer, x, out):
        def hook(name):
            if (layer, name) in hooks:
                hooks[layer, name]()

        k_q, k_kv, k_lse, k_att, k_res, k_sj, k_rc, k_ej, k_ret = kept[layer]
        saves = []

        def save(source, target):
            copy = pltpu.make_async_copy(source, target, k_sem.at[len(saves)])
            copy.start()
            saves.append(copy)

        def exchange(index, source, target, everyone, block_of=None):
            sems = x_send.at[layer, index], x_recv.at[layer, index]
            return Exchange(source, target, *sems, everyone, block_of)

        scale, unit = rms_parts(x)
        hook("start")
        loaded(layer, 0, 2)
        wide_l, small_l = wide.at[layer], small.at[layer]
        gains = jnp.transpose(small_l[...].astype(jnp.float32))
        normed = low(unit * gains[0:1, :])
        keys = low(rotate(dot(normed, wide_l[:, D : 2 * D]), cosine[...], sine[...]))
        values = low(dot(normed, wide_l[:, 2 * D : 3 * D]))
        for g in range(4):
            kv_pack[g, :, 0:192] = keys[:, 192 * g : 192 * g + 192]
            kv_pack[g, :, 192:384] = values[:, 192 * g : 192 * g + 192]
        ex_kv = exchange(0, kv_pack, kv_all, True, "ring")
        ex_kv.start()
        hook("keys")
        queries = low(rotate(dot(normed, wide_l[:, 0:D]), cosine[...], sine[...]))
        for g in range(4):
            q_pack[g] = queries[:, 192 * g : 192 * g + 192]
        ex_q = exchange(1, q_pack, q_all, False)
        ex_q.start()
        kv_all[ctx] = kv_pack[z]
        q_all[z] = q_pack[z]
        hook("queries")
        ex_q.wait_recv()
        ex_kv.wait_recv()
        save(kv_all, k_kv)
        save(q_all, k_q)

        def attend(d):
            block = lax.rem(z + d + 1, 4)
            seen = visible_keys(qidx[block], qlab[block], klab[...])
            for head in range(3):
                span = slice(64 * head, 64 * head + 64)
                vspan = slice(192 + 64 * head, 256 + 64 * head)
                k = kv_all[:, :, span].reshape(SEQ, HEAD_DIM)
                v = kv_all[:, :, vspan].reshape(SEQ, HEAD_DIM)
                scores = jnp.where(seen, dot_t(q_all[block, :, span], k) * SCALE, NEG)
                top = jnp.max(scores, axis=-1, keepdims=True)
                weights = jnp.exp(scores - top)
                total = jnp.sum(weights, axis=-1, keepdims=True)
                o_pack[block, :, span] = low(dot(low(weights / total), v))
                lse[block, :, head : head + 1] = top + jnp.log(total)

        for d in range(4):
            pl.loop(d, d + 1)(attend)
            hook(f"block{d}")

        ex_o = exchange(2, o_pack, o_in, False)
        ex_o.start()
        save(lse, k_lse)
        o_in[z] = o_pack[z]
        hook("attended")
        ex_o.wait_recv()
        for g in range(4):
            att[:, 192 * g : 192 * g + 192] = o_in[g]
        save(att, k_att)
        res[...] = x + dot(att[...], wide_l[:, 3 * D :])
        save(res, k_res)
        scale, unit = rms_parts(res[...])
        normed = low(unit * gains[1:2, :])
        sent[...] = low(dot(taken_t[layer], normed)).reshape(EXPERTS, PAD_CAP, D)
        ex_s = exchange(3, sent, rc, True)
        ex_s.start()
        rc[ctx] = sent[ctx]
        _, gates = pair_gates(dot(normed, small_l[...]), route[layer])
        mix = first_table[layer].astype(jnp.float32) * gates[0] + second_table[layer].astype(jnp.float32) * gates[1]
        hook("sent")
        ex_s.wait_recv()
        save(rc, k_rc)
        loaded(layer, 4)

        def expert_part(j):
            at = pl.ds(pl.multiple_of(j * 256, 256), 256)
            up_at = pl.ds(pl.multiple_of(FF + j * 256, 256), 256)
            gate, up = dot(rc[...].reshape(SLOTS, D), egu[:, at]), dot(rc[...].reshape(SLOTS, D), egu[:, up_at])
            ej[:, at] = gate
            ej[:, up_at] = up
            eh[:, at] = low(gate * jax.nn.sigmoid(gate) * up)

        for d in range(4):
            pl.loop(2 * d, 2 * d + 2)(expert_part)
            hook(f"expert{d}")

        save(ej, k_ej)
        loaded(layer, 5)
        for j in range(D // 256):
            span = slice(256 * j, 256 * j + 256)
            result[:, :, span] = low(dot(eh[...], ed[:, span])).reshape(EXPERTS, PAD_CAP, 256)
        ex_r = exchange(4, result, ret, True)
        for copy in saves[:2]:
            copy.wait()
        ex_r.start()
        ret[ctx] = result[ctx]
        hook("returned")
        loaded(layer, 1)

        def shared_part(j):
            at = pl.ds(pl.multiple_of(j * 256, 256), 256)
            up_at = pl.ds(pl.multiple_of(FF + j * 256, 256), 256)
            gate, up = dot(normed, gu[:, at]), dot(normed, gu[:, up_at])
            sj[:, at] = gate
            sj[:, up_at] = up
            sh[:, at] = low(gate * jax.nn.sigmoid(gate) * up)

        pl.loop(0, FF // 256)(shared_part)

        save(sj, k_sj)
        loaded(layer, 3)
        shared_out = dot(sh[...], sd[...].reshape(FF, D))
        ex_r.wait_recv()
        save(ret, k_ret)
        high, rest_of = split(mix)
        returned = ret[...].reshape(SLOTS, D)
        mixed = dot(high, returned) + dot(rest_of, returned)
        out[...] = low(res[...] + shared_out + mixed)
        for ex in (ex_kv, ex_q, ex_o, ex_s, ex_r):
            ex.wait_send()
        for copy in saves[2:]:
            copy.wait()

    one_layer(0, state[...].astype(jnp.float32), out_lower)
    one_layer(1, out_lower[...].astype(jnp.float32), out_upper)
    for layer in range(2):
        drive(layer, firsts[layer].drain, *[tree.drain for tree in trees[layer].values()])


def weight_scratch():
    bf = jnp.bfloat16
    return [
        pltpu.VMEM((D, WIDE), bf), pltpu.VMEM((D, 2 * FF), bf), pltpu.VMEM((D, SMALL), bf),
        pltpu.VMEM((8, 8, 32, D), bf), pltpu.VMEM((D, 2 * FF), bf), pltpu.VMEM((FF, D), bf), DMA((6,)),
    ]


KEPT = (
    ((4, ROWS, 192), jnp.bfloat16), ((8, ROWS, 384), jnp.bfloat16), ((4, ROWS, 128), jnp.float32), ((ROWS, D), jnp.bfloat16),
    ((ROWS, D), jnp.float32), ((ROWS, 2 * FF), jnp.float32), ((EXPERTS, PAD_CAP, D), jnp.bfloat16),
    ((SLOTS, 2 * FF), jnp.float32), ((EXPERTS, PAD_CAP, D), jnp.bfloat16),
)


WEIGHTS = ((D, WIDE), (D, 2 * FF), (D, SMALL), (8, 8, 32, D), (D, 2 * FF), (FF, D))


def forward(pack, sd, egu, ed, state, geometry, plans):
    bf, f32 = jnp.bfloat16, jnp.float32
    slots = pltpu.VMEM((EXPERTS, PAD_CAP, D), bf)
    tables = [jnp.stack(pair) for pair in zip(*plans)]
    outs = pl.pallas_call(
        forward_kernel,
        out_shape=[jax.ShapeDtypeStruct((ROWS, D), bf)] * 2
        + [jax.ShapeDtypeStruct(s, bf) for s in WEIGHTS] * 2
        + [jax.ShapeDtypeStruct(s, t) for s, t in KEPT] * 2,
        in_specs=[ANY] * 4 + [VMEM] * 10,
        out_specs=[VMEM] * 2 + [ANY] * (2 * len(WEIGHTS) + 2 * len(KEPT)),
        scratch_shapes=[
            pltpu.VMEM((2, D, WIDE), bf), pltpu.VMEM((D, 2 * FF), bf), pltpu.VMEM((2, D, SMALL), bf),
            pltpu.VMEM((8, 8, 32, D), bf), pltpu.VMEM((D, 2 * FF), bf), pltpu.VMEM((FF, D), bf), DMA((2, 6)),
            pltpu.VMEM((128, PACK), bf), pltpu.VMEM((96, WIDE), bf), pltpu.VMEM((96, SMALL), bf),
            pltpu.VMEM((96, 2 * FF), bf), pltpu.VMEM((32, D), bf), pltpu.VMEM((96, 2 * FF), bf), pltpu.VMEM((256, D), bf),
            DMA((5, 3)), DMA((7, 3)), DMA((7, 3)),
        ]
        + [DMA((9, 2))] * 8
        + [DMA((2, 8, 2))] * 8
        + [
            pltpu.VMEM((4, ROWS, 384), bf), pltpu.VMEM((4, ROWS, 192), bf),
            pltpu.VMEM((8, ROWS, 384), bf), pltpu.VMEM((4, ROWS, 192), bf),
            pltpu.VMEM((4, ROWS, 192), bf), pltpu.VMEM((4, ROWS, 192), bf),
            pltpu.VMEM((4, ROWS, 128), f32), pltpu.VMEM((ROWS, D), bf), pltpu.VMEM((ROWS, D), f32),
            pltpu.VMEM((ROWS, 2 * FF), f32), pltpu.VMEM((ROWS, FF), bf),
            slots, slots, pltpu.VMEM((SLOTS, 2 * FF), f32), pltpu.VMEM((SLOTS, FF), bf), slots, slots, DMA((len(KEPT),)),
            DMA((2, 5, 7)), DMA((2, 5, 7)),
        ],
        compiler_params=pltpu.CompilerParams(collective_id=1, has_side_effects=True, vmem_limit_bytes=60 << 20),
        name="forward",
    )(pack, sd, egu, ed, state, *geometry, *tables)
    weights, kept = outs[2 : 2 + 2 * len(WEIGHTS)], outs[2 + 2 * len(WEIGHTS) :]
    return outs[:2], (weights[: len(WEIGHTS)], weights[len(WEIGHTS) :]), (kept[: len(KEPT)], kept[len(KEPT) :])


def backward_kernel(
    layer,
    grad, state, cosine, sine, qidx, qlab, klab, route, first_table, second_table, taken, small_t,
    g_wide, g_gu, g_small, g_sd, g_egu, g_ed,
    k_q, k_kv, k_lse, k_att, k_res, k_sj, k_rc, k_ej, k_ret,
    out, out_both,
    p_na, p_at, p_nf, p_sh, p_rc, p_hd, p_qkv, p_pr, p_gu, p_sd, p_j, p_er, p_small,
    wide, gu, small, sd, egu, ed, w_sem,
    q_all, kv_all, lse, att, res, sj, rc, ej, ret, i_sem,
    t_na, t_at, t_nf, t_sh, t_rc, t_hd, m_qkv, m_pr, m_gu, m_sd, m_j, grad_small, p_sem, p_send, p_recv,
    sent, er, back, slots, o_pack, o_in, dq_pack, dq_in, dkv_pack, dkv_in, dkv_sum, normed_grad, sh, eh,
    s_send, s_recv, r_send, r_recv, o_send, o_recv, q_send, q_recv, kv_send, kv_recv,
):
    section, a, z, y, h = place_ids()
    ctx = ctx_of(a, z)
    loads = [
        pltpu.make_async_copy(s, t, w_sem.at[i])
        for i, (s, t) in enumerate(((g_wide, wide), (g_gu, gu), (g_small, small), (g_sd, sd), (g_egu, egu), (g_ed, ed)))
    ]
    reads = [
        pltpu.make_async_copy(s, t, i_sem.at[i])
        for i, (s, t) in enumerate(zip((k_q, k_kv, k_lse, k_att, k_res, k_sj, k_rc, k_ej, k_ret), (q_all, kv_all, lse, att, res, sj, rc, ej, ret)))
    ]
    loads[2].start()
    reads[4].start()
    loads[3].start()
    reads[5].start()
    loads[1].start()
    reads[8].start()
    loads[5].start()
    reads[7].start()
    loads[4].start()
    for i in (6, 3, 0, 1, 2):
        reads[i].start()
    loads[0].start()
    near = neighbours()
    greet([near["core"]] + ctx_peers())
    saves = []

    def save(source, target):
        i = len(saves)
        here = pltpu.make_async_copy(source, target.at[0], p_sem.at[i])
        away = pltpu.make_async_remote_copy(
            source, target.at[1], p_send.at[i], p_recv.at[i], device_id=near["core"], device_id_type=MESH
        )
        saves.append((here, away))

        @pl.when(section == layer)
        def _():
            here.start()

        @pl.when(section != layer)
        def _():
            away.start()

    grad_out = grad[...].astype(jnp.float32)
    m_sd[...] = low(grad_out)
    save(m_sd, p_sd)
    loads[2].wait()
    reads[4].wait()
    scale_ffn, unit_ffn = rms_parts(res[...])
    normed = low(unit_ffn * small_t[1:2, :])
    picks, gates = pair_gates(dot(normed, small[...]), route[...])
    first, second = first_table[...].astype(jnp.float32), second_table[...].astype(jnp.float32)
    mix_high, mix_rest = split(first * gates[0] + second * gates[1])
    out_high, out_rest = split(grad_out)
    slot_grads = t_dot(mix_high, out_high) + t_dot(mix_rest, out_high) + t_dot(mix_high, out_rest)
    sent[...] = low(slot_grads).reshape(EXPERTS, PAD_CAP, D)
    ex_s = Exchange(sent, er, s_send, s_recv, True)
    ex_s.start()
    er[ctx] = sent[ctx]

    loads[3].wait()
    reads[5].wait()

    @pl.loop(0, FF // 1024)
    def _(j):
        at = pl.ds(pl.multiple_of(j * 1024, 256), 1024)
        up_at = pl.ds(pl.multiple_of(FF + j * 1024, 256), 1024)
        hidden_grad = dot_t(m_sd[...], sd[pl.ds(j * 4, 4)].reshape(1024, D))
        gate, up = sj[:, at], sj[:, up_at]
        sig = jax.nn.sigmoid(gate)
        m_gu[:, at] = low(hidden_grad * up * sig * (1.0 + gate * (1.0 - sig)))
        m_gu[:, up_at] = low(hidden_grad * gate * sig)
        sh[:, at] = low(gate * sig * up)
        t_sh[at, :] = low(jnp.transpose(gate * sig * up))

    save(m_gu, p_gu)
    save(t_sh, p_sh)
    t_nf[...] = low(jnp.transpose(unit_ffn * small_t[1:2, :]))
    save(t_nf, p_nf)
    loads[1].wait()

    @pl.loop(0, D // 768)
    def _(j):
        at = pl.ds(pl.multiple_of(j * 768, 256), 768)
        normed_grad[:, at] = dot_t(m_gu[...], gu[at, :])

    reads[8].wait()
    products = dot_t(m_sd[...], ret[...].reshape(SLOTS, D))
    gate_grads = [jnp.sum(products * first, axis=1, keepdims=True), jnp.sum(products * second, axis=1, keepdims=True)]
    inner = gates[0] * gate_grads[0] + gates[1] * gate_grads[1]
    chosen = [g * (d - inner) for g, d in zip(gates, gate_grads)]
    logit_grads = jnp.where(picks[0], chosen[0], 0.0) + jnp.where(picks[1], chosen[1], 0.0)
    logit_high, logit_rest = split(logit_grads)
    grad_small[...] = t_dot(normed, logit_high) + t_dot(normed, logit_rest)
    normed_grad[...] += dot_t(logit_high, small[...]) + dot_t(logit_rest, small[...])

    loads[5].wait()
    reads[7].wait()
    ex_s.wait_recv()
    save(er, p_er)

    @pl.loop(0, FF // 1024)
    def _(j):
        at = pl.ds(pl.multiple_of(j * 1024, 256), 1024)
        up_at = pl.ds(pl.multiple_of(FF + j * 1024, 256), 1024)
        hidden_grad = dot_t(er[...].reshape(SLOTS, D), ed[at, :])
        gate, up = ej[:, at], ej[:, up_at]
        sig = jax.nn.sigmoid(gate)
        m_j[:, at] = low(hidden_grad * up * sig * (1.0 + gate * (1.0 - sig)))
        m_j[:, up_at] = low(hidden_grad * gate * sig)
        eh[:, at] = low(gate * sig * up)

    save(m_j, p_j)
    loads[4].wait()

    @pl.loop(0, D // 768)
    def _(j):
        at = pl.ds(pl.multiple_of(j * 768, 256), 768)
        back[:, :, at] = low(dot_t(m_j[...], egu[at, :])).reshape(EXPERTS, PAD_CAP, 768)

    ex_r = Exchange(back, slots, r_send, r_recv, True)
    ex_r.start()
    slots[ctx] = back[ctx]
    reads[6].wait()
    t_hd[...] = jnp.transpose(eh[...])
    save(t_hd, p_hd)
    t_rc[...] = jnp.transpose(rc[...].reshape(SLOTS, D))
    save(t_rc, p_rc)
    reads[3].wait()
    t_at[...] = jnp.transpose(att[...])
    save(t_at, p_at)
    loads[0].wait()
    ex_r.wait_recv()
    grad_normed = normed_grad[...] + dot(taken[...], slots[...].reshape(SLOTS, D))
    grad_values, gain_ffn = rms_back(grad_normed, small_t[1:2, :], scale_ffn, unit_ffn)
    grad_res = grad_out + grad_values
    m_pr[...] = low(grad_res)
    save(m_pr, p_pr)
    grad_att = low(dot_t(m_pr[...], wide[:, 3 * D :]))
    for g in range(4):
        o_pack[g] = grad_att[:, 192 * g : 192 * g + 192]
    ex_o = Exchange(o_pack, o_in, o_send, o_recv, False)
    ex_o.start()
    o_in[z] = o_pack[z]
    scale_attn, unit_attn = rms_parts(state[...].astype(jnp.float32))
    t_na[...] = low(jnp.transpose(unit_attn * small_t[0:1, :]))
    save(t_na, p_na)
    dkv_sum[...] = jnp.zeros_like(dkv_sum)
    for i in (0, 1, 2):
        reads[i].wait()
    ex_o.wait_recv()

    @pl.loop(0, 4)
    def _(d):
        block = lax.rem(z + d + 1, 4)
        seen = visible_keys(qidx[block], qlab[block], klab[...])
        for head in range(3):
            span = slice(64 * head, 64 * head + 64)
            vspan = slice(192 + 64 * head, 256 + 64 * head)
            q, do = q_all[block, :, span], o_in[block, :, span]
            k = kv_all[:, :, span].reshape(SEQ, HEAD_DIM)
            v = kv_all[:, :, vspan].reshape(SEQ, HEAD_DIM)
            scores = dot_t(q, k) * SCALE
            probs = jnp.where(seen, jnp.exp(scores - lse[block, :, head : head + 1]), 0.0)
            dprobs = dot_t(do, v)
            delta = jnp.sum(probs * dprobs, axis=-1, keepdims=True)
            dscores = low(probs * (dprobs - delta))
            dq_pack[block, :, span] = low(dot(dscores, k) * SCALE)
            dkv_sum[:, span] += t_dot(dscores, q) * SCALE
            dkv_sum[:, vspan] += t_dot(low(probs), do)

    ex_q = Exchange(dq_pack, dq_in, q_send, q_recv, False)
    ex_q.start()
    dkv_pack[...] = low(dkv_sum[...]).reshape(8, ROWS, 384)
    ex_kv = Exchange(dkv_pack, dkv_in, kv_send, kv_recv, True)
    ex_kv.start()
    dq_in[z] = dq_pack[z]
    dkv_in[ctx] = dkv_pack[ctx]
    ex_q.wait_recv()
    ex_kv.wait_recv()
    dq = jnp.concatenate([dq_in[g].astype(jnp.float32) for g in range(4)], axis=1)
    both = [dkv_in[g].astype(jnp.float32) + dkv_in[4 + g].astype(jnp.float32) for g in range(4)]
    dk = jnp.concatenate([v[:, :192] for v in both], axis=1)
    dv = jnp.concatenate([v[:, 192:] for v in both], axis=1)
    m_qkv[:, 0:D] = low(rotate(dq, cosine[...], -sine[...]))
    m_qkv[:, D : 2 * D] = low(rotate(dk, cosine[...], -sine[...]))
    m_qkv[:, 2 * D :] = low(dv)
    save(m_qkv, p_qkv)
    grad_normed = dot_t(m_qkv[...], wide[:, 0 : 3 * D])
    grad_values, gain_attn = rms_back(grad_normed, small_t[0:1, :], scale_attn, unit_attn)
    out[...] = grad_res + grad_values
    lane = lax.broadcasted_iota(jnp.int32, (D, SMALL), 1)
    gains_t = jnp.transpose(jnp.concatenate([gain_attn, gain_ffn, jnp.zeros((SMALL - 2, D), jnp.float32)], axis=0))
    grad_small[...] = jnp.where(lane < 2, gains_t, grad_small[...])
    save(grad_small, p_small)
    save(out, out_both)
    for ex in (ex_s, ex_r, ex_o, ex_q, ex_kv):
        ex.wait_send()

    @pl.when(section == layer)
    def _():
        for here, away in saves:
            here.wait()
            away.wait_recv()

    @pl.when(section != layer)
    def _():
        for here, away in saves:
            away.wait_send()


def layer_backward(layer, grad, state, geometry, plan, taken, small_t, weights, kept):
    bf, f32 = jnp.bfloat16, jnp.float32
    cosine, sine, qidx, qlab, klab = geometry
    route, first_table, second_table, _ = plan
    slots = pltpu.VMEM((EXPERTS, PAD_CAP, D), bf)
    shapes = dict(OPERANDS)
    order = ("na", "at", "nf", "sh", "rc", "hd", "qkv", "pr", "gu", "sd", "j", "er", "small")
    outs = pl.pallas_call(
        functools.partial(backward_kernel, layer),
        out_shape=[jax.ShapeDtypeStruct((ROWS, D), f32), jax.ShapeDtypeStruct((2, ROWS, D), f32)]
        + [jax.ShapeDtypeStruct((2,) + shapes[n], operand_type(n)) for n in order],
        in_specs=[VMEM] * 12 + [ANY] * (6 + len(KEPT)),
        out_specs=[VMEM, ANY] + [ANY] * N_OPS,
        scratch_shapes=weight_scratch()
        + [pltpu.VMEM(s, t) for s, t in KEPT] + [DMA((len(KEPT),))]
        + [pltpu.VMEM(shapes[n], operand_type(n)) for n in order if n != "er"] + [DMA((N_OPS + 1,))] * 3
        + [
            slots, slots, slots, slots,
            pltpu.VMEM((4, ROWS, 192), bf), pltpu.VMEM((4, ROWS, 192), bf),
            pltpu.VMEM((4, ROWS, 192), bf), pltpu.VMEM((4, ROWS, 192), bf),
            pltpu.VMEM((8, ROWS, 384), bf), pltpu.VMEM((8, ROWS, 384), bf), pltpu.VMEM((SEQ, 384), f32),
            pltpu.VMEM((ROWS, D), f32), pltpu.VMEM((ROWS, FF), bf), pltpu.VMEM((SLOTS, FF), bf),
            DMA((7,)), DMA((7,)), DMA((7,)), DMA((7,)), DMA((3,)), DMA((3,)), DMA((3,)), DMA((3,)), DMA((7,)), DMA((7,)),
        ],
        compiler_params=pltpu.CompilerParams(collective_id=3 + layer, has_side_effects=True, vmem_limit_bytes=62 << 20),
        name="layer_backward",
    )(grad, state, cosine, sine, qidx, qlab, klab, route, first_table, second_table, taken, small_t, *weights, *kept)
    return outs[0], outs[1], outs[2:]


def token_positions(group_row):
    labels = jnp.arange(CONT + 1, dtype=jnp.int32)
    member = (group_row[:, None] == labels[None, :]).astype(jnp.int32)
    run_sizes = jnp.sum(member, axis=0)
    run_starts = jnp.cumsum(run_sizes) - run_sizes
    first_index = jnp.sum(member * run_starts[None, :], axis=1)
    token_index = jnp.arange(group_row.shape[0], dtype=jnp.int32)
    return jnp.where(group_row == 0, token_index, run_sizes[0] + token_index - first_index)


def rotation_tables(positions):
    half = HEAD_DIM // 2
    frequency = jnp.exp(-math.log(10000.0) * jnp.arange(half, dtype=jnp.float32) / half)
    angles = positions.astype(jnp.float32)[:, None] * frequency[None, :]
    cosine, sine = jnp.cos(angles), jnp.sin(angles)
    cosine = jnp.tile(jnp.concatenate([cosine, cosine], axis=1), (1, HEADS))
    sine = jnp.tile(jnp.concatenate([-sine, sine], axis=1), (1, HEADS))
    return cosine, sine


def slot_tables(route, rank):
    pairs = ROWS * TOP
    expert = route.reshape(-1)
    key = rank.reshape(-1) * pairs + jnp.arange(pairs, dtype=jnp.int32)
    earlier = (expert[None, :] == expert[:, None]) & (key[None, :] < key[:, None])
    slot = jnp.sum(earlier.astype(jnp.int32), axis=1)
    place = jnp.where(slot < CAP, expert * PAD_CAP + slot, -1).reshape(ROWS, TOP)
    every = jnp.arange(SLOTS, dtype=jnp.int32)
    first, second = [place[:, c : c + 1] == every[None, :] for c in range(TOP)]
    both = low(first | second)
    return (route, low(first), low(second), both.T), both


def swap_cores(value):
    return lax.ppermute(value, "section", [(0, 1), (1, 0)])


def on_device(
    x_in, cotangent, group_ids, routes, priority,
    gains, w_qkv, w_out, router, shared_gate_up, shared_down, expert_gate_up, expert_down,
):
    section = lax.axis_index("section")
    ctx = lax.axis_index("ctx")
    first = section == 0

    pack = jnp.concatenate(
        [w_qkv[0], w_out[0], gains[0], router[0], jnp.zeros((OWN, SMALL - 2 - EXPERTS), jnp.bfloat16), shared_gate_up[0]],
        axis=1,
    )
    pack = jnp.pad(pack, ((0, 16 - OWN), (0, 0)))

    def mine(value):
        return jnp.where(first, value[0], value[1])

    def other(value):
        return jnp.where(first, value[1], value[0])

    picked = jnp.stack([routes[0, :, 0], priority[0, :, 0]], axis=1)
    passed = swap_cores(other(picked))
    own = mine(picked)
    plans = [jnp.where(first, own, passed), jnp.where(first, passed, own)]
    plans, taken = zip(*[slot_tables(plan[0], plan[1]) for plan in plans])

    group_row = mine(group_ids[:, 0])
    positions = token_positions(group_row)
    cosine, sine = rotation_tables(lax.dynamic_slice_in_dim(positions, ctx * ROWS, ROWS))
    half_start = ctx // 4 * 512
    qlab = lax.dynamic_slice_in_dim(group_row, half_start, 512).reshape(4, ROWS, 1)
    qidx = (half_start + jnp.arange(512, dtype=jnp.int32)).reshape(4, ROWS, 1)
    geometry = (cosine, sine, qidx, qlab, group_row[None, :])

    state = mine(x_in[:, 0])
    (hidden, final), weights, kept = forward(
        pack, shared_down[0], expert_gate_up[0, 0], expert_down[0, 0], state, geometry, plans
    )
    small_t = [weights[layer][2][:, :8].astype(jnp.float32).T for layer in range(2)]
    hidden_grad, hidden_grads, operands_upper = layer_backward(
        1, mine(cotangent[:, 0]), hidden, geometry, plans[1], taken[1], small_t[1], weights[1], kept[1]
    )
    _, input_grads, operands_lower = layer_backward(
        0, low(hidden_grad), state, geometry, plans[0], taken[0], small_t[0], weights[0], kept[0]
    )
    qkv_grad, out_grad, small_grad, gu_grad, sd_grad, egu_grad, ed_grad = weight_grads(operands_lower, operands_upper)

    outputs = jnp.where(first, hidden, final)
    arrived = swap_cores(jnp.where(first, final, hidden))
    outputs = jnp.stack([jnp.where(first, outputs, arrived), jnp.where(first, arrived, outputs)])
    grads = jnp.where(first, input_grads, hidden_grads[::-1])
    return (
        outputs.reshape(1, 2, 1, ROWS, D),
        grads.reshape(1, 2, 1, ROWS, D),
        small_grad[None, :, :2],
        qkv_grad[None],
        out_grad[None],
        small_grad[None, :, 2 : 2 + EXPERTS],
        gu_grad[None],
        sd_grad[None],
        egu_grad[None, None],
        ed_grad[None, None],
    )


def solution(mesh):
    dense = P("section", ("ctx", "fsdp"), None)
    expert = P("section", "ctx", "fsdp", None)
    tokens = P("section", None, "fsdp", "ctx", None)
    rows = P(None, "fsdp", "ctx", None)
    return jax.shard_map(
        on_device,
        mesh=mesh,
        in_specs=(rows, rows, P(None, "fsdp", None), tokens, tokens) + (dense,) * 6 + (expert,) * 2,
        out_specs=(tokens, tokens) + (dense,) * 6 + (expert,) * 2,
        check_vma=False,
    )
```
